128 devices in a mesh: frames: 32 (over z, y, core), obj: 4 (over x).
Axes of the slice: x: 4, y: 4, z: 4, core: 2. Of those that a mesh axis runs over, the one named last changes fastest.
Arguments:
- object_tiles: float32 [2, 4096, 32, 128], P(None, ('frames', 'obj')), may hold values from -6 to 6
- amplitudes: bfloat16 [2048, 256, 256], P(('frames', 'obj')), may hold values from 0.5 to 3
- probe: float32 [2, 256, 256], replicated, may hold values from -6 to 6
- frame_pos: int32 [2048, 2], P(('frames', 'obj')), may hold values from 0 to 126, as said below
Outputs:
- object_out: float32 [2, 4096, 32, 128], P(None, ('frames', 'obj'))
The draws below stay inside these ranges and needn't reach their ends.
Inputs may be any that keep to these rules, and one draw needn't show every extreme that they name: `frame_pos`: each row is (r, c) with 0 <= r <= 24 and 0 <= c <= 126, and c + 2 r is a multiple of 16. `frame_pos`: A frame's group is ((c + 2 r) mod 128) // 16. Within each aligned block of 16 frames (the frames of one device) no group holds more than 3 frames, and in every draw one group holds exactly 3 frames in every block.
All inputs are finite; a program needn't handle non-finite values.
Results may differ from the reference program's by a relative error of at most 0.0085.
The reference program's roundings to bfloat16 on the way count: a program that leaves them out, or rounds other values in their place, can miss the bound.
Values may be sent and summed in bfloat16 or wider, within the bound.
No kernel may reach another device: no remote copies, remote signals or barrier semaphores. Data moves between devices by JAX's collectives and lax.ppermute only.
A program may use at most 128 MiB of HBM per device.

```python
import jax
import jax.numpy as jnp
from jax import lax

FRAME = 256
TH = 32
TW = 128
FR_DEV = 16
TROWS = 32
ITERS = 2
CAP = 3
FRAMES = 2048
TILES = 4096
DEVICES = 128


def draw_frame_pos(key, part):
    key = jax.random.fold_in(key, 7)
    groups = DEVICES // 16
    spare = CAP * groups - CAP
    hot_key, device_key = jax.random.split(key)
    hot_group = jax.random.randint(hot_key, (), 0, groups)

    def one_device(single_key):
        pick_key, order_key, row_key = jax.random.split(single_key, 3)
        others = jax.random.permutation(pick_key, spare)[:FR_DEV - CAP] + CAP
        slots = jnp.concatenate([jnp.arange(CAP, dtype=jnp.int32), others.astype(jnp.int32)])
        owner_group = (slots // CAP + hot_group) % groups
        owner_group = owner_group[jax.random.permutation(order_key, FR_DEV)]
        start_rows = jax.random.randint(row_key, (FR_DEV,), 0, TROWS - 7)
        start_cols = (16 * owner_group - 2 * start_rows) % DEVICES
        return jnp.stack([start_rows, start_cols], axis=1)
    device_keys = jax.random.split(device_key, DEVICES)
    return jax.vmap(one_device)(device_keys).reshape(FRAMES, 2).astype(jnp.int32)


def block_scale(stream_key, extent, cuts, least, high):
    factor_of = 1.0
    for axis_at, blocks in cuts:
        heights = jax.random.uniform(jax.random.fold_in(jax.random.fold_in(stream_key, 6), axis_at), (blocks,), jnp.float32, least / len(cuts), high / len(cuts))
        factor_of = factor_of * jnp.repeat(jnp.exp(heights), extent[axis_at] // blocks).reshape((-1,) + (1,) * (len(extent) - 1 - axis_at))
    return factor_of


def bell_draw(own_key, extent, scale, most, shards=(), kind=jnp.bfloat16):
    entries = scale * jax.random.normal(own_key, extent, jnp.float32)
    if shards:
        entries = entries * block_scale(own_key, extent, shards, -0.22, 0.18)
    return jnp.clip(entries, -most, most).astype(kind)


def setup_inputs(seed: int = 0) -> dict:
    arg_keys = jax.random.split(jax.random.key(seed), 5)
    object_tiles = bell_draw(arg_keys[0], (2, TILES, TH, TW), 1.0, 6.0, ((1, 128),), jnp.float32)
    amplitudes = jnp.clip(0.5 + 2.5 * jax.random.uniform(arg_keys[1], (FRAMES, FRAME, FRAME), jnp.float32) ** block_scale(arg_keys[1], (FRAMES, FRAME, FRAME), ((0, 128),), -0.2, 0.2), 0.5, 3.0).astype(jnp.bfloat16)
    probe = bell_draw(arg_keys[2], (2, FRAME, FRAME), 1.0, 6.0, (), jnp.float32)
    frame_pos = draw_frame_pos(jax.random.fold_in(arg_keys[4], 71), 0)
    return {"object_tiles": object_tiles, "amplitudes": amplitudes, "probe": probe, "frame_pos": frame_pos}


magnitude_floor = 0.3
delta_reg = 1.0
tv_step = 0.1
smooth_eps = 0.1

def dft_tables(frame_size):
    indices = jnp.arange(frame_size, dtype=jnp.int32)
    phase_step = indices[:, None] * indices[None, :] % frame_size
    angles = phase_step.astype(jnp.float32) * (2.0 * jnp.pi / frame_size)
    norm_scale = 1.0 / jnp.sqrt(jnp.float32(frame_size))
    cosine = jnp.cos(angles) * norm_scale
    minus_sine = -jnp.sin(angles) * norm_scale
    forward = jnp.stack([jnp.stack([cosine, -minus_sine]), jnp.stack([minus_sine, cosine])])
    inverse = jnp.stack([jnp.stack([cosine, minus_sine]), jnp.stack([-minus_sine, cosine])])
    return (forward.astype(jnp.bfloat16), inverse.astype(jnp.bfloat16))

def left_apply(table, data):
    return jnp.einsum('pqab,fqbc->fpac', table.astype(jnp.float32), data.astype(jnp.float32), precision=lax.Precision.HIGHEST)

def right_apply(data, table):
    return jnp.einsum('fqab,qpbc->fpac', data.astype(jnp.float32), table.astype(jnp.float32), precision=lax.Precision.HIGHEST)

def project_frames(patches, amplitudes, probe, forward, inverse):
    real_part = patches[:, 0].astype(jnp.float32)
    imag_part = patches[:, 1].astype(jnp.float32)
    object_wave = jnp.stack([probe[0] * real_part - probe[1] * imag_part, probe[0] * imag_part + probe[1] * real_part], axis=1).astype(jnp.bfloat16)
    midway = left_apply(forward, object_wave).astype(jnp.bfloat16)
    far_field = right_apply(midway, inverse)
    modulus = jnp.sqrt(far_field[:, 0] * far_field[:, 0] + far_field[:, 1] * far_field[:, 1])
    rescale = amplitudes.astype(jnp.float32) / jnp.maximum(modulus, magnitude_floor) - 1.0
    change = (far_field * rescale[:, None]).astype(jnp.bfloat16)
    halfway = left_apply(inverse, change).astype(jnp.bfloat16)
    returned_wave = right_apply(halfway, forward)
    return jnp.stack([probe[0] * returned_wave[:, 0] + probe[1] * returned_wave[:, 1], probe[0] * returned_wave[:, 1] - probe[1] * returned_wave[:, 0]], axis=1)

def tv_image(image):
    across = image[:, :, 1:] - image[:, :, :-1]
    weight_across = across / jnp.sqrt(across[0] * across[0] + across[1] * across[1] + smooth_eps)[None]
    zero_col = jnp.zeros((2, image.shape[1], 1), image.dtype)
    pull_across = jnp.concatenate([zero_col, weight_across], axis=2) - jnp.concatenate([weight_across, zero_col], axis=2)
    down = image[:, 1:, :] - image[:, :-1, :]
    weight_down = down / jnp.sqrt(down[0] * down[0] + down[1] * down[1] + smooth_eps)[None]
    zero_row = jnp.zeros((2, 1, image.shape[2]), image.dtype)
    pull_down = jnp.concatenate([zero_row, weight_down], axis=1) - jnp.concatenate([weight_down, zero_row], axis=1)
    return pull_across + pull_down

def reference(object_tiles, amplitudes, probe, frame_pos):
    forward, inverse = dft_tables(FRAME)
    row_ids = jnp.arange(TROWS, dtype=jnp.int32)
    col_ids = jnp.arange(DEVICES, dtype=jnp.int32)
    to_image = (col_ids[None, :] + 2 * row_ids[:, None]) % DEVICES * TROWS + row_ids[:, None]
    owners = jnp.arange(DEVICES, dtype=jnp.int32)[:, None]
    from_image = (row_ids[None, :] * DEVICES + (owners - 2 * row_ids[None, :]) % DEVICES).reshape(-1)
    image = object_tiles[:, to_image].transpose(0, 1, 3, 2, 4).reshape(2, TROWS * TH, DEVICES * TW)
    zero_index = jnp.zeros((), jnp.int32)
    intensity = probe[0] * probe[0] + probe[1] * probe[1]

    def add_power(member, running):
        corner = frame_pos[member]
        start = (corner[0] * TH, corner[1] * TW)
        current_block = lax.dynamic_slice(running, start, (FRAME, FRAME))
        return lax.dynamic_update_slice(running, current_block + intensity, start)
    illumination = lax.fori_loop(0, FRAMES, add_power, jnp.zeros((TROWS * TH, DEVICES * TW), jnp.float32))
    block_amplitudes = amplitudes.reshape(-1, 16, FRAME, FRAME)
    block_positions = frame_pos.reshape(-1, 16, 2)
    for sweep in range(ITERS):
        image_low = image.astype(jnp.bfloat16)

        def per_block(numerator, block):
            amps_block, pos_block = block

            def cut_window(corner):
                return lax.dynamic_slice(image_low, (zero_index, corner[0] * TH, corner[1] * TW), (2, FRAME, FRAME))
            patches = jax.vmap(cut_window)(pos_block)
            update = project_frames(patches, amps_block, probe, forward, inverse)

            def place_frame(member, running):
                corner = pos_block[member]
                start = (zero_index, corner[0] * TH, corner[1] * TW)
                current_block = lax.dynamic_slice(running, start, (2, FRAME, FRAME))
                return lax.dynamic_update_slice(running, current_block + update[member], start)
            return (lax.fori_loop(0, 16, place_frame, numerator), None)
        numerator, _ = lax.scan(per_block, jnp.zeros((2, TROWS * TH, DEVICES * TW), jnp.float32), (block_amplitudes, block_positions))
        relaxed = image + numerator / (illumination[None] + delta_reg)
        image = relaxed - tv_step * tv_image(relaxed)
    tiles_ordered = image.reshape(2, TROWS, TH, DEVICES, TW).transpose(0, 1, 3, 2, 4).reshape(2, TROWS * DEVICES, TH, TW)
    return tiles_ordered[:, from_image]
```

```python
import jax
import jax.numpy as jnp
import numpy as np
from jax import lax
from jax.experimental import pallas as pl
from jax.experimental.pallas import tpu as pltpu
from jax.sharding import PartitionSpec as P

FLOOR = 0.3
DELTA = 1.0
STEP = 0.1
EPS = 0.1
CENTRE = 1.75
F32 = jnp.float32
BF16 = jnp.bfloat16
SIDE = 256
ALL = ("frames", "obj")
GROUPS = [list(range(16 * g, 16 * g + 16)) for g in range(8)]


def params(limit_mb=40):
    return pltpu.CompilerParams(vmem_limit_bytes=limit_mb << 20)


def dft_blocks():
    index = np.arange(SIDE)
    angle = (index[:, None] * index[None, :] % SIDE) * (2.0 * np.pi / SIDE)
    cosine, sine = np.cos(angle) / 16.0, np.sin(angle) / 16.0
    forward = np.block([[cosine, sine], [-sine, cosine]])
    return jnp.asarray(forward, F32).astype(BF16), jnp.asarray(forward.T, F32).astype(BF16)


def iota(shape, axis):
    return lax.broadcasted_iota(jnp.int32, shape, axis)


def dot(a, b):
    return jnp.dot(a, b, preferred_element_type=F32)


def picker(source_of):
    return (iota((256, 256), 1) == source_of(iota((256, 256), 0))).astype(F32).astype(BF16)


def window_rows(dev):
    group, member = dev // 16, dev % 16
    return group, [(2 * member + 8 * group + w) % 32 for w in range(2)]


def pieces_kernel(pos_ref, amp_ref, out_ref):
    swap = picker(lambda o: (o % 16) * 16 + o // 16)
    lane = iota((8, 128), 1)
    code = jnp.zeros((8, 128), jnp.int32)
    for f in range(16):
        row, column = pos_ref[f, 0], pos_ref[f, 1]
        group = ((column + 2 * row) & 127) >> 4
        local = (row - 8 * group) & 31
        owner = (local & 1) * 128 + 16 * group + (local >> 1)
        code = jnp.where((lane & 15) == f, owner, code)
    code = code.astype(F32).astype(BF16)
    for block in range(4):
        rows = amp_ref[:, 16 * block:16 * block + 16, :].reshape(256, 256)
        turned = dot(swap, rows).astype(BF16)
        for part in range(8):
            quad, half = part // 2, part % 2
            out_ref[8 * block + part, 0:64, :] = turned[64 * quad:64 * quad + 64, 128 * half:128 * half + 128]
            out_ref[8 * block + part, 64:72, :] = code


def amplitude_pieces(frame_pos, amplitudes):
    return pl.pallas_call(
        pieces_kernel,
        grid=(4,),
        in_specs=[
            pl.BlockSpec(memory_space=pltpu.SMEM),
            pl.BlockSpec((16, 64, 256), lambda s: (0, s, 0)),
        ],
        out_specs=pl.BlockSpec((32, 72, 128), lambda s: (s, 0, 0)),
        out_shape=jax.ShapeDtypeStruct((128, 72, 128), BF16),
        compiler_params=params(),
        name="amplitude_pieces",
    )(frame_pos, amplitudes)


def sums_kernel(dev_ref, in_ref, out_ref, count_ref, total_ref, number_ref):
    step = pl.program_id(0)

    @pl.when(step == 0)
    def _():
        total_ref[...] = jnp.zeros_like(total_ref)

    lane = iota((8, 128), 1)
    owner = iota((256, 128), 0).astype(F32)
    members, values = [], []
    for t in range(4):
        code = jnp.zeros((8, 128), F32)
        for s in range(8):
            code = jnp.where((lane >> 4) == s, in_ref[8 * t + s, 64:72, :].astype(F32), code)
        members.append((owner == jnp.tile(code, (32, 1))).astype(F32).astype(BF16))
        values.append(
            jnp.concatenate(
                [in_ref[8 * t:8 * t + 8, 16 * c:16 * c + 16, :].reshape(128, 128) for c in range(4)]
                + [jnp.ones((128, 128), BF16)],
                axis=1,
            )
        )
    total_ref[...] += dot(jnp.concatenate(members, axis=1), jnp.concatenate(values, axis=0))

    @pl.when(step == pl.num_programs(0) - 1)
    def _():
        turn = picker(lambda o: (o % 8) * 32 + o // 8)
        for block in range(4):
            parts = []
            for w in range(2):
                rows = slice(128 * w + 32 * block, 128 * w + 32 * block + 32)
                mean = CENTRE * total_ref[rows, 512:640]
                for c in range(4):
                    parts.append(total_ref[rows, 128 * c:128 * c + 128] - mean)
            stacked = jnp.concatenate(parts, axis=0).astype(BF16)
            out_ref[32 * block:32 * block + 32] = dot(turn, stacked).reshape(32, 8, 128).astype(BF16)
        number_ref[...] = total_ref[:, 512:640]
        for w in range(2):
            own = number_ref[pl.ds(dev_ref[0] + 128 * w, 1), :]
            count_ref[8 * w:8 * w + 8, :] = jnp.broadcast_to(own, (8, 128))


def window_sums(dev, arrived):
    return pl.pallas_call(
        sums_kernel,
        grid=(4,),
        in_specs=[
            pl.BlockSpec(memory_space=pltpu.SMEM),
            pl.BlockSpec((32, 72, 128), lambda s: (s, 0, 0)),
        ],
        out_specs=[
            pl.BlockSpec((128, 8, 128), lambda s: (0, 0, 0)),
            pl.BlockSpec((16, 128), lambda s: (0, 0)),
        ],
        out_shape=[
            jax.ShapeDtypeStruct((128, 8, 128), BF16),
            jax.ShapeDtypeStruct((16, 128), F32),
        ],
        scratch_shapes=[pltpu.VMEM((256, 640), F32), pltpu.VMEM((256, 128), F32)],
        compiler_params=params(),
        name="window_sums",
    )(dev, arrived)


def outbound_kernel(dev_ref, in_ref, out_ref):
    dev = dev_ref[0]
    shift = 8 * (dev // 16) + (dev % 16) // 2
    for member in range(16):
        for w in range(2):
            row = (shift + 2 * member + w) % 32
            for part in range(2):
                out_ref[member, w, part] = in_ref[part, row].astype(BF16)


def outbound_tiles(dev, tiles):
    return pl.pallas_call(
        outbound_kernel,
        in_specs=[pl.BlockSpec(memory_space=pltpu.SMEM), pl.BlockSpec(memory_space=pltpu.VMEM)],
        out_specs=pl.BlockSpec(memory_space=pltpu.VMEM),
        out_shape=jax.ShapeDtypeStruct((16, 2, 2, 32, 128), BF16),
        compiler_params=params(),
        name="outbound_tiles",
    )(dev, tiles)


def inbound_kernel(dev_ref, in_ref, out_ref):
    dev = dev_ref[0]
    shift = 8 * (dev // 16) + (dev % 16) // 2
    for member in range(16):
        for w in range(2):
            row = (shift + 2 * member + w) % 32
            for part in range(2):
                out_ref[part, row] = in_ref[member, w, part].astype(F32)


def inbound_tiles(dev, arrived):
    return pl.pallas_call(
        inbound_kernel,
        in_specs=[pl.BlockSpec(memory_space=pltpu.SMEM), pl.BlockSpec(memory_space=pltpu.VMEM)],
        out_specs=pl.BlockSpec(memory_space=pltpu.VMEM),
        out_shape=jax.ShapeDtypeStruct((2, 32, 32, 128), F32),
        compiler_params=params(),
        name="inbound_tiles",
    )(dev, arrived)


def to_far_field(image, probe_ref, forward_ref, inverse_ref):
    waves = []
    for w in range(2):
        real, imag = [image[w][part].astype(BF16).astype(F32) for part in range(2)]
        waves.append(
            [
                (probe_ref[0] * real - probe_ref[1] * imag).astype(BF16),
                (probe_ref[0] * imag + probe_ref[1] * real).astype(BF16),
            ]
        )
    wave = jnp.concatenate(
        [jnp.concatenate([waves[0][part], waves[1][part]], axis=1) for part in range(2)], axis=0
    )
    midway = dot(forward_ref[...], wave).astype(BF16)
    midway = jnp.concatenate(
        [
            jnp.concatenate([midway[:256, 256 * w:256 * w + 256], midway[256:, 256 * w:256 * w + 256]], axis=1)
            for w in range(2)
        ],
        axis=0,
    )
    return dot(midway, inverse_ref[...])


def from_far_field(far, totals, counts, image, probe_ref, forward_ref, inverse_ref):
    changes = []
    for w in range(2):
        real, imag = far[256 * w:256 * w + 256, :256], far[256 * w:256 * w + 256, 256:]
        power = jnp.maximum(real * real + imag * imag, FLOOR * FLOOR)
        scale = totals[w] * lax.rsqrt(power) - counts[w]
        changes.append([(real * scale).astype(BF16), (imag * scale).astype(BF16)])
    change = jnp.concatenate(
        [jnp.concatenate([changes[0][part], changes[1][part]], axis=1) for part in range(2)], axis=0
    )
    halfway = dot(inverse_ref[...], change).astype(BF16)
    halfway = jnp.concatenate(
        [
            jnp.concatenate([halfway[:256, 256 * w:256 * w + 256], halfway[256:, 256 * w:256 * w + 256]], axis=1)
            for w in range(2)
        ],
        axis=0,
    )
    returned = dot(halfway, forward_ref[...])
    intensity = probe_ref[0] * probe_ref[0] + probe_ref[1] * probe_ref[1]
    relaxed = []
    for w in range(2):
        real, imag = returned[256 * w:256 * w + 256, :256], returned[256 * w:256 * w + 256, 256:]
        weight = 1.0 / (counts[w] * intensity + DELTA)
        relaxed.append(
            [
                image[w][0] + (probe_ref[0] * real + probe_ref[1] * imag) * weight,
                image[w][1] + (probe_ref[0] * imag - probe_ref[1] * real) * weight,
            ]
        )
    return relaxed


def own_counts(count_ref):
    return [jnp.tile(count_ref[8 * w:8 * w + 8, :], (32, 2)) for w in range(2)]


def write_relaxed(relaxed, relaxed_ref, edge_refs):
    ahead_ref, behind_ref, up_ref, down_ref = edge_refs
    for w in range(2):
        for part in range(2):
            relaxed_ref[w, part] = relaxed[w][part]
    lane = iota((256, 128), 1)
    sources = []
    for w, side in ((0, 1), (1, 0), (1, 1), (0, 0)):
        for part in range(2):
            sources.append((relaxed[w][part][:, 128 * side:128 * side + 128], 127 * side))
    columns = jnp.zeros((256, 128), F32)
    for place, (block, at) in enumerate(sources):
        turned = pltpu.roll(block, (place - at) % 128, 1) if place != at else block
        columns = jnp.where(lane == place, turned, columns)
    rows = columns.T[:8]
    place = iota((8, 256), 0)
    zero = jnp.zeros((8, 256), F32)
    ahead_ref[...] = jnp.where(place >= 6, pltpu.roll(rows, 6, 0), zero)
    behind_ref[...] = jnp.where(place >= 6, pltpu.roll(rows, 4, 0), zero)
    up = jnp.where(place >= 4, rows, zero)
    down = jnp.where(place >= 4, pltpu.roll(rows, 6, 0), zero)
    for w in range(2):
        for part in range(2):
            at = 2 * w + part
            up = jnp.where(place == at, pltpu.roll(relaxed[w][part][248:], (at - 7) % 8, 0), up)
            first = relaxed[w][part][:8]
            down = jnp.where(place == at, pltpu.roll(first, at, 0) if at else first, down)
    up_ref[...] = jnp.where(place >= 6, zero, up)
    down_ref[...] = jnp.where(place >= 6, zero, down)


def smooth(dev, relaxed_ref, halo_refs):
    up_own, up_in, down_own, down_in = [ref[...] for ref in halo_refs]
    group, starts = window_rows(dev)
    lane8 = iota((8, 256), 1)
    left = jnp.where(lane8 < 32, pltpu.roll(up_in, 32, 1), pltpu.roll(up_own, 32, 1))
    right = jnp.where(lane8 >= 224, pltpu.roll(down_in, 224, 1), pltpu.roll(down_own, 224, 1))
    sides = jnp.concatenate([left, right, jnp.zeros((112, 256), F32)], axis=0).T
    lane = iota((256, 256), 1)
    row = iota((256, 256), 0)
    row8 = iota((8, 256), 0)
    image = []
    for w in range(2):
        start = starts[w]
        x = [relaxed_ref[w, part] for part in range(2)]
        wrapped = (row // 32 + start) >= 32
        column = (16 * group - 2 * start + jnp.where(wrapped, 64, 0)) & 127
        keep_left = (column[:, :128] != 0).astype(F32)
        keep_right = jnp.logical_not((lane == 255) & (column == 126)).astype(F32)
        keep_down = (((32 * start + row) & 1023) != 1023).astype(F32)
        keep_up = (start != 0).astype(F32)

        def halo(at, to):
            shift = (to - at) % 128
            return pltpu.roll(sides, shift, 1) if shift else sides

        across, edge, down, top = [], [], [], []
        for part in range(2):
            beyond = halo(8 + 4 + 2 * (1 - w) + part, 127)
            beyond = jnp.concatenate([beyond, beyond], axis=1)
            across.append(jnp.where(lane == 255, beyond, pltpu.roll(x[part], 255, 1)) - x[part])
            edge.append(x[part][:, :128] - halo(4 + 2 * w + part, 0))
            at = 2 * w + part
            below = jnp.broadcast_to(down_in[at:at + 1], (256, 256))
            down.append(jnp.where(row == 255, below, pltpu.roll(x[part], 255, 0)) - x[part])
            top.append(x[part][:8] - jnp.broadcast_to(up_in[at:at + 1], (8, 256)))
        across_weight = lax.rsqrt(across[0] * across[0] + across[1] * across[1] + EPS) * keep_right
        edge_weight = lax.rsqrt(edge[0] * edge[0] + edge[1] * edge[1] + EPS) * keep_left
        down_weight = lax.rsqrt(down[0] * down[0] + down[1] * down[1] + EPS) * keep_down
        top_weight = lax.rsqrt(top[0] * top[0] + top[1] * top[1] + EPS) * keep_up
        parts = []
        for part in range(2):
            to_right = across[part] * across_weight
            first = edge[part] * edge_weight
            to_left = jnp.where(lane == 0, jnp.concatenate([first, first], axis=1), pltpu.roll(to_right, 1, 1))
            to_below = down[part] * down_weight
            moved = pltpu.roll(to_below, 1, 0)
            to_above = jnp.concatenate(
                [jnp.where(row8 == 0, top[part] * top_weight, moved[:8]), moved[8:]], axis=0
            )
            parts.append(x[part] - STEP * ((to_left - to_right) + (to_above - to_below)))
        image.append(parts)
    return image


def first_far_kernel(in_ref, probe_ref, forward_ref, inverse_ref, far_ref, image_ref):
    image = []
    for w in range(2):
        image.append([])
        for part in range(2):
            whole = jnp.concatenate(
                [
                    jnp.concatenate([in_ref[2 * i, w, part], in_ref[2 * i + 1, w, part]], axis=1)
                    for i in range(8)
                ],
                axis=0,
            )
            image_ref[w, part] = whole
            image[w].append(whole)
    far_ref[...] = to_far_field(image, probe_ref, forward_ref, inverse_ref)


def first_back_kernel(
    far_ref, image_ref, sums_ref, count_ref, probe_ref, forward_ref, inverse_ref, relaxed_ref, total_ref, *edge_refs
):
    counts = own_counts(count_ref)

    def source(o):
        w, half, row = o // 128, (o // 64) % 2, o % 64
        return ((row // 4) * 2 + half) * 8 + w * 4 + row % 4

    place = picker(source)
    blocks = []
    for block in range(4):
        rows = sums_ref[32 * block:32 * block + 32].astype(F32).reshape(256, 128).astype(BF16)
        blocks.append(dot(place, rows))
    totals = []
    for w in range(2):
        total = jnp.concatenate(
            [
                jnp.concatenate([b[128 * w:128 * w + 64], b[128 * w + 64:128 * w + 128]], axis=1)
                for b in blocks
            ],
            axis=0,
        ) + CENTRE * counts[w]
        total_ref[w] = total
        totals.append(total)
    image = [[image_ref[w, part].astype(F32) for part in range(2)] for w in range(2)]
    relaxed = from_far_field(far_ref[...], totals, counts, image, probe_ref, forward_ref, inverse_ref)
    write_relaxed(relaxed, relaxed_ref, edge_refs)


def second_kernel(
    dev_ref, in_ref, up_own, up_in, down_own, down_in, total_ref, count_ref, probe_ref, forward_ref, inverse_ref,
    relaxed_ref, *edge_refs
):
    image = smooth(dev_ref[0], in_ref, (up_own, up_in, down_own, down_in))
    far = to_far_field(image, probe_ref, forward_ref, inverse_ref)
    totals = [total_ref[w] for w in range(2)]
    relaxed = from_far_field(far, totals, own_counts(count_ref), image, probe_ref, forward_ref, inverse_ref)
    write_relaxed(relaxed, relaxed_ref, edge_refs)


def last_kernel(dev_ref, in_ref, up_own, up_in, down_own, down_in, out_ref):
    image = smooth(dev_ref[0], in_ref, (up_own, up_in, down_own, down_in))
    for w in range(2):
        for part in range(2):
            low = image[w][part].astype(BF16)
            for k in range(16):
                i, j = k // 2, k % 2
                out_ref[k, w, part] = low[32 * i:32 * i + 32, 128 * j:128 * j + 128]


SCALAR = pl.BlockSpec(memory_space=pltpu.SMEM)
BLOCK = pl.BlockSpec(memory_space=pltpu.VMEM)
PAIR = jax.ShapeDtypeStruct((2, 2, SIDE, SIDE), F32)
EDGE = jax.ShapeDtypeStruct((8, SIDE), F32)


def exchange_edges(ahead, behind, up, down):
    devices = range(128)
    from_next = lax.ppermute(ahead, ALL, [(s, s // 16 * 16 + (s - 1) % 16) for s in devices])
    from_previous = lax.ppermute(behind, ALL, [(s, s // 16 * 16 + (s + 1) % 16) for s in devices])
    up, down = up + from_next, down + from_previous
    up_in = lax.ppermute(up, ALL, [(s, (s + 16) % 128) for s in devices])
    down_in = lax.ppermute(down, ALL, [(s, (s - 16) % 128) for s in devices])
    return up, up_in, down, down_in


def shards(object_tiles, amplitudes, probe, frame_pos):
    dev = lax.axis_index(ALL).astype(jnp.int32).reshape(1)
    forward, inverse = dft_blocks()

    pieces = lax.all_to_all(amplitude_pieces(frame_pos, amplitudes), ALL, 0, 0, tiled=True)
    tiles = lax.all_to_all(
        outbound_tiles(dev, object_tiles), ALL, 0, 0, axis_index_groups=GROUPS, tiled=True
    )
    sums, counts = window_sums(dev, pieces)
    far, image = pl.pallas_call(
        first_far_kernel,
        in_specs=[BLOCK] * 4,
        out_specs=[BLOCK] * 2,
        out_shape=[jax.ShapeDtypeStruct((512, 512), F32), jax.ShapeDtypeStruct((2, 2, SIDE, SIDE), BF16)],
        compiler_params=params(),
        name="first_far",
    )(tiles, probe, forward, inverse)
    sums = lax.all_to_all(sums, ALL, 0, 0, tiled=True)
    relaxed, totals, *edges = pl.pallas_call(
        first_back_kernel,
        in_specs=[BLOCK] * 7,
        out_specs=[BLOCK] * 6,
        out_shape=[PAIR, jax.ShapeDtypeStruct((2, SIDE, SIDE), F32)] + [EDGE] * 4,
        compiler_params=params(),
        name="first_back",
    )(far, image, sums, counts, probe, forward, inverse)
    relaxed, *edges = pl.pallas_call(
        second_kernel,
        in_specs=[SCALAR] + [BLOCK] * 10,
        out_specs=[BLOCK] * 5,
        out_shape=[PAIR] + [EDGE] * 4,
        compiler_params=params(),
        name="second_sweep",
    )(dev, relaxed, *exchange_edges(*edges), totals, counts, probe, forward, inverse)
    tiles = pl.pallas_call(
        last_kernel,
        in_specs=[SCALAR] + [BLOCK] * 5,
        out_specs=BLOCK,
        out_shape=jax.ShapeDtypeStruct((16, 2, 2, 32, 128), BF16),
        compiler_params=params(),
        name="last_smoothing",
    )(dev, relaxed, *exchange_edges(*edges))
    tiles = lax.all_to_all(tiles, ALL, 0, 0, axis_index_groups=GROUPS, tiled=True)
    return inbound_tiles(dev, tiles)


def solution(mesh):
    return jax.shard_map(
        shards,
        mesh=mesh,
        in_specs=(P(None, ALL, None, None), P(ALL, None, None), P(), P(ALL, None)),
        out_specs=P(None, ALL, None, None),
        check_vma=False,
    )
```

```python
import jax
import jax.numpy as jnp
import numpy as np
from jax import lax
from jax.experimental import pallas as pl
from jax.experimental.pallas import tpu as pltpu
from jax.sharding import PartitionSpec as P

FLOOR = 0.3
DELTA = 1.0
STEP = 0.1
EPS = 0.1
CENTRE = 1.75
F32 = jnp.float32
BF16 = jnp.bfloat16
SIDE = 256
ALL = ("frames", "obj")
GROUPS = [list(range(16 * g, 16 * g + 16)) for g in range(8)]
SCALAR = pl.BlockSpec(memory_space=pltpu.SMEM)
BLOCK = pl.BlockSpec(memory_space=pltpu.VMEM)
ANYWHERE = pl.BlockSpec(memory_space=pl.ANY)
PAIR = jax.ShapeDtypeStruct((2, 2, SIDE, SIDE), F32)
EDGE = jax.ShapeDtypeStruct((8, SIDE), F32)


def place_of(group, member):
    far = (member // 8) ^ (group & 1)
    along = member % 4
    chip = along + far * (7 - 2 * along)
    return 2 * chip + (((member // 4) & 1) ^ (chip & 1))


def member_of(group, place):
    chip = place // 2
    far = chip // 4
    along = chip + far * (7 - 2 * chip)
    return 8 * (far ^ (group & 1)) + 4 * ((place & 1) ^ (chip & 1)) + along


def partners(move):
    pairs = []
    for dev in range(128):
        group, place = move(dev // 16, place_of(dev // 16, dev % 16))
        group, place = group % 8, place % 16
        pairs.append((dev, 16 * group + member_of(group, place)))
    return pairs


def params(limit_mb=40):
    return pltpu.CompilerParams(vmem_limit_bytes=limit_mb << 20)


def dft_blocks():
    index = np.arange(SIDE)
    angle = (index[:, None] * index[None, :] % SIDE) * (2.0 * np.pi / SIDE)
    cosine, sine = np.cos(angle) / 16.0, np.sin(angle) / 16.0
    forward = np.block([[cosine, sine], [-sine, cosine]])
    return jnp.asarray(forward, F32).astype(BF16), jnp.asarray(forward.T, F32).astype(BF16)


def iota(shape, axis):
    return lax.broadcasted_iota(jnp.int32, shape, axis)


def dot(a, b):
    return jnp.dot(a, b, preferred_element_type=F32)


def picker(source_of):
    return (iota((256, 256), 1) == source_of(iota((256, 256), 0))).astype(F32).astype(BF16)


def window_rows(dev):
    group = dev // 16
    place = place_of(group, dev % 16)
    return group, place, [(2 * place + 8 * group + w) % 32 for w in range(2)]


def pieces_kernel(pos_ref, amp_ref, out_ref, amp, out, in_sem, out_sem):
    fetch = [
        pltpu.make_async_copy(amp_ref.at[:, pl.ds(64 * b, 64), :], amp.at[:, pl.ds(64 * b, 64), :], in_sem.at[b])
        for b in range(4)
    ]
    store = [
        pltpu.make_async_copy(out.at[pl.ds(32 * b, 32)], out_ref.at[pl.ds(32 * b, 32)], out_sem.at[b])
        for b in range(4)
    ]
    for copy in fetch:
        copy.start()
    swap = picker(lambda o: (o % 16) * 16 + o // 16)
    row, column = pos_ref[0:1, :], pos_ref[1:2, :]
    group = ((column + 2 * row) & 127) >> 4
    local = (row - 8 * group) & 31
    owner = ((local & 1) * 128 + 16 * group + member_of(group, local >> 1)).astype(F32)
    code = jnp.where(iota((16, 16), 0) == iota((16, 16), 1), owner, 0.0)
    code = jnp.sum(code, axis=1, keepdims=True)
    mine = (iota((16, 128), 1) & 15) == iota((16, 128), 0)
    code = jnp.sum(jnp.where(mine, code, 0.0), axis=0, keepdims=True)
    code = jnp.broadcast_to(code, (8, 128)).astype(BF16)
    for b in range(4):
        fetch[b].wait()
        for block in range(4 * b, 4 * b + 4):
            rows = amp[:, 16 * block:16 * block + 16, :].reshape(256, 256)
            turned = dot(swap, rows).astype(BF16)
            for part in range(8):
                quad, half = part // 2, part % 2
                out[8 * block + part, 0:64, :] = turned[64 * quad:64 * quad + 64, 128 * half:128 * half + 128]
                out[8 * block + part, 64:72, :] = code
        store[b].start()
    for copy in store:
        copy.wait()


def amplitude_pieces(frame_pos, amplitudes):
    return pl.pallas_call(
        pieces_kernel,
        in_specs=[BLOCK, ANYWHERE],
        out_specs=ANYWHERE,
        out_shape=jax.ShapeDtypeStruct((128, 72, 128), BF16),
        scratch_shapes=[
            pltpu.VMEM((16, 256, 256), BF16),
            pltpu.VMEM((128, 72, 128), BF16),
            pltpu.SemaphoreType.DMA((4,)),
            pltpu.SemaphoreType.DMA((4,)),
        ],
        compiler_params=params(60),
        name="amplitude_pieces",
    )(frame_pos.T, amplitudes)


def sums_kernel(dev_ref, in_ref, out_ref, count_ref, pieces, total_ref, number_ref, sem):
    fetch = [
        pltpu.make_async_copy(in_ref.at[pl.ds(32 * b, 32)], pieces.at[pl.ds(32 * b, 32)], sem.at[b])
        for b in range(4)
    ]
    for copy in fetch:
        copy.start()
    lane = iota((8, 128), 1)
    owner = iota((256, 128), 0).astype(F32)
    turn = picker(lambda o: (o % 8) * 32 + o // 8)
    for b in range(4):
        fetch[b].wait()
        members, values = [], []
        for t in range(4 * b, 4 * b + 4):
            code = jnp.zeros((8, 128), F32)
            for s in range(8):
                code = jnp.where((lane >> 4) == s, pieces[8 * t + s, 64:72, :].astype(F32), code)
            members.append((owner == jnp.tile(code, (32, 1))).astype(F32).astype(BF16))
            values.append(
                jnp.concatenate(
                    [pieces[8 * t:8 * t + 8, 16 * c:16 * c + 16, :].reshape(128, 128) for c in range(4)]
                    + [jnp.ones((128, 128), BF16)],
                    axis=1,
                )
            )
        total = dot(jnp.concatenate(members, axis=1), jnp.concatenate(values, axis=0))
        total_ref[...] = total if b == 0 else total_ref[...] + total
    for block in range(4):
        parts = []
        for w in range(2):
            rows = slice(128 * w + 32 * block, 128 * w + 32 * block + 32)
            mean = CENTRE * total_ref[rows, 512:640]
            for c in range(4):
                parts.append(total_ref[rows, 128 * c:128 * c + 128] - mean)
        stacked = jnp.concatenate(parts, axis=0).astype(BF16)
        out_ref[32 * block:32 * block + 32] = dot(turn, stacked).reshape(32, 8, 128).astype(BF16)
    number_ref[...] = total_ref[:, 512:640]
    for w in range(2):
        own = number_ref[pl.ds(dev_ref[0] + 128 * w, 1), :]
        count_ref[8 * w:8 * w + 8, :] = jnp.broadcast_to(own, (8, 128))


def window_sums(dev, arrived):
    return pl.pallas_call(
        sums_kernel,
        in_specs=[SCALAR, ANYWHERE],
        out_specs=[BLOCK] * 2,
        out_shape=[
            jax.ShapeDtypeStruct((128, 8, 128), BF16),
            jax.ShapeDtypeStruct((16, 128), F32),
        ],
        scratch_shapes=[
            pltpu.VMEM((128, 72, 128), BF16),
            pltpu.VMEM((256, 640), F32),
            pltpu.VMEM((256, 128), F32),
            pltpu.SemaphoreType.DMA((4,)),
        ],
        compiler_params=params(60),
        name="window_sums",
    )(dev, arrived)


def outbound_kernel(dev_ref, in_ref, *out_refs):
    dev = dev_ref[0]
    member = dev % 16
    shift = 8 * (dev // 16) + member // 2
    for s in range(4):
        for t in range(4):
            target = 4 * ((member // 4) ^ t) + (member + s) % 4
            for w in range(2):
                row = (shift + 2 * place_of(dev // 16, target) + w) % 32
                for part in range(2):
                    out_refs[s][t, w, part] = in_ref[part, row].astype(BF16)


def tiles_to_windows(dev, tiles):
    blocks = pl.pallas_call(
        outbound_kernel,
        in_specs=[SCALAR, BLOCK],
        out_specs=[BLOCK] * 4,
        out_shape=[jax.ShapeDtypeStruct((4, 2, 2, 32, 128), BF16)] * 4,
        compiler_params=params(),
        name="outbound_tiles",
    )(dev, tiles)
    blocks = list(blocks)
    for s in range(1, 4):
        blocks[s] = lax.ppermute(blocks[s], ALL, [(d, d // 4 * 4 + (d + s) % 4) for d in range(128)])
    return blocks


def windows_from_lines(blocks):
    blocks = [jnp.stack([block[t] for block in blocks]) for t in range(4)]
    for t in range(1, 4):
        blocks[t] = lax.ppermute(blocks[t], ALL, [(d, d ^ (4 * t)) for d in range(128)])
    return blocks


def to_far_field(image, probe_ref, forward_ref, inverse_ref):
    waves = []
    for w in range(2):
        real, imag = [image[w][part].astype(BF16).astype(F32) for part in range(2)]
        waves.append(
            [
                (probe_ref[0] * real - probe_ref[1] * imag).astype(BF16),
                (probe_ref[0] * imag + probe_ref[1] * real).astype(BF16),
            ]
        )
    wave = jnp.concatenate(
        [jnp.concatenate([waves[0][part], waves[1][part]], axis=1) for part in range(2)], axis=0
    )
    midway = dot(forward_ref[...], wave).astype(BF16)
    midway = jnp.concatenate(
        [
            jnp.concatenate([midway[:256, 256 * w:256 * w + 256], midway[256:, 256 * w:256 * w + 256]], axis=1)
            for w in range(2)
        ],
        axis=0,
    )
    return dot(midway, inverse_ref[...])


def from_far_field(far, totals, counts, image, probe_ref, forward_ref, inverse_ref):
    changes = []
    for w in range(2):
        real, imag = far[256 * w:256 * w + 256, :256], far[256 * w:256 * w + 256, 256:]
        power = jnp.maximum(real * real + imag * imag, FLOOR * FLOOR)
        scale = totals[w] * lax.rsqrt(power) - counts[w]
        changes.append([(real * scale).astype(BF16), (imag * scale).astype(BF16)])
    change = jnp.concatenate(
        [jnp.concatenate([changes[0][part], changes[1][part]], axis=1) for part in range(2)], axis=0
    )
    halfway = dot(inverse_ref[...], change).astype(BF16)
    halfway = jnp.concatenate(
        [
            jnp.concatenate([halfway[:256, 256 * w:256 * w + 256], halfway[256:, 256 * w:256 * w + 256]], axis=1)
            for w in range(2)
        ],
        axis=0,
    )
    returned = dot(halfway, forward_ref[...])
    intensity = probe_ref[0] * probe_ref[0] + probe_ref[1] * probe_ref[1]
    relaxed = []
    for w in range(2):
        real, imag = returned[256 * w:256 * w + 256, :256], returned[256 * w:256 * w + 256, 256:]
        weight = 1.0 / (counts[w] * intensity + DELTA)
        relaxed.append(
            [
                image[w][0] + (probe_ref[0] * real + probe_ref[1] * imag) * weight,
                image[w][1] + (probe_ref[0] * imag - probe_ref[1] * real) * weight,
            ]
        )
    return relaxed


def own_counts(count_ref):
    return [jnp.tile(count_ref[8 * w:8 * w + 8, :], (32, 2)) for w in range(2)]


def write_relaxed(dev, relaxed, relaxed_ref, own_ref, edge_refs):
    for w in range(2):
        for part in range(2):
            relaxed_ref[w, part] = relaxed[w][part]
    rows = columns_as_rows(
        [(relaxed[w][part], 255 * side) for w, side in ((0, 1), (1, 0), (1, 1), (0, 0)) for part in range(2)]
    )[:8]
    own_ref[...] = rows
    place = iota((8, 256), 0)
    ahead, behind = pltpu.roll(rows, 6, 0), pltpu.roll(rows, 4, 0)
    up, down = rows, pltpu.roll(rows, 6, 0)
    for w in range(2):
        for part in range(2):
            at = 2 * w + part
            up = jnp.where(place == at, pltpu.roll(relaxed[w][part][248:], (at - 7) % 8, 0), up)
            first = relaxed[w][part][:8]
            down = jnp.where(place == at, pltpu.roll(first, at, 0) if at else first, down)
    group, spot, _ = window_rows(dev)
    odd_group, odd_spot = (group & 1) == 1, (spot & 1) == 1
    for ref, odd, even_edge, odd_edge in (
        (edge_refs[0], odd_spot, behind, ahead),
        (edge_refs[1], odd_spot, ahead, behind),
        (edge_refs[2], odd_group, up, down),
        (edge_refs[3], odd_group, down, up),
        (edge_refs[4], odd_group, ahead, behind),
        (edge_refs[5], odd_group, behind, ahead),
    ):
        ref[...] = jnp.where(odd, odd_edge, even_edge)


def exchange_edges(edges):
    moves = []
    for odd in range(2):
        moves.append(lambda g, q, odd=odd: (g, q + 1 if q % 2 == odd else q - 1))
    for odd in range(2):
        moves.append(lambda g, q, odd=odd: (g + 1 if g % 2 == odd else g - 1, q))
    for odd in range(2):
        moves.append(lambda g, q, odd=odd: (g + 1, q - 1) if g % 2 == odd else (g - 1, q + 1))
    return [lax.ppermute(edge, ALL, partners(move)) for edge, move in zip(edges, moves)]


def descend(x, left, right, up, down, keep_left, keep_right, keep_up, keep_down):
    rows, lanes = x[0].shape
    lane, row, row8 = iota((rows, lanes), 1), iota((rows, lanes), 0), iota((8, lanes), 0)

    def wide(narrow):
        return jnp.concatenate([narrow] * (lanes // 128), axis=1)

    across, edge, below, top = [], [], [], []
    for part in range(2):
        next_lane = jnp.where(lane == lanes - 1, wide(right[part]), pltpu.roll(x[part], lanes - 1, 1))
        across.append(next_lane - x[part])
        edge.append(x[part][:, :128] - left[part])
        next_row = jnp.where(
            row == rows - 1, jnp.broadcast_to(down[part], (rows, lanes)), pltpu.roll(x[part], rows - 1, 0)
        )
        below.append(next_row - x[part])
        top.append(x[part][:8] - jnp.broadcast_to(up[part], (8, lanes)))
    across_weight, edge_weight, below_weight, top_weight = [
        lax.rsqrt(d[0] * d[0] + d[1] * d[1] + EPS) * keep
        for d, keep in ((across, keep_right), (edge, keep_left), (below, keep_down), (top, keep_up))
    ]
    result = []
    for part in range(2):
        to_right = across[part] * across_weight
        to_left = jnp.where(lane == 0, wide(edge[part] * edge_weight), pltpu.roll(to_right, 1, 1))
        to_below = below[part] * below_weight
        moved = pltpu.roll(to_below, 1, 0)
        to_above = jnp.concatenate(
            [jnp.where(row8 == 0, top[part] * top_weight, moved[:8]), moved[8:]], axis=0
        )
        result.append(x[part] - STEP * ((to_left - to_right) + (to_above - to_below)))
    return result


def to_lane(block, source, lane):
    shift = (lane - source) % 128
    return pltpu.roll(block, shift, 1) if shift else block


def smooth(dev, relaxed_ref, own_ref, halo_refs):
    group, spot, starts = window_rows(dev)
    odd_group, odd_spot = (group & 1) == 1, (spot & 1) == 1
    beside0, beside1, above0, above1, corner0, corner1 = [ref[...] for ref in halo_refs]
    extra = iota((8, 256), 0) >= 6
    up_own = jnp.where(extra, jnp.where(odd_spot, beside1, beside0), own_ref[...])
    down_own = jnp.where(extra, jnp.where(odd_spot, beside0, beside1), pltpu.roll(own_ref[...], 6, 0))
    up_in = jnp.where(extra, jnp.where(odd_group, corner0, corner1), jnp.where(odd_group, above0, above1))
    down_in = jnp.where(extra, jnp.where(odd_group, corner1, corner0), jnp.where(odd_group, above1, above0))
    lane8 = iota((8, 256), 1)
    left = jnp.where(lane8 < 32, pltpu.roll(up_in, 32, 1), pltpu.roll(up_own, 32, 1))
    right = jnp.where(lane8 >= 224, pltpu.roll(down_in, 224, 1), pltpu.roll(down_own, 224, 1))
    sides = jnp.concatenate([left, right, jnp.zeros((112, 256), F32)], axis=0).T
    lane, row = iota((256, 256), 1), iota((256, 256), 0)
    image = []
    for w in range(2):
        start = starts[w]
        wrapped = (row // 32 + start) >= 32
        column = (16 * group - 2 * start + jnp.where(wrapped, 64, 0)) & 127
        image.append(
            descend(
                [relaxed_ref[w, part] for part in range(2)],
                [to_lane(sides, 4 + 2 * w + part, 0) for part in range(2)],
                [to_lane(sides, 8 + 4 + 2 * (1 - w) + part, 127) for part in range(2)],
                [up_in[2 * w + part:2 * w + part + 1] for part in range(2)],
                [down_in[2 * w + part:2 * w + part + 1] for part in range(2)],
                (column[:, :128] != 0).astype(F32),
                jnp.logical_not((lane == 255) & (column == 126)).astype(F32),
                (start != 0).astype(F32),
                (((32 * start + row) & 1023) != 1023).astype(F32),
            )
        )
    return image


def first_far_kernel(
    dev_ref, in0_ref, in1_ref, in2_ref, in3_ref, probe_ref, forward_ref, inverse_ref, far_ref, image_ref, half_ref
):
    member = dev_ref[0] % 16
    for t, in_ref in enumerate((in0_ref, in1_ref, in2_ref, in3_ref)):
        for s in range(4):
            source = 4 * ((member // 4) ^ t) + (member - s) % 4
            rows = pl.ds(pl.multiple_of(source // 2 * 32, 32), 32)
            for w in range(2):
                for part in range(2):
                    half_ref[w, part, source % 2, rows, :] = in_ref[s, w, part]
    image = []
    for w in range(2):
        image.append([])
        for part in range(2):
            whole = jnp.concatenate([half_ref[w, part, 0], half_ref[w, part, 1]], axis=1)
            image_ref[w, part] = whole
            image[w].append(whole)
    far_ref[...] = to_far_field(image, probe_ref, forward_ref, inverse_ref)


def first_back_kernel(
    dev_ref, far_ref, image_ref, sums_ref, count_ref, probe_ref, forward_ref, inverse_ref, total_ref, relaxed_ref,
    own_ref, *edge_refs
):
    counts = own_counts(count_ref)

    def source(o):
        w, half, row = o // 128, (o // 64) % 2, o % 64
        return ((row // 4) * 2 + half) * 8 + w * 4 + row % 4

    place = picker(source)
    blocks = []
    for block in range(4):
        rows = sums_ref[32 * block:32 * block + 32].astype(F32).reshape(256, 128).astype(BF16)
        blocks.append(dot(place, rows))
    totals = []
    for w in range(2):
        total = jnp.concatenate(
            [
                jnp.concatenate([b[128 * w:128 * w + 64], b[128 * w + 64:128 * w + 128]], axis=1)
                for b in blocks
            ],
            axis=0,
        ) + CENTRE * counts[w]
        total_ref[w] = total
        totals.append(total)
    image = [[image_ref[w, part].astype(F32) for part in range(2)] for w in range(2)]
    relaxed = from_far_field(far_ref[...], totals, counts, image, probe_ref, forward_ref, inverse_ref)
    write_relaxed(dev_ref[0], relaxed, relaxed_ref, own_ref, edge_refs)


def columns_as_rows(columns):
    lane = iota((256, 128), 1)
    gathered = jnp.zeros((256, 128), F32)
    for place, (image, at) in enumerate(columns):
        block = image[:, at // 128 * 128:at // 128 * 128 + 128]
        gathered = jnp.where(lane == place, to_lane(block, at % 128, place), gathered)
    return gathered.T


def second_kernel(
    dev_ref, in_ref, own_in, in0, in1, in2, in3, in4, in5, total_ref, count_ref, probe_ref, forward_ref, inverse_ref,
    out_ref, extra_ref
):
    image = smooth(dev_ref[0], in_ref, own_in, (in0, in1, in2, in3, in4, in5))
    far = to_far_field(image, probe_ref, forward_ref, inverse_ref)
    totals = [total_ref[w] for w in range(2)]
    relaxed = from_far_field(far, totals, own_counts(count_ref), image, probe_ref, forward_ref, inverse_ref)
    planes = [relaxed[w][part] for w in range(2) for part in range(2)]
    rows = columns_as_rows([(plane, at) for at in (127, 255, 128, 0) for plane in planes])
    lines = {}
    place, lane = iota((8, 256), 0), iota((8, 128), 1)
    for names, both in (((127, 255), rows[0:8]), ((128, 0), rows[8:16])):
        skewed = both
        for q in range(1, 4):
            skewed = jnp.where((place & 3) == q, pltpu.roll(both, 32 * q, 1), skewed)
        for i in range(8):
            turned = (pltpu.roll(skewed, 256 - 32 * i, 1) if i else skewed)[:, :128]
            turned = jnp.where((lane >> 5) == (place[:, :128] & 3), turned, 0.0)
            for at, half in zip(names, (turned[0:4], turned[4:8])):
                lines[at, i] = jnp.sum(half, axis=0, keepdims=True)
    extra_ref[...] = jnp.zeros_like(extra_ref)
    for k in range(16):
        i, j = k // 2, k % 2
        across, other = slice(128 * j, 128 * j + 128), slice(128 - 128 * j, 256 - 128 * j)
        for q, plane in enumerate(planes):
            out_ref[k, 32 * q:32 * q + 32, :] = plane[32 * i:32 * i + 32, across].astype(BF16)
            if i > 0:
                extra_ref[k, q:q + 1, :] = plane[32 * i - 1:32 * i, across]
            if i < 7:
                extra_ref[k, 4 + q:5 + q, :] = plane[32 * i + 32:32 * i + 33, across]
            if k in (8, 9):
                extra_ref[k, 8 + q:9 + q, :] = plane[255:256, across]
            if k in (6, 7):
                extra_ref[k, 8 + q:9 + q, :] = plane[0:1, across]
        if j == 1:
            extra_ref[k, 12:13, :] = lines[127, i]
            if i < 7:
                extra_ref[k, 13:14, :] = lines[0, i + 1]
        else:
            if i > 0:
                extra_ref[k, 12:13, :] = lines[255, i - 1]
            extra_ref[k, 13:14, :] = lines[128, i]
        if k == 8:
            extra_ref[k, 14:15, :] = lines[255, 7]
        if k == 7:
            extra_ref[k, 14:15, :] = lines[0, 0]
        out_ref[k, 128:144, :] = extra_ref[k].astype(BF16)


def inner_kernel(dev_ref, in_ref, out_ref):
    dev = dev_ref[0]
    group, member = dev // 16, dev % 16
    i, j = member // 2, member % 2
    order = [member_of(group, place) for place in range(16)]
    extra = [in_ref[m, 128:144, :].astype(F32) for m in order]
    left = jnp.concatenate([e[12:13] for e in extra], axis=0)
    right = jnp.concatenate([e[13:14] for e in extra], axis=0)
    first_half = iota((16, 128), 1) < 64
    turned = pltpu.roll(left, 64, 1)
    left = jnp.where(j == 1, left, jnp.where(first_half, turned, pltpu.roll(turned, 15, 0)))
    turned = pltpu.roll(right, 64, 1)
    right = jnp.where(j == 0, right, jnp.where(first_half, pltpu.roll(turned, 1, 0), turned))
    fill = jnp.zeros((112, 128), F32)
    left = jnp.concatenate([left, fill], axis=0).T
    right = jnp.concatenate([right, fill], axis=0).T
    last_lane = (iota((32, 128), 1) == 127).astype(F32)
    last_row = (iota((32, 128), 0) == 31).astype(F32)
    for u in range(32):
        place, w = u // 2, u % 2
        tile_row = (u + 8 * group + i) % 32
        tile_column = (dev - 2 * tile_row) & 127
        near, q = extra[place], [2 * w, 2 * w + 1]
        image = descend(
            [in_ref[order[place], pl.ds(32 * at, 32), :].astype(F32) for at in q],
            [to_lane(left[32 * at:32 * at + 32], place, 0) for at in q],
            [to_lane(right[32 * at:32 * at + 32], place, 127) for at in q],
            [near[at:at + 1] for at in q],
            [near[4 + at:5 + at] for at in q],
            ((tile_column != 0) & (member != 0)).astype(F32),
            1.0 - last_lane * ((tile_column == 127) | (member == 15)).astype(F32),
            ((tile_row != 0) & (i != 0)).astype(F32),
            1.0 - last_row * ((tile_row == 31) | (i == 7)).astype(F32),
        )
        for part in range(2):
            out_ref[part, tile_row] = image[part]


def border_kernel(dev_ref, in_ref, beyond_ref, inner_ref, out_ref):
    dev = dev_ref[0]
    group, member = dev // 16, dev % 16
    out_ref[...] = inner_ref[...]
    tiles = []
    for u in range(32):
        tile_row = (u + 8 * group + member // 2) % 32
        at = [32 * (2 * (u % 2) + part) for part in range(2)]
        tiles.append((u // 2, u % 2, tile_row, (dev - 2 * tile_row) & 127, member_of(group, u // 2), at))

    def beyond(place):
        return beyond_ref[member_of(group + 1, place)].astype(F32)

    def pull(d, keep):
        weight = STEP * lax.rsqrt(d[0] * d[0] + d[1] * d[1] + EPS) * keep
        return [d[0] * weight, d[1] * weight]

    def rows(at_row, edge_row):
        here = iota((8, 128), 0) == at_row % 8
        start = at_row // 8 * 8
        for place, w, tile_row, _, source, at in tiles:
            block = beyond(place)
            d = []
            for part in range(2):
                own = in_ref[source, pl.ds(at[part] + start // 16 * 16, 16), :].astype(F32)
                row = 8 + 2 * w + part
                d.append(own[start % 16:start % 16 + 8] - jnp.broadcast_to(block[row:row + 1], (8, 128)))
            for part, change in enumerate(pull(d, (tile_row != edge_row).astype(F32))):
                slot = out_ref.at[part, tile_row]
                slot[start:start + 8, :] = slot[start:start + 8, :] - jnp.where(here, change, 0.0)

    def columns(at_lane, edge_column):
        here = iota((32, 128), 1) == at_lane
        side = jnp.concatenate([beyond(place)[14:15] for place in range(16)], axis=0)
        half = iota((16, 128), 1) < 64
        turned = pltpu.roll(side, 64, 1)
        if at_lane == 0:
            side = jnp.where(half, turned, pltpu.roll(turned, 15, 0))
        else:
            side = jnp.where(half, pltpu.roll(turned, 1, 0), turned)
        side = jnp.concatenate([side, jnp.zeros((112, 128), F32)], axis=0).T
        for place, w, tile_row, tile_column, source, at in tiles:
            d = []
            for part in range(2):
                own = in_ref[source, pl.ds(at[part], 32), :].astype(F32)
                d.append(own - to_lane(side[at[part]:at[part] + 32], place, at_lane))
            for part, change in enumerate(pull(d, (tile_column != edge_column).astype(F32))):
                out_ref[part, tile_row] = out_ref[part, tile_row] - jnp.where(here, change, 0.0)

    pl.when(member < 2)(lambda: rows(0, 0))
    pl.when(member >= 14)(lambda: rows(31, 31))
    pl.when(member == 0)(lambda: columns(0, 0))
    pl.when(member == 15)(lambda: columns(127, 127))


def shards(object_tiles, amplitudes, probe, frame_pos):
    dev = lax.axis_index(ALL).astype(jnp.int32).reshape(1)
    forward, inverse = dft_blocks()

    lines = tiles_to_windows(dev, object_tiles)
    pieces = lax.all_to_all(amplitude_pieces(frame_pos, amplitudes), ALL, 0, 0, tiled=True)
    sums, counts = window_sums(dev, pieces)
    lines, sums = lax.optimization_barrier((lines, sums))
    tiles = windows_from_lines(lines)
    far, image = pl.pallas_call(
        first_far_kernel,
        in_specs=[SCALAR] + [BLOCK] * 7,
        out_specs=[BLOCK] * 2,
        out_shape=[jax.ShapeDtypeStruct((512, 512), F32), jax.ShapeDtypeStruct((2, 2, SIDE, SIDE), BF16)],
        scratch_shapes=[pltpu.VMEM((2, 2, 2, SIDE, 128), BF16)],
        compiler_params=params(),
        name="first_far",
    )(dev, *tiles, probe, forward, inverse)
    sums = lax.all_to_all(sums, ALL, 0, 0, tiled=True)
    totals, relaxed, own, *edges = pl.pallas_call(
        first_back_kernel,
        in_specs=[SCALAR] + [BLOCK] * 7,
        out_specs=[BLOCK] * 9,
        out_shape=[jax.ShapeDtypeStruct((2, SIDE, SIDE), F32), PAIR] + [EDGE] * 7,
        compiler_params=params(),
        name="first_back",
    )(dev, far, image, sums, counts, probe, forward, inverse)
    tiles = pl.pallas_call(
        second_kernel,
        in_specs=[SCALAR] + [BLOCK] * 13,
        out_specs=BLOCK,
        out_shape=jax.ShapeDtypeStruct((16, 144, 128), BF16),
        scratch_shapes=[pltpu.VMEM((16, 16, 128), F32)],
        compiler_params=params(),
        name="second_sweep",
    )(dev, relaxed, own, *exchange_edges(edges), totals, counts, probe, forward, inverse)
    tiles = lax.all_to_all(tiles, ALL, 0, 0, axis_index_groups=GROUPS, tiled=True)
    turns = ((8, 16), (9, 17), (7, -1), (6, -2))
    beyond = lax.ppermute(
        tiles[:, 128:], ALL, [(16 * g + k, (16 * g + to) % 128) for g in range(8) for k, to in turns]
    )
    result = jax.ShapeDtypeStruct((2, 32, 32, 128), F32)
    inner = pl.pallas_call(
        inner_kernel,
        in_specs=[SCALAR, BLOCK],
        out_specs=BLOCK,
        out_shape=result,
        compiler_params=params(),
        name="last_smoothing",
    )(dev, tiles)
    return pl.pallas_call(
        border_kernel,
        in_specs=[SCALAR] + [BLOCK] * 3,
        out_specs=BLOCK,
        out_shape=result,
        compiler_params=params(),
        name="last_borders",
    )(dev, tiles, beyond, inner)


def solution(mesh):
    return jax.shard_map(
        shards,
        mesh=mesh,
        in_specs=(P(None, ALL, None, None), P(ALL, None, None), P(), P(ALL, None)),
        out_specs=P(None, ALL, None, None),
        check_vma=False,
    )
```

```python
import jax
import jax.numpy as jnp
import numpy as np
from jax import lax
from jax.experimental import pallas as pl
from jax.experimental.pallas import tpu as pltpu
from jax.sharding import PartitionSpec as P

FLOOR = 0.3
DELTA = 1.0
STEP = 0.1
EPS = 0.1
CENTRE = 1.75
F32 = jnp.float32
BF16 = jnp.bfloat16
SIDE = 256
ALL = ("frames", "obj")
GROUPS = [list(range(16 * g, 16 * g + 16)) for g in range(8)]
SCALAR = pl.BlockSpec(memory_space=pltpu.SMEM)
BLOCK = pl.BlockSpec(memory_space=pltpu.VMEM)
ANYWHERE = pl.BlockSpec(memory_space=pl.ANY)
PAIR = jax.ShapeDtypeStruct((2, 2, SIDE, SIDE), F32)
EDGE = jax.ShapeDtypeStruct((8, SIDE), F32)


def place_of(group, member):
    far = (member // 8) ^ (group & 1)
    along = member % 4
    chip = along + far * (7 - 2 * along)
    return 2 * chip + (((member // 4) & 1) ^ (chip & 1))


def member_of(group, place):
    chip = place // 2
    far = chip // 4
    along = chip + far * (7 - 2 * chip)
    return 8 * (far ^ (group & 1)) + 4 * ((place & 1) ^ (chip & 1)) + along


def partners(move):
    pairs = []
    for dev in range(128):
        group, place = move(dev // 16, place_of(dev // 16, dev % 16))
        group, place = group % 8, place % 16
        pairs.append((dev, 16 * group + member_of(group, place)))
    return pairs


def params(limit_mb=40):
    return pltpu.CompilerParams(vmem_limit_bytes=limit_mb << 20)


def dft_blocks():
    index = np.arange(SIDE)
    angle = (index[:, None] * index[None, :] % SIDE) * (2.0 * np.pi / SIDE)
    cosine, sine = np.cos(angle) / 16.0, np.sin(angle) / 16.0
    forward = np.block([[cosine, sine], [-sine, cosine]])
    return jnp.asarray(forward, F32).astype(BF16), jnp.asarray(forward.T, F32).astype(BF16)


def iota(shape, axis):
    return lax.broadcasted_iota(jnp.int32, shape, axis)


def dot(a, b):
    return jnp.dot(a, b, preferred_element_type=F32)


def picker(source_of):
    return (iota((256, 256), 1) == source_of(iota((256, 256), 0))).astype(F32).astype(BF16)


def window_rows(dev):
    group = dev // 16
    place = place_of(group, dev % 16)
    return group, place, [(2 * place + 8 * group + w) % 32 for w in range(2)]


def pieces_kernel(pos_ref, amp_ref, out_ref, amp, out, in_sem, out_sem):
    fetch = [
        pltpu.make_async_copy(amp_ref.at[:, pl.ds(64 * b, 64), :], amp.at[:, pl.ds(64 * b, 64), :], in_sem.at[b])
        for b in range(4)
    ]
    store = [
        pltpu.make_async_copy(out.at[pl.ds(32 * b, 32)], out_ref.at[pl.ds(32 * b, 32)], out_sem.at[b])
        for b in range(4)
    ]
    for copy in fetch:
        copy.start()
    swap = picker(lambda o: (o % 16) * 16 + o // 16)
    row, column = pos_ref[0:1, :], pos_ref[1:2, :]
    group = ((column + 2 * row) & 127) >> 4
    local = (row - 8 * group) & 31
    owner = ((local & 1) * 128 + 16 * group + member_of(group, local >> 1)).astype(F32)
    code = jnp.where(iota((16, 16), 0) == iota((16, 16), 1), owner, 0.0)
    code = jnp.sum(code, axis=1, keepdims=True)
    mine = (iota((16, 128), 1) & 15) == iota((16, 128), 0)
    code = jnp.sum(jnp.where(mine, code, 0.0), axis=0, keepdims=True)
    code = jnp.broadcast_to(code, (8, 128)).astype(BF16)
    for b in range(4):
        fetch[b].wait()
        for block in range(4 * b, 4 * b + 4):
            rows = amp[:, 16 * block:16 * block + 16, :].reshape(256, 256)
            turned = dot(swap, rows).astype(BF16)
            for part in range(8):
                quad, half = part // 2, part % 2
                out[8 * block + part, 0:64, :] = turned[64 * quad:64 * quad + 64, 128 * half:128 * half + 128]
                out[8 * block + part, 64:72, :] = code
        store[b].start()
    for copy in store:
        copy.wait()


def amplitude_pieces(frame_pos, amplitudes):
    return pl.pallas_call(
        pieces_kernel,
        in_specs=[BLOCK, ANYWHERE],
        out_specs=ANYWHERE,
        out_shape=jax.ShapeDtypeStruct((128, 72, 128), BF16),
        scratch_shapes=[
            pltpu.VMEM((16, 256, 256), BF16),
            pltpu.VMEM((128, 72, 128), BF16),
            pltpu.SemaphoreType.DMA((4,)),
            pltpu.SemaphoreType.DMA((4,)),
        ],
        compiler_params=params(60),
        name="amplitude_pieces",
    )(frame_pos.T, amplitudes)


def sums_kernel(dev_ref, in_ref, out_ref, count_ref, pieces, total_ref, number_ref, sem):
    fetch = [
        pltpu.make_async_copy(in_ref.at[pl.ds(32 * b, 32)], pieces.at[pl.ds(32 * b, 32)], sem.at[b])
        for b in range(4)
    ]
    for copy in fetch:
        copy.start()
    lane = iota((8, 128), 1)
    owner = iota((256, 128), 0).astype(F32)
    turn = picker(lambda o: (o % 8) * 32 + o // 8)
    for b in range(4):
        fetch[b].wait()
        members, values = [], []
        for t in range(4 * b, 4 * b + 4):
            code = jnp.zeros((8, 128), F32)
            for s in range(8):
                code = jnp.where((lane >> 4) == s, pieces[8 * t + s, 64:72, :].astype(F32), code)
            members.append((owner == jnp.tile(code, (32, 1))).astype(F32).astype(BF16))
            values.append(
                jnp.concatenate(
                    [pieces[8 * t:8 * t + 8, 16 * c:16 * c + 16, :].reshape(128, 128) for c in range(4)]
                    + [jnp.ones((128, 128), BF16)],
                    axis=1,
                )
            )
        total = dot(jnp.concatenate(members, axis=1), jnp.concatenate(values, axis=0))
        total_ref[...] = total if b == 0 else total_ref[...] + total
    for block in range(4):
        parts = []
        for w in range(2):
            rows = slice(128 * w + 32 * block, 128 * w + 32 * block + 32)
            mean = CENTRE * total_ref[rows, 512:640]
            for c in range(4):
                parts.append(total_ref[rows, 128 * c:128 * c + 128] - mean)
        stacked = jnp.concatenate(parts, axis=0).astype(BF16)
        out_ref[32 * block:32 * block + 32] = dot(turn, stacked).reshape(32, 8, 128).astype(BF16)
    number_ref[...] = total_ref[:, 512:640]
    for w in range(2):
        own = number_ref[pl.ds(dev_ref[0] + 128 * w, 1), :]
        count_ref[8 * w:8 * w + 8, :] = jnp.broadcast_to(own, (8, 128))


def window_sums(dev, arrived):
    return pl.pallas_call(
        sums_kernel,
        in_specs=[SCALAR, ANYWHERE],
        out_specs=[BLOCK] * 2,
        out_shape=[
            jax.ShapeDtypeStruct((128, 8, 128), BF16),
            jax.ShapeDtypeStruct((16, 128), F32),
        ],
        scratch_shapes=[
            pltpu.VMEM((128, 72, 128), BF16),
            pltpu.VMEM((256, 640), F32),
            pltpu.VMEM((256, 128), F32),
            pltpu.SemaphoreType.DMA((4,)),
        ],
        compiler_params=params(60),
        name="window_sums",
    )(dev, arrived)


def outbound_kernel(dev_ref, in_ref, *out_refs):
    dev = dev_ref[0]
    member = dev % 16
    shift = 8 * (dev // 16) + member // 2
    for s in range(4):
        for t in range(4):
            target = 4 * ((member // 4) ^ t) + (member + s) % 4
            for w in range(2):
                row = (shift + 2 * place_of(dev // 16, target) + w) % 32
                for part in range(2):
                    out_refs[s][t, w, part] = in_ref[part, row].astype(BF16)


def tiles_to_windows(dev, tiles):
    blocks = pl.pallas_call(
        outbound_kernel,
        in_specs=[SCALAR, BLOCK],
        out_specs=[BLOCK] * 4,
        out_shape=[jax.ShapeDtypeStruct((4, 2, 2, 32, 128), BF16)] * 4,
        compiler_params=params(),
        name="outbound_tiles",
    )(dev, tiles)
    blocks = list(blocks)
    for s in (2, 1, 3):
        blocks[s] = lax.ppermute(blocks[s], ALL, [(d, d // 4 * 4 + (d + s) % 4) for d in range(128)])
    return blocks


def windows_from_lines(blocks):
    blocks = [jnp.stack([block[t] for block in blocks]) for t in range(4)]
    for t in (3, 2, 1):
        blocks[t] = lax.ppermute(blocks[t], ALL, [(d, d ^ (4 * t)) for d in range(128)])
    return blocks


def to_far_field(image, probe_ref, forward_ref, inverse_ref):
    waves = []
    for w in range(2):
        real, imag = [image[w][part].astype(BF16).astype(F32) for part in range(2)]
        waves.append(
            [
                (probe_ref[0] * real - probe_ref[1] * imag).astype(BF16),
                (probe_ref[0] * imag + probe_ref[1] * real).astype(BF16),
            ]
        )
    wave = jnp.concatenate(
        [jnp.concatenate([waves[0][part], waves[1][part]], axis=1) for part in range(2)], axis=0
    )
    midway = dot(forward_ref[...], wave).astype(BF16)
    midway = jnp.concatenate(
        [
            jnp.concatenate([midway[:256, 256 * w:256 * w + 256], midway[256:, 256 * w:256 * w + 256]], axis=1)
            for w in range(2)
        ],
        axis=0,
    )
    return dot(midway, inverse_ref[...])


def from_far_field(far, totals, counts, image, probe_ref, forward_ref, inverse_ref):
    changes = []
    for w in range(2):
        real, imag = far[256 * w:256 * w + 256, :256], far[256 * w:256 * w + 256, 256:]
        power = jnp.maximum(real * real + imag * imag, FLOOR * FLOOR)
        scale = totals[w] * lax.rsqrt(power) - counts[w]
        changes.append([(real * scale).astype(BF16), (imag * scale).astype(BF16)])
    change = jnp.concatenate(
        [jnp.concatenate([changes[0][part], changes[1][part]], axis=1) for part in range(2)], axis=0
    )
    halfway = dot(inverse_ref[...], change).astype(BF16)
    halfway = jnp.concatenate(
        [
            jnp.concatenate([halfway[:256, 256 * w:256 * w + 256], halfway[256:, 256 * w:256 * w + 256]], axis=1)
            for w in range(2)
        ],
        axis=0,
    )
    returned = dot(halfway, forward_ref[...])
    intensity = probe_ref[0] * probe_ref[0] + probe_ref[1] * probe_ref[1]
    relaxed = []
    for w in range(2):
        real, imag = returned[256 * w:256 * w + 256, :256], returned[256 * w:256 * w + 256, 256:]
        weight = 1.0 / (counts[w] * intensity + DELTA)
        relaxed.append(
            [
                image[w][0] + (probe_ref[0] * real + probe_ref[1] * imag) * weight,
                image[w][1] + (probe_ref[0] * imag - probe_ref[1] * real) * weight,
            ]
        )
    return relaxed


def own_counts(count_ref):
    return [jnp.tile(count_ref[8 * w:8 * w + 8, :], (32, 2)) for w in range(2)]


def write_relaxed(dev, relaxed, relaxed_ref, own_ref, edge_refs):
    for w in range(2):
        for part in range(2):
            relaxed_ref[w, part] = relaxed[w][part]
    rows = columns_as_rows(
        [(relaxed[w][part], 255 * side) for w, side in ((0, 1), (1, 0), (1, 1), (0, 0)) for part in range(2)]
    )[:8]
    own_ref[...] = rows
    place = iota((8, 256), 0)
    ahead, behind = pltpu.roll(rows, 6, 0), pltpu.roll(rows, 4, 0)
    up, down = rows, pltpu.roll(rows, 6, 0)
    for w in range(2):
        for part in range(2):
            at = 2 * w + part
            up = jnp.where(place == at, pltpu.roll(relaxed[w][part][248:], (at - 7) % 8, 0), up)
            first = relaxed[w][part][:8]
            down = jnp.where(place == at, pltpu.roll(first, at, 0) if at else first, down)
    group, spot, _ = window_rows(dev)
    odd_group, odd_spot = (group & 1) == 1, (spot & 1) == 1
    for ref, odd, even_edge, odd_edge in (
        (edge_refs[0], odd_group, behind, ahead),
        (edge_refs[1], odd_group, ahead, behind),
        (edge_refs[2], odd_group, down, up),
        (edge_refs[3], odd_group, up, down),
        (edge_refs[4], odd_spot, ahead, behind),
        (edge_refs[5], odd_spot, behind, ahead),
    ):
        ref[...] = jnp.where(odd, odd_edge, even_edge)


def exchange_edges(edges):
    moves = []
    for odd in (1, 0):
        moves.append(lambda g, q, odd=odd: (g + 1, q - 1) if g % 2 == odd else (g - 1, q + 1))
    for odd in (1, 0):
        moves.append(lambda g, q, odd=odd: (g + 1 if g % 2 == odd else g - 1, q))
    for odd in (1, 0):
        moves.append(lambda g, q, odd=odd: (g, q + 1 if q % 2 == odd else q - 1))
    return [lax.ppermute(edge, ALL, partners(move)) for edge, move in zip(edges, moves)]


def descend(x, left, right, up, down, keep_left, keep_right, keep_up, keep_down):
    rows, lanes = x[0].shape
    lane, row, row8 = iota((rows, lanes), 1), iota((rows, lanes), 0), iota((8, lanes), 0)

    def wide(narrow):
        return jnp.concatenate([narrow] * (lanes // 128), axis=1)

    across, edge, below, top = [], [], [], []
    for part in range(2):
        next_lane = jnp.where(lane == lanes - 1, wide(right[part]), pltpu.roll(x[part], lanes - 1, 1))
        across.append(next_lane - x[part])
        edge.append(x[part][:, :128] - left[part])
        next_row = jnp.where(
            row == rows - 1, jnp.broadcast_to(down[part], (rows, lanes)), pltpu.roll(x[part], rows - 1, 0)
        )
        below.append(next_row - x[part])
        top.append(x[part][:8] - jnp.broadcast_to(up[part], (8, lanes)))
    across_weight, edge_weight, below_weight, top_weight = [
        lax.rsqrt(d[0] * d[0] + d[1] * d[1] + EPS) * keep
        for d, keep in ((across, keep_right), (edge, keep_left), (below, keep_down), (top, keep_up))
    ]
    result = []
    for part in range(2):
        to_right = across[part] * across_weight
        to_left = jnp.where(lane == 0, wide(edge[part] * edge_weight), pltpu.roll(to_right, 1, 1))
        to_below = below[part] * below_weight
        moved = pltpu.roll(to_below, 1, 0)
        to_above = jnp.concatenate(
            [jnp.where(row8 == 0, top[part] * top_weight, moved[:8]), moved[8:]], axis=0
        )
        result.append(x[part] - STEP * ((to_left - to_right) + (to_above - to_below)))
    return result


def to_lane(block, source, lane):
    shift = (lane - source) % 128
    return pltpu.roll(block, shift, 1) if shift else block


def smooth(dev, relaxed_ref, own_ref, halo_refs):
    group, spot, starts = window_rows(dev)
    odd_group, odd_spot = (group & 1) == 1, (spot & 1) == 1
    corner1, corner0, above1, above0, beside1, beside0 = [ref[...] for ref in halo_refs]
    extra = iota((8, 256), 0) >= 6
    up_own = jnp.where(extra, jnp.where(odd_spot, beside1, beside0), own_ref[...])
    down_own = jnp.where(extra, jnp.where(odd_spot, beside0, beside1), pltpu.roll(own_ref[...], 6, 0))
    up_in = jnp.where(extra, jnp.where(odd_group, corner0, corner1), jnp.where(odd_group, above0, above1))
    down_in = jnp.where(extra, jnp.where(odd_group, corner1, corner0), jnp.where(odd_group, above1, above0))
    lane8 = iota((8, 256), 1)
    left = jnp.where(lane8 < 32, pltpu.roll(up_in, 32, 1), pltpu.roll(up_own, 32, 1))
    right = jnp.where(lane8 >= 224, pltpu.roll(down_in, 224, 1), pltpu.roll(down_own, 224, 1))
    sides = jnp.concatenate([left, right, jnp.zeros((112, 256), F32)], axis=0).T
    lane, row = iota((256, 256), 1), iota((256, 256), 0)
    image = []
    for w in range(2):
        start = starts[w]
        wrapped = (row // 32 + start) >= 32
        column = (16 * group - 2 * start + jnp.where(wrapped, 64, 0)) & 127
        image.append(
            descend(
                [relaxed_ref[w, part] for part in range(2)],
                [to_lane(sides, 4 + 2 * w + part, 0) for part in range(2)],
                [to_lane(sides, 8 + 4 + 2 * (1 - w) + part, 127) for part in range(2)],
                [up_in[2 * w + part:2 * w + part + 1] for part in range(2)],
                [down_in[2 * w + part:2 * w + part + 1] for part in range(2)],
                (column[:, :128] != 0).astype(F32),
                jnp.logical_not((lane == 255) & (column == 126)).astype(F32),
                (start != 0).astype(F32),
                (((32 * start + row) & 1023) != 1023).astype(F32),
            )
        )
    return image


def first_kernel(
    dev_ref, in0_ref, in1_ref, in2_ref, in3_ref, sums_ref, count_ref, probe_ref, forward_ref, inverse_ref, total_ref,
    relaxed_ref, own_ref, *more_refs
):
    *edge_refs, half_ref = more_refs
    member = dev_ref[0] % 16
    for t, in_ref in enumerate((in0_ref, in1_ref, in2_ref, in3_ref)):
        for s in range(4):
            source = 4 * ((member // 4) ^ t) + (member - s) % 4
            rows = pl.ds(pl.multiple_of(source // 2 * 32, 32), 32)
            for w in range(2):
                for part in range(2):
                    half_ref[w, part, source % 2, rows, :] = in_ref[s, w, part]
    image = [
        [jnp.concatenate([half_ref[w, part, 0], half_ref[w, part, 1]], axis=1).astype(F32) for part in range(2)]
        for w in range(2)
    ]
    far = to_far_field(image, probe_ref, forward_ref, inverse_ref)
    counts = own_counts(count_ref)

    def source(o):
        w, half, row = o // 128, (o // 64) % 2, o % 64
        return ((row // 4) * 2 + half) * 8 + w * 4 + row % 4

    place = picker(source)
    blocks = []
    for block in range(4):
        rows = sums_ref[32 * block:32 * block + 32].astype(F32).reshape(256, 128).astype(BF16)
        blocks.append(dot(place, rows))
    totals = []
    for w in range(2):
        total = jnp.concatenate(
            [
                jnp.concatenate([b[128 * w:128 * w + 64], b[128 * w + 64:128 * w + 128]], axis=1)
                for b in blocks
            ],
            axis=0,
        ) + CENTRE * counts[w]
        total_ref[w] = total
        totals.append(total)
    relaxed = from_far_field(far, totals, counts, image, probe_ref, forward_ref, inverse_ref)
    write_relaxed(dev_ref[0], relaxed, relaxed_ref, own_ref, edge_refs)


def columns_as_rows(columns):
    lane = iota((256, 128), 1)
    gathered = jnp.zeros((256, 128), F32)
    for place, (image, at) in enumerate(columns):
        block = image[:, at // 128 * 128:at // 128 * 128 + 128]
        gathered = jnp.where(lane == place, to_lane(block, at % 128, place), gathered)
    return gathered.T


def second_kernel(
    dev_ref, in_ref, own_in, in0, in1, in2, in3, in4, in5, total_ref, count_ref, probe_ref, forward_ref, inverse_ref,
    out_ref, extra_ref
):
    image = smooth(dev_ref[0], in_ref, own_in, (in0, in1, in2, in3, in4, in5))
    far = to_far_field(image, probe_ref, forward_ref, inverse_ref)
    totals = [total_ref[w] for w in range(2)]
    relaxed = from_far_field(far, totals, own_counts(count_ref), image, probe_ref, forward_ref, inverse_ref)
    planes = [relaxed[w][part] for w in range(2) for part in range(2)]
    rows = columns_as_rows([(plane, at) for at in (127, 255, 128, 0) for plane in planes])
    lines = {}
    place, lane = iota((8, 256), 0), iota((8, 128), 1)
    for names, both in (((127, 255), rows[0:8]), ((128, 0), rows[8:16])):
        skewed = both
        for q in range(1, 4):
            skewed = jnp.where((place & 3) == q, pltpu.roll(both, 32 * q, 1), skewed)
        for i in range(8):
            turned = (pltpu.roll(skewed, 256 - 32 * i, 1) if i else skewed)[:, :128]
            turned = jnp.where((lane >> 5) == (place[:, :128] & 3), turned, 0.0)
            for at, half in zip(names, (turned[0:4], turned[4:8])):
                lines[at, i] = jnp.sum(half, axis=0, keepdims=True)
    extra_ref[...] = jnp.zeros_like(extra_ref)
    for k in range(16):
        i, j = k // 2, k % 2
        across, other = slice(128 * j, 128 * j + 128), slice(128 - 128 * j, 256 - 128 * j)
        for q, plane in enumerate(planes):
            out_ref[k, 32 * q:32 * q + 32, :] = plane[32 * i:32 * i + 32, across].astype(BF16)
            if i > 0:
                extra_ref[k, q:q + 1, :] = plane[32 * i - 1:32 * i, across]
            if i < 7:
                extra_ref[k, 4 + q:5 + q, :] = plane[32 * i + 32:32 * i + 33, across]
            if k in (8, 9):
                extra_ref[k, 8 + q:9 + q, :] = plane[255:256, across]
            if k in (6, 7):
                extra_ref[k, 8 + q:9 + q, :] = plane[0:1, across]
        if j == 1:
            extra_ref[k, 12:13, :] = lines[127, i]
            if i < 7:
                extra_ref[k, 13:14, :] = lines[0, i + 1]
        else:
            if i > 0:
                extra_ref[k, 12:13, :] = lines[255, i - 1]
            extra_ref[k, 13:14, :] = lines[128, i]
        if k == 8:
            extra_ref[k, 14:15, :] = lines[255, 7]
        if k == 7:
            extra_ref[k, 14:15, :] = lines[0, 0]
        out_ref[k, 128:144, :] = extra_ref[k].astype(BF16)


def inner_kernel(dev_ref, in_ref, out_ref):
    dev = dev_ref[0]
    group, member = dev // 16, dev % 16
    i, j = member // 2, member % 2
    order = [member_of(group, place) for place in range(16)]
    extra = [in_ref[m, 128:144, :].astype(F32) for m in order]
    left = jnp.concatenate([e[12:13] for e in extra], axis=0)
    right = jnp.concatenate([e[13:14] for e in extra], axis=0)
    first_half = iota((16, 128), 1) < 64
    turned = pltpu.roll(left, 64, 1)
    left = jnp.where(j == 1, left, jnp.where(first_half, turned, pltpu.roll(turned, 15, 0)))
    turned = pltpu.roll(right, 64, 1)
    right = jnp.where(j == 0, right, jnp.where(first_half, pltpu.roll(turned, 1, 0), turned))
    fill = jnp.zeros((112, 128), F32)
    left = jnp.concatenate([left, fill], axis=0).T
    right = jnp.concatenate([right, fill], axis=0).T
    last_lane = (iota((32, 128), 1) == 127).astype(F32)
    last_row = (iota((32, 128), 0) == 31).astype(F32)
    for u in range(32):
        place, w = u // 2, u % 2
        tile_row = (u + 8 * group + i) % 32
        tile_column = (dev - 2 * tile_row) & 127
        near, q = extra[place], [2 * w, 2 * w + 1]
        image = descend(
            [in_ref[order[place], pl.ds(32 * at, 32), :].astype(F32) for at in q],
            [to_lane(left[32 * at:32 * at + 32], place, 0) for at in q],
            [to_lane(right[32 * at:32 * at + 32], place, 127) for at in q],
            [near[at:at + 1] for at in q],
            [near[4 + at:5 + at] for at in q],
            ((tile_column != 0) & (member != 0)).astype(F32),
            1.0 - last_lane * ((tile_column == 127) | (member == 15)).astype(F32),
            ((tile_row != 0) & (i != 0)).astype(F32),
            1.0 - last_row * ((tile_row == 31) | (i == 7)).astype(F32),
        )
        for part in range(2):
            out_ref[part, tile_row] = image[part]


def border_kernel(dev_ref, in_ref, beyond_ref, inner_ref, out_ref):
    dev = dev_ref[0]
    group, member = dev // 16, dev % 16
    out_ref[...] = inner_ref[...]
    tiles = []
    for u in range(32):
        tile_row = (u + 8 * group + member // 2) % 32
        at = [32 * (2 * (u % 2) + part) for part in range(2)]
        tiles.append((u // 2, u % 2, tile_row, (dev - 2 * tile_row) & 127, member_of(group, u // 2), at))

    def beyond(place):
        return beyond_ref[member_of(group + 1, place)].astype(F32)

    def pull(d, keep):
        weight = STEP * lax.rsqrt(d[0] * d[0] + d[1] * d[1] + EPS) * keep
        return [d[0] * weight, d[1] * weight]

    def rows(at_row, edge_row):
        here = iota((8, 128), 0) == at_row % 8
        start = at_row // 8 * 8
        for place, w, tile_row, _, source, at in tiles:
            block = beyond(place)
            d = []
            for part in range(2):
                own = in_ref[source, pl.ds(at[part] + start // 16 * 16, 16), :].astype(F32)
                row = 2 * w + part
                d.append(own[start % 16:start % 16 + 8] - jnp.broadcast_to(block[row:row + 1], (8, 128)))
            for part, change in enumerate(pull(d, (tile_row != edge_row).astype(F32))):
                slot = out_ref.at[part, tile_row]
                slot[start:start + 8, :] = slot[start:start + 8, :] - jnp.where(here, change, 0.0)

    def columns(at_lane, edge_column):
        here = iota((32, 128), 1) == at_lane
        side = jnp.concatenate([beyond(place)[6:7] for place in range(16)], axis=0)
        half = iota((16, 128), 1) < 64
        turned = pltpu.roll(side, 64, 1)
        if at_lane == 0:
            side = jnp.where(half, turned, pltpu.roll(turned, 15, 0))
        else:
            side = jnp.where(half, pltpu.roll(turned, 1, 0), turned)
        side = jnp.concatenate([side, jnp.zeros((112, 128), F32)], axis=0).T
        for place, w, tile_row, tile_column, source, at in tiles:
            d = []
            for part in range(2):
                own = in_ref[source, pl.ds(at[part], 32), :].astype(F32)
                d.append(own - to_lane(side[at[part]:at[part] + 32], place, at_lane))
            for part, change in enumerate(pull(d, (tile_column != edge_column).astype(F32))):
                out_ref[part, tile_row] = out_ref[part, tile_row] - jnp.where(here, change, 0.0)

    pl.when(member < 2)(lambda: rows(0, 0))
    pl.when(member >= 14)(lambda: rows(31, 31))
    pl.when(member == 0)(lambda: columns(0, 0))
    pl.when(member == 15)(lambda: columns(127, 127))


def shards(object_tiles, amplitudes, probe, frame_pos):
    dev = lax.axis_index(ALL).astype(jnp.int32).reshape(1)
    forward, inverse = dft_blocks()

    lines = tiles_to_windows(dev, object_tiles)
    pieces = lax.all_to_all(amplitude_pieces(frame_pos, amplitudes), ALL, 0, 0, tiled=True)
    sums, counts = window_sums(dev, pieces)
    lines, sums = lax.optimization_barrier((lines, sums))
    tiles = windows_from_lines(lines)
    sums = lax.all_to_all(sums, ALL, 0, 0, tiled=True)
    totals, relaxed, own, *edges = pl.pallas_call(
        first_kernel,
        in_specs=[SCALAR] + [BLOCK] * 9,
        out_specs=[BLOCK] * 9,
        out_shape=[jax.ShapeDtypeStruct((2, SIDE, SIDE), F32), PAIR] + [EDGE] * 7,
        scratch_shapes=[pltpu.VMEM((2, 2, 2, SIDE, 128), BF16)],
        compiler_params=params(),
        name="first_sweep",
    )(dev, *tiles, sums, counts, probe, forward, inverse)
    tiles = pl.pallas_call(
        second_kernel,
        in_specs=[SCALAR] + [BLOCK] * 13,
        out_specs=BLOCK,
        out_shape=jax.ShapeDtypeStruct((16, 144, 128), BF16),
        scratch_shapes=[pltpu.VMEM((16, 16, 128), F32)],
        compiler_params=params(),
        name="second_sweep",
    )(dev, relaxed, own, *exchange_edges(edges), totals, counts, probe, forward, inverse)
    tiles = lax.all_to_all(tiles, ALL, 0, 0, axis_index_groups=GROUPS, tiled=True)
    turns = ((8, 16), (9, 17), (7, -1), (6, -2))
    beyond = lax.ppermute(
        tiles[:, 136:], ALL, [(16 * g + k, (16 * g + to) % 128) for g in range(8) for k, to in turns]
    )
    result = jax.ShapeDtypeStruct((2, 32, 32, 128), F32)
    inner = pl.pallas_call(
        inner_kernel,
        in_specs=[SCALAR, BLOCK],
        out_specs=BLOCK,
        out_shape=result,
        compiler_params=params(),
        name="last_smoothing",
    )(dev, tiles)
    return pl.pallas_call(
        border_kernel,
        in_specs=[SCALAR] + [BLOCK] * 3,
        out_specs=BLOCK,
        out_shape=result,
        compiler_params=params(),
        name="last_borders",
    )(dev, tiles, beyond, inner)


def solution(mesh):
    return jax.shard_map(
        shards,
        mesh=mesh,
        in_specs=(P(None, ALL, None, None), P(ALL, None, None), P(), P(ALL, None)),
        out_specs=P(None, ALL, None, None),
        check_vma=False,
    )
```

```python
import jax
import jax.numpy as jnp
import numpy as np
from jax import lax
from jax.experimental import pallas as pl
from jax.experimental.pallas import tpu as pltpu
from jax.sharding import PartitionSpec as P

FLOOR = 0.3
DELTA = 1.0
STEP = 0.1
EPS = 0.1
CENTRE = 1.75
F32 = jnp.float32
BF16 = jnp.bfloat16
SIDE = 256
ALL = ("frames", "obj")
GROUPS = [list(range(16 * g, 16 * g + 16)) for g in range(8)]
SCALAR = pl.BlockSpec(memory_space=pltpu.SMEM)
BLOCK = pl.BlockSpec(memory_space=pltpu.VMEM)
EARLY, LATE = (0, 6, 5, 7, 2, 3), (4, 1)
ANYWHERE = pl.BlockSpec(memory_space=pl.ANY)
PAIR = jax.ShapeDtypeStruct((2, 2, SIDE, SIDE), F32)
EDGE = jax.ShapeDtypeStruct((8, SIDE), F32)


def place_of(group, member):
    far = (member // 8) ^ (group & 1)
    along = member % 4
    chip = along + far * (7 - 2 * along)
    return 2 * chip + (((member // 4) & 1) ^ (chip & 1))


def member_of(group, place):
    chip = place // 2
    far = chip // 4
    along = chip + far * (7 - 2 * chip)
    return 8 * (far ^ (group & 1)) + 4 * ((place & 1) ^ (chip & 1)) + along


def partners(move):
    pairs = []
    for dev in range(128):
        group, place = move(dev // 16, place_of(dev // 16, dev % 16))
        group, place = group % 8, place % 16
        pairs.append((dev, 16 * group + member_of(group, place)))
    return pairs


def params(limit_mb=40):
    return pltpu.CompilerParams(vmem_limit_bytes=limit_mb << 20)


def dft_blocks():
    index = np.arange(SIDE)
    angle = (index[:, None] * index[None, :] % SIDE) * (2.0 * np.pi / SIDE)
    cosine, sine = np.cos(angle) / 16.0, np.sin(angle) / 16.0
    forward = np.block([[cosine, sine], [-sine, cosine]])
    return jnp.asarray(forward, F32).astype(BF16), jnp.asarray(forward.T, F32).astype(BF16)


def iota(shape, axis):
    return lax.broadcasted_iota(jnp.int32, shape, axis)


def dot(a, b):
    return jnp.dot(a, b, preferred_element_type=F32)


def picker(source_of):
    return (iota((256, 256), 1) == source_of(iota((256, 256), 0))).astype(F32).astype(BF16)


def window_rows(dev):
    group = dev // 16
    place = place_of(group, dev % 16)
    return group, place, [(2 * place + 8 * group + w) % 32 for w in range(2)]


def pieces_kernel(pos_ref, amp_ref, out_ref, amp, out, in_sem, out_sem):
    fetch = [
        pltpu.make_async_copy(amp_ref.at[:, pl.ds(64 * b, 64), :], amp.at[:, pl.ds(64 * b, 64), :], in_sem.at[b])
        for b in range(4)
    ]
    store = [
        pltpu.make_async_copy(out.at[pl.ds(32 * b, 32)], out_ref.at[pl.ds(32 * b, 32)], out_sem.at[b])
        for b in range(4)
    ]
    for copy in fetch:
        copy.start()
    swap = picker(lambda o: (o % 16) * 16 + o // 16)
    row, column = pos_ref[0:1, :], pos_ref[1:2, :]
    group = ((column + 2 * row) & 127) >> 4
    local = (row - 8 * group) & 31
    owner = ((local & 1) * 128 + 16 * group + member_of(group, local >> 1)).astype(F32)
    code = jnp.where(iota((16, 16), 0) == iota((16, 16), 1), owner, 0.0)
    code = jnp.sum(code, axis=1, keepdims=True)
    mine = (iota((16, 128), 1) & 15) == iota((16, 128), 0)
    code = jnp.sum(jnp.where(mine, code, 0.0), axis=0, keepdims=True)
    code = jnp.broadcast_to(code, (8, 128)).astype(BF16)
    for b in range(4):
        fetch[b].wait()
        for block in range(4 * b, 4 * b + 4):
            rows = amp[:, 16 * block:16 * block + 16, :].reshape(256, 256)
            turned = dot(swap, rows).astype(BF16)
            for part in range(8):
                quad, half = part // 2, part % 2
                out[8 * block + part, 0:64, :] = turned[64 * quad:64 * quad + 64, 128 * half:128 * half + 128]
                out[8 * block + part, 64:72, :] = code
        store[b].start()
    for copy in store:
        copy.wait()


def amplitude_pieces(frame_pos, amplitudes):
    return pl.pallas_call(
        pieces_kernel,
        in_specs=[BLOCK, ANYWHERE],
        out_specs=ANYWHERE,
        out_shape=jax.ShapeDtypeStruct((128, 72, 128), BF16),
        scratch_shapes=[
            pltpu.VMEM((16, 256, 256), BF16),
            pltpu.VMEM((128, 72, 128), BF16),
            pltpu.SemaphoreType.DMA((4,)),
            pltpu.SemaphoreType.DMA((4,)),
        ],
        compiler_params=params(60),
        name="amplitude_pieces",
    )(frame_pos.T, amplitudes)


def sums_kernel(dev_ref, in_ref, out_ref, count_ref, pieces, total_ref, number_ref, sem):
    fetch = [
        pltpu.make_async_copy(in_ref.at[pl.ds(32 * b, 32)], pieces.at[pl.ds(32 * b, 32)], sem.at[b])
        for b in range(4)
    ]
    for copy in fetch:
        copy.start()
    lane = iota((8, 128), 1)
    owner = iota((256, 128), 0).astype(F32)
    turn = picker(lambda o: (o % 8) * 32 + o // 8)
    for b in range(4):
        fetch[b].wait()
        members, values = [], []
        for t in range(4 * b, 4 * b + 4):
            code = jnp.zeros((8, 128), F32)
            for s in range(8):
                code = jnp.where((lane >> 4) == s, pieces[8 * t + s, 64:72, :].astype(F32), code)
            members.append((owner == jnp.tile(code, (32, 1))).astype(F32).astype(BF16))
            values.append(
                jnp.concatenate(
                    [pieces[8 * t:8 * t + 8, 16 * c:16 * c + 16, :].reshape(128, 128) for c in range(4)]
                    + [jnp.ones((128, 128), BF16)],
                    axis=1,
                )
            )
        total = dot(jnp.concatenate(members, axis=1), jnp.concatenate(values, axis=0))
        total_ref[...] = total if b == 0 else total_ref[...] + total
    for block in range(4):
        parts = []
        for w in range(2):
            rows = slice(128 * w + 32 * block, 128 * w + 32 * block + 32)
            mean = CENTRE * total_ref[rows, 512:640]
            for c in range(4):
                parts.append(total_ref[rows, 128 * c:128 * c + 128] - mean)
        stacked = jnp.concatenate(parts, axis=0).astype(BF16)
        out_ref[32 * block:32 * block + 32] = dot(turn, stacked).reshape(32, 8, 128).astype(BF16)
    number_ref[...] = total_ref[:, 512:640]
    for w in range(2):
        own = number_ref[pl.ds(dev_ref[0] + 128 * w, 1), :]
        count_ref[8 * w:8 * w + 8, :] = jnp.broadcast_to(own, (8, 128))


def window_sums(dev, arrived):
    return pl.pallas_call(
        sums_kernel,
        in_specs=[SCALAR, ANYWHERE],
        out_specs=[BLOCK] * 2,
        out_shape=[
            jax.ShapeDtypeStruct((128, 8, 128), BF16),
            jax.ShapeDtypeStruct((16, 128), F32),
        ],
        scratch_shapes=[
            pltpu.VMEM((128, 72, 128), BF16),
            pltpu.VMEM((256, 640), F32),
            pltpu.VMEM((256, 128), F32),
            pltpu.SemaphoreType.DMA((4,)),
        ],
        compiler_params=params(60),
        name="window_sums",
    )(dev, arrived)


def outbound_kernel(dev_ref, in_ref, *out_refs):
    dev = dev_ref[0]
    member = dev % 16
    shift = 8 * (dev // 16) + member // 2
    for t in range(8):
        for e in range(2):
            target = member ^ (8 * (t // 4) + t % 4 + 4 * e)
            for w in range(2):
                row = (shift + 2 * place_of(dev // 16, target) + w) % 32
                for part in range(2):
                    out_refs[t][e, w, part] = in_ref[part, row].astype(BF16)


def tiles_to_windows(dev, tiles):
    blocks = pl.pallas_call(
        outbound_kernel,
        in_specs=[SCALAR, BLOCK],
        out_specs=[BLOCK] * 8,
        out_shape=[jax.ShapeDtypeStruct((2, 2, 2, 32, 128), BF16)] * 8,
        compiler_params=params(),
        name="outbound_tiles",
    )(dev, tiles)
    blocks = list(blocks)
    for t in EARLY[1:]:
        blocks[t] = across_chips(blocks[t], t)
    return blocks


def across_chips(block, t):
    return lax.ppermute(block, ALL, [(d, d ^ (8 * (t // 4) + t % 4)) for d in range(128)])


def windows_from_lines(blocks):
    for t in LATE:
        blocks[t] = across_chips(blocks[t], t)
    other = [
        lax.ppermute(jnp.stack([blocks[t][1] for t in part]), ALL, [(d, d ^ 4) for d in range(128)])
        for part in (EARLY, LATE)
    ]
    return blocks + other


def to_far_field(image, probe_ref, forward_ref, inverse_ref):
    waves = []
    for w in range(2):
        real, imag = [image[w][part].astype(BF16).astype(F32) for part in range(2)]
        waves.append(
            [
                (probe_ref[0] * real - probe_ref[1] * imag).astype(BF16),
                (probe_ref[0] * imag + probe_ref[1] * real).astype(BF16),
            ]
        )
    wave = jnp.concatenate(
        [jnp.concatenate([waves[0][part], waves[1][part]], axis=1) for part in range(2)], axis=0
    )
    midway = dot(forward_ref[...], wave).astype(BF16)
    midway = jnp.concatenate(
        [
            jnp.concatenate([midway[:256, 256 * w:256 * w + 256], midway[256:, 256 * w:256 * w + 256]], axis=1)
            for w in range(2)
        ],
        axis=0,
    )
    return dot(midway, inverse_ref[...])


def from_far_field(far, totals, counts, image, probe_ref, forward_ref, inverse_ref):
    changes = []
    for w in range(2):
        real, imag = far[256 * w:256 * w + 256, :256], far[256 * w:256 * w + 256, 256:]
        power = jnp.maximum(real * real + imag * imag, FLOOR * FLOOR)
        scale = totals[w] * lax.rsqrt(power) - counts[w]
        changes.append([(real * scale).astype(BF16), (imag * scale).astype(BF16)])
    change = jnp.concatenate(
        [jnp.concatenate([changes[0][part], changes[1][part]], axis=1) for part in range(2)], axis=0
    )
    halfway = dot(inverse_ref[...], change).astype(BF16)
    halfway = jnp.concatenate(
        [
            jnp.concatenate([halfway[:256, 256 * w:256 * w + 256], halfway[256:, 256 * w:256 * w + 256]], axis=1)
            for w in range(2)
        ],
        axis=0,
    )
    returned = dot(halfway, forward_ref[...])
    intensity = probe_ref[0] * probe_ref[0] + probe_ref[1] * probe_ref[1]
    relaxed = []
    for w in range(2):
        real, imag = returned[256 * w:256 * w + 256, :256], returned[256 * w:256 * w + 256, 256:]
        weight = 1.0 / (counts[w] * intensity + DELTA)
        relaxed.append(
            [
                image[w][0] + (probe_ref[0] * real + probe_ref[1] * imag) * weight,
                image[w][1] + (probe_ref[0] * imag - probe_ref[1] * real) * weight,
            ]
        )
    return relaxed


def own_counts(count_ref):
    return [jnp.tile(count_ref[8 * w:8 * w + 8, :], (32, 2)) for w in range(2)]


def write_relaxed(dev, relaxed, relaxed_ref, own_ref, edge_refs):
    for w in range(2):
        for part in range(2):
            relaxed_ref[w, part] = relaxed[w][part]
    rows = columns_as_rows(
        [(relaxed[w][part], 255 * side) for w, side in ((0, 1), (1, 0), (1, 1), (0, 0)) for part in range(2)]
    )[:8]
    own_ref[...] = rows
    place = iota((8, 256), 0)
    ahead, behind = pltpu.roll(rows, 6, 0), pltpu.roll(rows, 4, 0)
    up, down = rows, pltpu.roll(rows, 6, 0)
    for w in range(2):
        for part in range(2):
            at = 2 * w + part
            up = jnp.where(place == at, pltpu.roll(relaxed[w][part][248:], (at - 7) % 8, 0), up)
            first = relaxed[w][part][:8]
            down = jnp.where(place == at, pltpu.roll(first, at, 0) if at else first, down)
    group, spot, _ = window_rows(dev)
    odd_group, odd_spot = (group & 1) == 1, (spot & 1) == 1
    for ref, odd, even_edge, odd_edge in (
        (edge_refs[0], odd_group, behind, ahead),
        (edge_refs[1], odd_group, ahead, behind),
        (edge_refs[2], odd_group, down, up),
        (edge_refs[3], odd_group, up, down),
        (edge_refs[4], odd_spot, ahead, behind),
        (edge_refs[5], odd_spot, behind, ahead),
    ):
        ref[...] = jnp.where(odd, odd_edge, even_edge)


def exchange_edges(edges):
    moves = []
    for odd in (1, 0):
        moves.append(lambda g, q, odd=odd: (g + 1, q - 1) if g % 2 == odd else (g - 1, q + 1))
    for odd in (1, 0):
        moves.append(lambda g, q, odd=odd: (g + 1 if g % 2 == odd else g - 1, q))
    for odd in (1, 0):
        moves.append(lambda g, q, odd=odd: (g, q + 1 if q % 2 == odd else q - 1))
    return [lax.ppermute(edge, ALL, partners(move)) for edge, move in zip(edges, moves)]


def descend(x, left, right, up, down, keep_left, keep_right, keep_up, keep_down):
    rows, lanes = x[0].shape
    lane, row, row8 = iota((rows, lanes), 1), iota((rows, lanes), 0), iota((8, lanes), 0)

    def wide(narrow):
        return jnp.concatenate([narrow] * (lanes // 128), axis=1)

    across, edge, below, top = [], [], [], []
    for part in range(2):
        next_lane = jnp.where(lane == lanes - 1, wide(right[part]), pltpu.roll(x[part], lanes - 1, 1))
        across.append(next_lane - x[part])
        edge.append(x[part][:, :128] - left[part])
        next_row = jnp.where(
            row == rows - 1, jnp.broadcast_to(down[part], (rows, lanes)), pltpu.roll(x[part], rows - 1, 0)
        )
        below.append(next_row - x[part])
        top.append(x[part][:8] - jnp.broadcast_to(up[part], (8, lanes)))
    across_weight, edge_weight, below_weight, top_weight = [
        lax.rsqrt(d[0] * d[0] + d[1] * d[1] + EPS) * keep
        for d, keep in ((across, keep_right), (edge, keep_left), (below, keep_down), (top, keep_up))
    ]
    result = []
    for part in range(2):
        to_right = across[part] * across_weight
        to_left = jnp.where(lane == 0, wide(edge[part] * edge_weight), pltpu.roll(to_right, 1, 1))
        to_below = below[part] * below_weight
        moved = pltpu.roll(to_below, 1, 0)
        to_above = jnp.concatenate(
            [jnp.where(row8 == 0, top[part] * top_weight, moved[:8]), moved[8:]], axis=0
        )
        result.append(x[part] - STEP * ((to_left - to_right) + (to_above - to_below)))
    return result


def to_lane(block, source, lane):
    shift = (lane - source) % 128
    return pltpu.roll(block, shift, 1) if shift else block


def smooth(dev, relaxed_ref, own_ref, halo_refs):
    group, spot, starts = window_rows(dev)
    odd_group, odd_spot = (group & 1) == 1, (spot & 1) == 1
    corner1, corner0, above1, above0, beside1, beside0 = [ref[...] for ref in halo_refs]
    extra = iota((8, 256), 0) >= 6
    up_own = jnp.where(extra, jnp.where(odd_spot, beside1, beside0), own_ref[...])
    down_own = jnp.where(extra, jnp.where(odd_spot, beside0, beside1), pltpu.roll(own_ref[...], 6, 0))
    up_in = jnp.where(extra, jnp.where(odd_group, corner0, corner1), jnp.where(odd_group, above0, above1))
    down_in = jnp.where(extra, jnp.where(odd_group, corner1, corner0), jnp.where(odd_group, above1, above0))
    lane8 = iota((8, 256), 1)
    left = jnp.where(lane8 < 32, pltpu.roll(up_in, 32, 1), pltpu.roll(up_own, 32, 1))
    right = jnp.where(lane8 >= 224, pltpu.roll(down_in, 224, 1), pltpu.roll(down_own, 224, 1))
    sides = jnp.concatenate([left, right, jnp.zeros((112, 256), F32)], axis=0).T
    lane, row = iota((256, 256), 1), iota((256, 256), 0)
    image = []
    for w in range(2):
        start = starts[w]
        wrapped = (row // 32 + start) >= 32
        column = (16 * group - 2 * start + jnp.where(wrapped, 64, 0)) & 127
        image.append(
            descend(
                [relaxed_ref[w, part] for part in range(2)],
                [to_lane(sides, 4 + 2 * w + part, 0) for part in range(2)],
                [to_lane(sides, 8 + 4 + 2 * (1 - w) + part, 127) for part in range(2)],
                [up_in[2 * w + part:2 * w + part + 1] for part in range(2)],
                [down_in[2 * w + part:2 * w + part + 1] for part in range(2)],
                (column[:, :128] != 0).astype(F32),
                jnp.logical_not((lane == 255) & (column == 126)).astype(F32),
                (start != 0).astype(F32),
                (((32 * start + row) & 1023) != 1023).astype(F32),
            )
        )
    return image


def first_kernel(dev_ref, *refs):
    block_refs, other_refs, (sums_ref, count_ref, probe_ref, forward_ref, inverse_ref) = refs[:8], refs[8:10], refs[10:15]
    total_ref, relaxed_ref, own_ref, *edge_refs, half_ref = refs[15:]
    member = dev_ref[0] % 16
    for t in range(8):
        for e in range(2):
            source = member ^ (8 * (t // 4) + t % 4 + 4 * e)
            rows = pl.ds(pl.multiple_of(source // 2 * 32, 32), 32)
            for w in range(2):
                for part in range(2):
                    if e == 0:
                        tile = block_refs[t][0, w, part]
                    elif t in LATE:
                        tile = other_refs[1][LATE.index(t), w, part]
                    else:
                        tile = other_refs[0][EARLY.index(t), w, part]
                    half_ref[w, part, source % 2, rows, :] = tile
    image = [
        [jnp.concatenate([half_ref[w, part, 0], half_ref[w, part, 1]], axis=1).astype(F32) for part in range(2)]
        for w in range(2)
    ]
    far = to_far_field(image, probe_ref, forward_ref, inverse_ref)
    counts = own_counts(count_ref)

    def source(o):
        w, half, row = o // 128, (o // 64) % 2, o % 64
        return ((row // 4) * 2 + half) * 8 + w * 4 + row % 4

    place = picker(source)
    blocks = []
    for block in range(4):
        rows = sums_ref[32 * block:32 * block + 32].astype(F32).reshape(256, 128).astype(BF16)
        blocks.append(dot(place, rows))
    totals = []
    for w in range(2):
        total = jnp.concatenate(
            [
                jnp.concatenate([b[128 * w:128 * w + 64], b[128 * w + 64:128 * w + 128]], axis=1)
                for b in blocks
            ],
            axis=0,
        ) + CENTRE * counts[w]
        total_ref[w] = total
        totals.append(total)
    relaxed = from_far_field(far, totals, counts, image, probe_ref, forward_ref, inverse_ref)
    write_relaxed(dev_ref[0], relaxed, relaxed_ref, own_ref, edge_refs)


def columns_as_rows(columns):
    lane = iota((256, 128), 1)
    gathered = jnp.zeros((256, 128), F32)
    for place, (image, at) in enumerate(columns):
        block = image[:, at // 128 * 128:at // 128 * 128 + 128]
        gathered = jnp.where(lane == place, to_lane(block, at % 128, place), gathered)
    return gathered.T


def second_kernel(
    dev_ref, in_ref, own_in, in0, in1, in2, in3, in4, in5, total_ref, count_ref, probe_ref, forward_ref, inverse_ref,
    out_ref, extra_ref
):
    image = smooth(dev_ref[0], in_ref, own_in, (in0, in1, in2, in3, in4, in5))
    far = to_far_field(image, probe_ref, forward_ref, inverse_ref)
    totals = [total_ref[w] for w in range(2)]
    relaxed = from_far_field(far, totals, own_counts(count_ref), image, probe_ref, forward_ref, inverse_ref)
    planes = [relaxed[w][part] for w in range(2) for part in range(2)]
    rows = columns_as_rows([(plane, at) for at in (127, 255, 128, 0) for plane in planes])
    lines = {}
    place, lane = iota((8, 256), 0), iota((8, 128), 1)
    for names, both in (((127, 255), rows[0:8]), ((128, 0), rows[8:16])):
        skewed = both
        for q in range(1, 4):
            skewed = jnp.where((place & 3) == q, pltpu.roll(both, 32 * q, 1), skewed)
        for i in range(8):
            turned = (pltpu.roll(skewed, 256 - 32 * i, 1) if i else skewed)[:, :128]
            turned = jnp.where((lane >> 5) == (place[:, :128] & 3), turned, 0.0)
            for at, half in zip(names, (turned[0:4], turned[4:8])):
                lines[at, i] = jnp.sum(half, axis=0, keepdims=True)
    extra_ref[...] = jnp.zeros_like(extra_ref)
    for k in range(16):
        i, j = k // 2, k % 2
        across, other = slice(128 * j, 128 * j + 128), slice(128 - 128 * j, 256 - 128 * j)
        for q, plane in enumerate(planes):
            out_ref[k, 32 * q:32 * q + 32, :] = plane[32 * i:32 * i + 32, across].astype(BF16)
            if i > 0:
                extra_ref[k, q:q + 1, :] = plane[32 * i - 1:32 * i, across]
            if i < 7:
                extra_ref[k, 4 + q:5 + q, :] = plane[32 * i + 32:32 * i + 33, across]
            if k in (8, 9):
                extra_ref[k, 8 + q:9 + q, :] = plane[255:256, across]
            if k in (6, 7):
                extra_ref[k, 8 + q:9 + q, :] = plane[0:1, across]
        if j == 1:
            extra_ref[k, 12:13, :] = lines[127, i]
            if i < 7:
                extra_ref[k, 13:14, :] = lines[0, i + 1]
        else:
            if i > 0:
                extra_ref[k, 12:13, :] = lines[255, i - 1]
            extra_ref[k, 13:14, :] = lines[128, i]
        if k == 8:
            extra_ref[k, 14:15, :] = lines[255, 7]
        if k == 7:
            extra_ref[k, 14:15, :] = lines[0, 0]
        out_ref[k, 128:144, :] = extra_ref[k].astype(BF16)


def inner_kernel(dev_ref, in_ref, out_ref):
    dev = dev_ref[0]
    group, member = dev // 16, dev % 16
    i, j = member // 2, member % 2
    order = [member_of(group, place) for place in range(16)]
    extra = [in_ref[m, 128:144, :].astype(F32) for m in order]
    left = jnp.concatenate([e[12:13] for e in extra], axis=0)
    right = jnp.concatenate([e[13:14] for e in extra], axis=0)
    first_half = iota((16, 128), 1) < 64
    turned = pltpu.roll(left, 64, 1)
    left = jnp.where(j == 1, left, jnp.where(first_half, turned, pltpu.roll(turned, 15, 0)))
    turned = pltpu.roll(right, 64, 1)
    right = jnp.where(j == 0, right, jnp.where(first_half, pltpu.roll(turned, 1, 0), turned))
    fill = jnp.zeros((112, 128), F32)
    left = jnp.concatenate([left, fill], axis=0).T
    right = jnp.concatenate([right, fill], axis=0).T
    last_lane = (iota((32, 128), 1) == 127).astype(F32)
    last_row = (iota((32, 128), 0) == 31).astype(F32)
    for u in range(32):
        place, w = u // 2, u % 2
        tile_row = (u + 8 * group + i) % 32
        tile_column = (dev - 2 * tile_row) & 127
        near, q = extra[place], [2 * w, 2 * w + 1]
        image = descend(
            [in_ref[order[place], pl.ds(32 * at, 32), :].astype(F32) for at in q],
            [to_lane(left[32 * at:32 * at + 32], place, 0) for at in q],
            [to_lane(right[32 * at:32 * at + 32], place, 127) for at in q],
            [near[at:at + 1] for at in q],
            [near[4 + at:5 + at] for at in q],
            ((tile_column != 0) & (member != 0)).astype(F32),
            1.0 - last_lane * ((tile_column == 127) | (member == 15)).astype(F32),
            ((tile_row != 0) & (i != 0)).astype(F32),
            1.0 - last_row * ((tile_row == 31) | (i == 7)).astype(F32),
        )
        for part in range(2):
            out_ref[part, tile_row] = image[part]


def border_kernel(dev_ref, in_ref, beyond_ref, inner_ref, out_ref):
    dev = dev_ref[0]
    group, member = dev // 16, dev % 16
    out_ref[...] = inner_ref[...]
    tiles = []
    for u in range(32):
        tile_row = (u + 8 * group + member // 2) % 32
        at = [32 * (2 * (u % 2) + part) for part in range(2)]
        tiles.append((u // 2, u % 2, tile_row, (dev - 2 * tile_row) & 127, member_of(group, u // 2), at))

    def beyond(place):
        return beyond_ref[member_of(group + 1, place)].astype(F32)

    def pull(d, keep):
        weight = STEP * lax.rsqrt(d[0] * d[0] + d[1] * d[1] + EPS) * keep
        return [d[0] * weight, d[1] * weight]

    def rows(at_row, edge_row):
        here = iota((8, 128), 0) == at_row % 8
        start = at_row // 8 * 8
        for place, w, tile_row, _, source, at in tiles:
            block = beyond(place)
            d = []
            for part in range(2):
                own = in_ref[source, pl.ds(at[part] + start // 16 * 16, 16), :].astype(F32)
                row = 2 * w + part
                d.append(own[start % 16:start % 16 + 8] - jnp.broadcast_to(block[row:row + 1], (8, 128)))
            for part, change in enumerate(pull(d, (tile_row != edge_row).astype(F32))):
                slot = out_ref.at[part, tile_row]
                slot[start:start + 8, :] = slot[start:start + 8, :] - jnp.where(here, change, 0.0)

    def columns(at_lane, edge_column):
        here = iota((32, 128), 1) == at_lane
        side = jnp.concatenate([beyond(place)[6:7] for place in range(16)], axis=0)
        half = iota((16, 128), 1) < 64
        turned = pltpu.roll(side, 64, 1)
        if at_lane == 0:
            side = jnp.where(half, turned, pltpu.roll(turned, 15, 0))
        else:
            side = jnp.where(half, pltpu.roll(turned, 1, 0), turned)
        side = jnp.concatenate([side, jnp.zeros((112, 128), F32)], axis=0).T
        for place, w, tile_row, tile_column, source, at in tiles:
            d = []
            for part in range(2):
                own = in_ref[source, pl.ds(at[part], 32), :].astype(F32)
                d.append(own - to_lane(side[at[part]:at[part] + 32], place, at_lane))
            for part, change in enumerate(pull(d, (tile_column != edge_column).astype(F32))):
                out_ref[part, tile_row] = out_ref[part, tile_row] - jnp.where(here, change, 0.0)

    pl.when(member < 2)(lambda: rows(0, 0))
    pl.when(member >= 14)(lambda: rows(31, 31))
    pl.when(member == 0)(lambda: columns(0, 0))
    pl.when(member == 15)(lambda: columns(127, 127))


def shards(object_tiles, amplitudes, probe, frame_pos):
    dev = lax.axis_index(ALL).astype(jnp.int32).reshape(1)
    forward, inverse = dft_blocks()

    lines = tiles_to_windows(dev, object_tiles)
    pieces = lax.all_to_all(amplitude_pieces(frame_pos, amplitudes), ALL, 0, 0, tiled=True)
    sums, counts = window_sums(dev, pieces)
    lines, sums = lax.optimization_barrier((lines, sums))
    tiles = windows_from_lines(lines)
    sums = lax.all_to_all(sums, ALL, 0, 0, tiled=True)
    totals, relaxed, own, *edges = pl.pallas_call(
        first_kernel,
        in_specs=[SCALAR] + [BLOCK] * 15,
        out_specs=[BLOCK] * 9,
        out_shape=[jax.ShapeDtypeStruct((2, SIDE, SIDE), F32), PAIR] + [EDGE] * 7,
        scratch_shapes=[pltpu.VMEM((2, 2, 2, SIDE, 128), BF16)],
        compiler_params=params(),
        name="first_sweep",
    )(dev, *tiles, sums, counts, probe, forward, inverse)
    tiles = pl.pallas_call(
        second_kernel,
        in_specs=[SCALAR] + [BLOCK] * 13,
        out_specs=BLOCK,
        out_shape=jax.ShapeDtypeStruct((16, 144, 128), BF16),
        scratch_shapes=[pltpu.VMEM((16, 16, 128), F32)],
        compiler_params=params(),
        name="second_sweep",
    )(dev, relaxed, own, *exchange_edges(edges), totals, counts, probe, forward, inverse)
    tiles = lax.all_to_all(tiles, ALL, 0, 0, axis_index_groups=GROUPS, tiled=True)
    turns = ((8, 16), (9, 17), (7, -1), (6, -2))
    beyond = lax.ppermute(
        tiles[:, 136:], ALL, [(16 * g + k, (16 * g + to) % 128) for g in range(8) for k, to in turns]
    )
    result = jax.ShapeDtypeStruct((2, 32, 32, 128), F32)
    inner = pl.pallas_call(
        inner_kernel,
        in_specs=[SCALAR, BLOCK],
        out_specs=BLOCK,
        out_shape=result,
        compiler_params=params(),
        name="last_smoothing",
    )(dev, tiles)
    return pl.pallas_call(
        border_kernel,
        in_specs=[SCALAR] + [BLOCK] * 3,
        out_specs=BLOCK,
        out_shape=result,
        compiler_params=params(),
        name="last_borders",
    )(dev, tiles, beyond, inner)


def solution(mesh):
    return jax.shard_map(
        shards,
        mesh=mesh,
        in_specs=(P(None, ALL, None, None), P(ALL, None, None), P(), P(ALL, None)),
        out_specs=P(None, ALL, None, None),
        check_vma=False,
    )
```

```python
import jax
import jax.numpy as jnp
import numpy as np
from jax import lax
from jax.experimental import pallas as pl
from jax.experimental.pallas import tpu as pltpu
from jax.sharding import PartitionSpec as P

FLOOR = 0.3
DELTA = 1.0
STEP = 0.1
EPS = 0.1
CENTRE = 1.75
F32 = jnp.float32
BF16 = jnp.bfloat16
SIDE = 256
ALL = ("frames", "obj")
GROUPS = [list(range(16 * g, 16 * g + 16)) for g in range(8)]
SCALAR = pl.BlockSpec(memory_space=pltpu.SMEM)
BLOCK = pl.BlockSpec(memory_space=pltpu.VMEM)
EARLY, LATE = (0, 6, 5, 7, 2, 3), (4, 1)
ANYWHERE = pl.BlockSpec(memory_space=pl.ANY)
PAIR = jax.ShapeDtypeStruct((2, 2, SIDE, SIDE), F32)
EDGE = jax.ShapeDtypeStruct((8, SIDE), F32)


def place_of(group, member):
    far = (member // 8) ^ (group & 1)
    along = member % 4
    chip = along + far * (7 - 2 * along)
    return 2 * chip + (((member // 4) & 1) ^ (chip & 1))


def member_of(group, place):
    chip = place // 2
    far = chip // 4
    along = chip + far * (7 - 2 * chip)
    return 8 * (far ^ (group & 1)) + 4 * ((place & 1) ^ (chip & 1)) + along


def partners(move):
    pairs = []
    for dev in range(128):
        group, place = move(dev // 16, place_of(dev // 16, dev % 16))
        group, place = group % 8, place % 16
        pairs.append((dev, 16 * group + member_of(group, place)))
    return pairs


def params(limit_mb=40):
    return pltpu.CompilerParams(vmem_limit_bytes=limit_mb << 20)


def dft_blocks():
    index = np.arange(SIDE)
    angle = (index[:, None] * index[None, :] % SIDE) * (2.0 * np.pi / SIDE)
    cosine, sine = np.cos(angle) / 16.0, np.sin(angle) / 16.0
    forward = np.block([[cosine, sine], [-sine, cosine]])
    return jnp.asarray(forward, F32).astype(BF16), jnp.asarray(forward.T, F32).astype(BF16)


def iota(shape, axis):
    return lax.broadcasted_iota(jnp.int32, shape, axis)


def dot(a, b):
    return jnp.dot(a, b, preferred_element_type=F32)


def picker(source_of):
    return (iota((256, 256), 1) == source_of(iota((256, 256), 0))).astype(F32).astype(BF16)


def window_rows(dev):
    group = dev // 16
    place = place_of(group, dev % 16)
    return group, place, [(2 * place + 8 * group + w) % 32 for w in range(2)]


def pieces_kernel(pos_ref, amp_ref, out_ref, amp, out, in_sem, out_sem):
    fetch = [
        pltpu.make_async_copy(amp_ref.at[:, pl.ds(64 * b, 64), :], amp.at[:, pl.ds(64 * b, 64), :], in_sem.at[b])
        for b in range(4)
    ]
    store = [
        pltpu.make_async_copy(out.at[pl.ds(32 * b, 32)], out_ref.at[pl.ds(32 * b, 32)], out_sem.at[b])
        for b in range(4)
    ]
    for copy in fetch:
        copy.start()
    swap = picker(lambda o: (o % 16) * 16 + o // 16)
    row, column = pos_ref[0:1, :], pos_ref[1:2, :]
    group = ((column + 2 * row) & 127) >> 4
    local = (row - 8 * group) & 31
    owner = ((local & 1) * 128 + 16 * group + member_of(group, local >> 1)).astype(F32)
    code = jnp.where(iota((16, 16), 0) == iota((16, 16), 1), owner, 0.0)
    code = jnp.sum(code, axis=1, keepdims=True)
    mine = (iota((16, 128), 1) & 15) == iota((16, 128), 0)
    code = jnp.sum(jnp.where(mine, code, 0.0), axis=0, keepdims=True)
    code = jnp.broadcast_to(code, (8, 128)).astype(BF16)
    for b in range(4):
        fetch[b].wait()
        for block in range(4 * b, 4 * b + 4):
            rows = amp[:, 16 * block:16 * block + 16, :].reshape(256, 256)
            turned = dot(swap, rows).astype(BF16)
            for part in range(8):
                quad, half = part // 2, part % 2
                out[8 * block + part, 0:64, :] = turned[64 * quad:64 * quad + 64, 128 * half:128 * half + 128]
                out[8 * block + part, 64:72, :] = code
        store[b].start()
    for copy in store:
        copy.wait()


def amplitude_pieces(frame_pos, amplitudes):
    return pl.pallas_call(
        pieces_kernel,
        in_specs=[BLOCK, ANYWHERE],
        out_specs=ANYWHERE,
        out_shape=jax.ShapeDtypeStruct((128, 72, 128), BF16),
        scratch_shapes=[
            pltpu.VMEM((16, 256, 256), BF16),
            pltpu.VMEM((128, 72, 128), BF16),
            pltpu.SemaphoreType.DMA((4,)),
            pltpu.SemaphoreType.DMA((4,)),
        ],
        compiler_params=params(60),
        name="amplitude_pieces",
    )(frame_pos.T, amplitudes)


def sums_kernel(dev_ref, in_ref, out_ref, count_ref, pieces, total_ref, number_ref, sem):
    fetch = [
        pltpu.make_async_copy(in_ref.at[pl.ds(32 * b, 32)], pieces.at[pl.ds(32 * b, 32)], sem.at[b])
        for b in range(4)
    ]
    for copy in fetch:
        copy.start()
    lane = iota((8, 128), 1)
    owner = iota((256, 128), 0).astype(F32)
    turn = picker(lambda o: (o % 8) * 32 + o // 8)
    for b in range(4):
        fetch[b].wait()
        members, values = [], []
        for t in range(4 * b, 4 * b + 4):
            code = jnp.zeros((8, 128), F32)
            for s in range(8):
                code = jnp.where((lane >> 4) == s, pieces[8 * t + s, 64:72, :].astype(F32), code)
            members.append((owner == jnp.tile(code, (32, 1))).astype(F32).astype(BF16))
            values.append(
                jnp.concatenate(
                    [pieces[8 * t:8 * t + 8, 16 * c:16 * c + 16, :].reshape(128, 128) for c in range(4)]
                    + [jnp.ones((128, 128), BF16)],
                    axis=1,
                )
            )
        total = dot(jnp.concatenate(members, axis=1), jnp.concatenate(values, axis=0))
        total_ref[...] = total if b == 0 else total_ref[...] + total
    for block in range(4):
        parts = []
        for w in range(2):
            rows = slice(128 * w + 32 * block, 128 * w + 32 * block + 32)
            mean = CENTRE * total_ref[rows, 512:640]
            for c in range(4):
                parts.append(total_ref[rows, 128 * c:128 * c + 128] - mean)
        stacked = jnp.concatenate(parts, axis=0).astype(BF16)
        out_ref[32 * block:32 * block + 32] = dot(turn, stacked).reshape(32, 8, 128).astype(BF16)
    number_ref[...] = total_ref[:, 512:640]
    for w in range(2):
        own = number_ref[pl.ds(dev_ref[0] + 128 * w, 1), :]
        count_ref[8 * w:8 * w + 8, :] = jnp.broadcast_to(own, (8, 128))


def window_sums(dev, arrived):
    return pl.pallas_call(
        sums_kernel,
        in_specs=[SCALAR, ANYWHERE],
        out_specs=[BLOCK] * 2,
        out_shape=[
            jax.ShapeDtypeStruct((128, 8, 128), BF16),
            jax.ShapeDtypeStruct((16, 128), F32),
        ],
        scratch_shapes=[
            pltpu.VMEM((128, 72, 128), BF16),
            pltpu.VMEM((256, 640), F32),
            pltpu.VMEM((256, 128), F32),
            pltpu.SemaphoreType.DMA((4,)),
        ],
        compiler_params=params(60),
        name="window_sums",
    )(dev, arrived)


def outbound_kernel(dev_ref, in_ref, *out_refs):
    dev = dev_ref[0]
    member = dev % 16
    shift = 8 * (dev // 16) + member // 2
    for t in range(8):
        for e in range(2):
            target = member ^ (8 * (t // 4) + t % 4 + 4 * e)
            for w in range(2):
                row = (shift + 2 * place_of(dev // 16, target) + w) % 32
                for part in range(2):
                    out_refs[t][e, w, part] = in_ref[part, row].astype(BF16)


def tiles_to_windows(dev, tiles):
    blocks = pl.pallas_call(
        outbound_kernel,
        in_specs=[SCALAR, BLOCK],
        out_specs=[BLOCK] * 8,
        out_shape=[jax.ShapeDtypeStruct((2, 2, 2, 32, 128), BF16)] * 8,
        compiler_params=params(),
        name="outbound_tiles",
    )(dev, tiles)
    blocks = list(blocks)
    for t in EARLY[1:]:
        blocks[t] = across_chips(blocks[t], t)
    return blocks


def across_chips(block, t):
    return lax.ppermute(block, ALL, [(d, d ^ (8 * (t // 4) + t % 4)) for d in range(128)])


def windows_from_lines(blocks):
    for t in LATE:
        blocks[t] = across_chips(blocks[t], t)
    other = [
        lax.ppermute(jnp.stack([blocks[t][1] for t in part]), ALL, [(d, d ^ 4) for d in range(128)])
        for part in (EARLY, LATE)
    ]
    return blocks + other


def to_far_field(image, probe_ref, forward_ref, inverse_ref):
    waves = []
    for w in range(2):
        real, imag = [image[w][part].astype(BF16).astype(F32) for part in range(2)]
        waves.append(
            [
                (probe_ref[0] * real - probe_ref[1] * imag).astype(BF16),
                (probe_ref[0] * imag + probe_ref[1] * real).astype(BF16),
            ]
        )
    wave = jnp.concatenate(
        [jnp.concatenate([waves[0][part], waves[1][part]], axis=1) for part in range(2)], axis=0
    )
    midway = dot(forward_ref[...], wave).astype(BF16)
    midway = jnp.concatenate(
        [
            jnp.concatenate([midway[:256, 256 * w:256 * w + 256], midway[256:, 256 * w:256 * w + 256]], axis=1)
            for w in range(2)
        ],
        axis=0,
    )
    return dot(midway, inverse_ref[...])


def from_far_field(far, totals, counts, image, probe_ref, forward_ref, inverse_ref):
    changes = []
    for w in range(2):
        real, imag = far[256 * w:256 * w + 256, :256], far[256 * w:256 * w + 256, 256:]
        power = jnp.maximum(real * real + imag * imag, FLOOR * FLOOR)
        scale = totals[w] * lax.rsqrt(power) - counts[w]
        changes.append([(real * scale).astype(BF16), (imag * scale).astype(BF16)])
    change = jnp.concatenate(
        [jnp.concatenate([changes[0][part], changes[1][part]], axis=1) for part in range(2)], axis=0
    )
    halfway = dot(inverse_ref[...], change).astype(BF16)
    halfway = jnp.concatenate(
        [
            jnp.concatenate([halfway[:256, 256 * w:256 * w + 256], halfway[256:, 256 * w:256 * w + 256]], axis=1)
            for w in range(2)
        ],
        axis=0,
    )
    returned = dot(halfway, forward_ref[...])
    intensity = probe_ref[0] * probe_ref[0] + probe_ref[1] * probe_ref[1]
    relaxed = []
    for w in range(2):
        real, imag = returned[256 * w:256 * w + 256, :256], returned[256 * w:256 * w + 256, 256:]
        weight = 1.0 / (counts[w] * intensity + DELTA)
        relaxed.append(
            [
                image[w][0] + (probe_ref[0] * real + probe_ref[1] * imag) * weight,
                image[w][1] + (probe_ref[0] * imag - probe_ref[1] * real) * weight,
            ]
        )
    return relaxed


def own_counts(count_ref):
    return [jnp.tile(count_ref[8 * w:8 * w + 8, :], (32, 1)) for w in range(2)]


def write_relaxed(dev, relaxed, relaxed_ref, own_ref, edge_refs):
    for w in range(2):
        for part in range(2):
            relaxed_ref[w, part] = relaxed[w][part]
    rows = columns_as_rows(
        [(relaxed[w][part], 255 * side) for w, side in ((0, 1), (1, 0), (1, 1), (0, 0)) for part in range(2)]
    )[:8]
    own_ref[...] = rows
    place = iota((8, 256), 0)
    ahead, behind = pltpu.roll(rows, 6, 0), pltpu.roll(rows, 4, 0)
    up, down = rows, pltpu.roll(rows, 6, 0)
    for w in range(2):
        for part in range(2):
            at = 2 * w + part
            up = jnp.where(place == at, pltpu.roll(relaxed[w][part][248:], (at - 7) % 8, 0), up)
            first = relaxed[w][part][:8]
            down = jnp.where(place == at, pltpu.roll(first, at, 0) if at else first, down)
    group, spot, _ = window_rows(dev)
    odd_group, odd_spot = (group & 1) == 1, (spot & 1) == 1
    for ref, odd, even_edge, odd_edge in (
        (edge_refs[0], odd_group, behind, ahead),
        (edge_refs[1], odd_group, ahead, behind),
        (edge_refs[2], odd_group, down, up),
        (edge_refs[3], odd_group, up, down),
        (edge_refs[4], odd_spot, ahead, behind),
        (edge_refs[5], odd_spot, behind, ahead),
    ):
        ref[...] = jnp.where(odd, odd_edge, even_edge)


def exchange_edges(edges):
    moves = []
    for odd in (1, 0):
        moves.append(lambda g, q, odd=odd: (g + 1, q - 1) if g % 2 == odd else (g - 1, q + 1))
    for odd in (1, 0):
        moves.append(lambda g, q, odd=odd: (g + 1 if g % 2 == odd else g - 1, q))
    for odd in (1, 0):
        moves.append(lambda g, q, odd=odd: (g, q + 1 if q % 2 == odd else q - 1))
    return [lax.ppermute(edge, ALL, partners(move)) for edge, move in zip(edges, moves)]


def descend(x, left, right, up, down, keep_left, keep_right, keep_up, keep_down):
    rows, lanes = x[0].shape
    lane, row, row8 = iota((rows, lanes), 1), iota((rows, lanes), 0), iota((8, lanes), 0)

    def wide(narrow):
        return jnp.concatenate([narrow] * (lanes // 128), axis=1)

    across, edge, below, top = [], [], [], []
    for part in range(2):
        next_lane = jnp.where(lane == lanes - 1, wide(right[part]), pltpu.roll(x[part], lanes - 1, 1))
        across.append(next_lane - x[part])
        edge.append(x[part][:, :128] - left[part])
        next_row = jnp.where(
            row == rows - 1, jnp.broadcast_to(down[part], (rows, lanes)), pltpu.roll(x[part], rows - 1, 0)
        )
        below.append(next_row - x[part])
        top.append(x[part][:8] - jnp.broadcast_to(up[part], (8, lanes)))
    across_weight, edge_weight, below_weight, top_weight = [
        lax.rsqrt(d[0] * d[0] + d[1] * d[1] + EPS) * keep
        for d, keep in ((across, keep_right), (edge, keep_left), (below, keep_down), (top, keep_up))
    ]
    result = []
    for part in range(2):
        to_right = across[part] * across_weight
        to_left = jnp.where(lane == 0, wide(edge[part] * edge_weight), pltpu.roll(to_right, 1, 1))
        to_below = below[part] * below_weight
        moved = pltpu.roll(to_below, 1, 0)
        to_above = jnp.concatenate(
            [jnp.where(row8 == 0, top[part] * top_weight, moved[:8]), moved[8:]], axis=0
        )
        result.append(x[part] - STEP * ((to_left - to_right) + (to_above - to_below)))
    return result


def to_lane(block, source, lane):
    shift = (lane - source) % 128
    return pltpu.roll(block, shift, 1) if shift else block


def smooth(dev, relaxed_ref, own_ref, halo_refs):
    group, spot, starts = window_rows(dev)
    odd_group, odd_spot = (group & 1) == 1, (spot & 1) == 1
    corner1, corner0, above1, above0, beside1, beside0 = [ref[...] for ref in halo_refs]
    extra = iota((8, 256), 0) >= 6
    up_own = jnp.where(extra, jnp.where(odd_spot, beside1, beside0), own_ref[...])
    down_own = jnp.where(extra, jnp.where(odd_spot, beside0, beside1), pltpu.roll(own_ref[...], 6, 0))
    up_in = jnp.where(extra, jnp.where(odd_group, corner0, corner1), jnp.where(odd_group, above0, above1))
    down_in = jnp.where(extra, jnp.where(odd_group, corner1, corner0), jnp.where(odd_group, above1, above0))
    lane8 = iota((8, 256), 1)
    left = jnp.where(lane8 < 32, pltpu.roll(up_in, 32, 1), pltpu.roll(up_own, 32, 1))
    right = jnp.where(lane8 >= 224, pltpu.roll(down_in, 224, 1), pltpu.roll(down_own, 224, 1))
    sides = jnp.concatenate([left, right, jnp.zeros((112, 256), F32)], axis=0).T
    lane, row = iota((256, 256), 1), iota((256, 256), 0)
    image = []
    for w in range(2):
        start = starts[w]
        wrapped = (row // 32 + start) >= 32
        column = (16 * group - 2 * start + jnp.where(wrapped, 64, 0)) & 127
        image.append(
            descend(
                [relaxed_ref[w, part] for part in range(2)],
                [to_lane(sides, 4 + 2 * w + part, 0) for part in range(2)],
                [to_lane(sides, 8 + 4 + 2 * (1 - w) + part, 127) for part in range(2)],
                [up_in[2 * w + part:2 * w + part + 1] for part in range(2)],
                [down_in[2 * w + part:2 * w + part + 1] for part in range(2)],
                (column[:, :128] != 0).astype(F32),
                jnp.logical_not((lane == 255) & (column == 126)).astype(F32),
                (start != 0).astype(F32),
                (((32 * start + row) & 1023) != 1023).astype(F32),
            )
        )
    return image


def first_kernel(dev_ref, *refs):
    block_refs, other_refs, (sums_ref, count_ref, probe_ref, forward_ref, inverse_ref) = refs[:8], refs[8:10], refs[10:15]
    total_ref, relaxed_ref, own_ref, *edge_refs, half_ref = refs[15:]
    member = dev_ref[0] % 16
    for t in range(8):
        for e in range(2):
            source = member ^ (8 * (t // 4) + t % 4 + 4 * e)
            rows = pl.ds(pl.multiple_of(source // 2 * 32, 32), 32)
            for w in range(2):
                for part in range(2):
                    if e == 0:
                        tile = block_refs[t][0, w, part]
                    elif t in LATE:
                        tile = other_refs[1][LATE.index(t), w, part]
                    else:
                        tile = other_refs[0][EARLY.index(t), w, part]
                    half_ref[w, part, source % 2, rows, :] = tile
    image = [
        [jnp.concatenate([half_ref[w, part, 0], half_ref[w, part, 1]], axis=1).astype(F32) for part in range(2)]
        for w in range(2)
    ]
    far = to_far_field(image, probe_ref, forward_ref, inverse_ref)
    counts = own_counts(count_ref)

    def source(o):
        w, half, row = o // 128, (o // 64) % 2, o % 64
        return ((row // 4) * 2 + half) * 8 + w * 4 + row % 4

    place = picker(source)
    blocks = []
    for block in range(4):
        rows = sums_ref[32 * block:32 * block + 32].astype(F32).reshape(256, 128).astype(BF16)
        blocks.append(dot(place, rows))
    totals = []
    for w in range(2):
        total = jnp.concatenate(
            [
                jnp.concatenate([b[128 * w:128 * w + 64], b[128 * w + 64:128 * w + 128]], axis=1)
                for b in blocks
            ],
            axis=0,
        ) + CENTRE * counts[w]
        total_ref[w] = total
        totals.append(total)
    relaxed = from_far_field(far, totals, counts, image, probe_ref, forward_ref, inverse_ref)
    write_relaxed(dev_ref[0], relaxed, relaxed_ref, own_ref, edge_refs)


def columns_as_rows(columns):
    lane = iota((256, 128), 1)
    gathered = jnp.zeros((256, 128), F32)
    for place, (image, at) in enumerate(columns):
        block = image[:, at // 128 * 128:at // 128 * 128 + 128]
        gathered = jnp.where(lane == place, to_lane(block, at % 128, place), gathered)
    return gathered.T


def second_kernel(
    dev_ref, in_ref, own_in, in0, in1, in2, in3, in4, in5, total_ref, count_ref, probe_ref, forward_ref, inverse_ref,
    out_ref, extra_ref
):
    image = smooth(dev_ref[0], in_ref, own_in, (in0, in1, in2, in3, in4, in5))
    far = to_far_field(image, probe_ref, forward_ref, inverse_ref)
    totals = [total_ref[w] for w in range(2)]
    relaxed = from_far_field(far, totals, own_counts(count_ref), image, probe_ref, forward_ref, inverse_ref)
    planes = [relaxed[w][part] for w in range(2) for part in range(2)]
    rows = columns_as_rows([(plane, at) for at in (127, 255, 128, 0) for plane in planes])
    lines = {}
    place, lane = iota((8, 256), 0), iota((8, 128), 1)
    for names, both in (((127, 255), rows[0:8]), ((128, 0), rows[8:16])):
        skewed = both
        for q in range(1, 4):
            skewed = jnp.where((place & 3) == q, pltpu.roll(both, 32 * q, 1), skewed)
        for i in range(8):
            turned = (pltpu.roll(skewed, 256 - 32 * i, 1) if i else skewed)[:, :128]
            turned = jnp.where((lane >> 5) == (place[:, :128] & 3), turned, 0.0)
            for at, half in zip(names, (turned[0:4], turned[4:8])):
                lines[at, i] = jnp.sum(half, axis=0, keepdims=True)
    extra_ref[...] = jnp.zeros_like(extra_ref)
    for k in range(16):
        i, j = k // 2, k % 2
        across, other = slice(128 * j, 128 * j + 128), slice(128 - 128 * j, 256 - 128 * j)
        for q, plane in enumerate(planes):
            out_ref[k, 32 * q:32 * q + 32, :] = plane[32 * i:32 * i + 32, across].astype(BF16)
            if i > 0:
                extra_ref[k, q:q + 1, :] = plane[32 * i - 1:32 * i, across]
            if i < 7:
                extra_ref[k, 4 + q:5 + q, :] = plane[32 * i + 32:32 * i + 33, across]
            if k in (8, 9):
                extra_ref[k, 8 + q:9 + q, :] = plane[255:256, across]
            if k in (6, 7):
                extra_ref[k, 8 + q:9 + q, :] = plane[0:1, across]
        if j == 1:
            extra_ref[k, 12:13, :] = lines[127, i]
            if i < 7:
                extra_ref[k, 13:14, :] = lines[0, i + 1]
        else:
            if i > 0:
                extra_ref[k, 12:13, :] = lines[255, i - 1]
            extra_ref[k, 13:14, :] = lines[128, i]
        if k == 8:
            extra_ref[k, 14:15, :] = lines[255, 7]
        if k == 7:
            extra_ref[k, 14:15, :] = lines[0, 0]
        out_ref[k, 128:144, :] = extra_ref[k].astype(BF16)


def inner_kernel(dev_ref, in_ref, out_ref):
    dev = dev_ref[0]
    group, member = dev // 16, dev % 16
    i, j = member // 2, member % 2
    order = [member_of(group, place) for place in range(16)]
    extra = [in_ref[m, 128:144, :].astype(F32) for m in order]
    left = jnp.concatenate([e[12:13] for e in extra], axis=0)
    right = jnp.concatenate([e[13:14] for e in extra], axis=0)
    first_half = iota((16, 128), 1) < 64
    turned = pltpu.roll(left, 64, 1)
    left = jnp.where(j == 1, left, jnp.where(first_half, turned, pltpu.roll(turned, 15, 0)))
    turned = pltpu.roll(right, 64, 1)
    right = jnp.where(j == 0, right, jnp.where(first_half, pltpu.roll(turned, 1, 0), turned))
    fill = jnp.zeros((112, 128), F32)
    left = jnp.concatenate([left, fill], axis=0).T
    right = jnp.concatenate([right, fill], axis=0).T
    last_lane = (iota((32, 128), 1) == 127).astype(F32)
    last_row = (iota((32, 128), 0) == 31).astype(F32)
    for u in range(32):
        place, w = u // 2, u % 2
        tile_row = (u + 8 * group + i) % 32
        tile_column = (dev - 2 * tile_row) & 127
        near, q = extra[place], [2 * w, 2 * w + 1]
        image = descend(
            [in_ref[order[place], pl.ds(32 * at, 32), :].astype(F32) for at in q],
            [to_lane(left[32 * at:32 * at + 32], place, 0) for at in q],
            [to_lane(right[32 * at:32 * at + 32], place, 127) for at in q],
            [near[at:at + 1] for at in q],
            [near[4 + at:5 + at] for at in q],
            ((tile_column != 0) & (member != 0)).astype(F32),
            1.0 - last_lane * ((tile_column == 127) | (member == 15)).astype(F32),
            ((tile_row != 0) & (i != 0)).astype(F32),
            1.0 - last_row * ((tile_row == 31) | (i == 7)).astype(F32),
        )
        for part in range(2):
            out_ref[part, tile_row] = image[part]


def border_kernel(dev_ref, in_ref, beyond_ref, inner_ref, out_ref):
    dev = dev_ref[0]
    group, member = dev // 16, dev % 16
    out_ref[...] = inner_ref[...]
    tiles = []
    for u in range(32):
        tile_row = (u + 8 * group + member // 2) % 32
        at = [32 * (2 * (u % 2) + part) for part in range(2)]
        tiles.append((u // 2, u % 2, tile_row, (dev - 2 * tile_row) & 127, member_of(group, u // 2), at))

    def beyond(place):
        return beyond_ref[member_of(group + 1, place)].astype(F32)

    def pull(d, keep):
        weight = STEP * lax.rsqrt(d[0] * d[0] + d[1] * d[1] + EPS) * keep
        return [d[0] * weight, d[1] * weight]

    def rows(at_row, edge_row):
        here = iota((8, 128), 0) == at_row % 8
        start = at_row // 8 * 8
        for place, w, tile_row, _, source, at in tiles:
            block = beyond(place)
            d = []
            for part in range(2):
                own = in_ref[source, pl.ds(at[part] + start // 16 * 16, 16), :].astype(F32)
                row = 2 * w + part
                d.append(own[start % 16:start % 16 + 8] - jnp.broadcast_to(block[row:row + 1], (8, 128)))
            for part, change in enumerate(pull(d, (tile_row != edge_row).astype(F32))):
                slot = out_ref.at[part, tile_row]
                slot[start:start + 8, :] = slot[start:start + 8, :] - jnp.where(here, change, 0.0)

    def columns(at_lane, edge_column):
        here = iota((32, 128), 1) == at_lane
        side = jnp.concatenate([beyond(place)[6:7] for place in range(16)], axis=0)
        half = iota((16, 128), 1) < 64
        turned = pltpu.roll(side, 64, 1)
        if at_lane == 0:
            side = jnp.where(half, turned, pltpu.roll(turned, 15, 0))
        else:
            side = jnp.where(half, pltpu.roll(turned, 1, 0), turned)
        side = jnp.concatenate([side, jnp.zeros((112, 128), F32)], axis=0).T
        for place, w, tile_row, tile_column, source, at in tiles:
            d = []
            for part in range(2):
                own = in_ref[source, pl.ds(at[part], 32), :].astype(F32)
                d.append(own - to_lane(side[at[part]:at[part] + 32], place, at_lane))
            for part, change in enumerate(pull(d, (tile_column != edge_column).astype(F32))):
                out_ref[part, tile_row] = out_ref[part, tile_row] - jnp.where(here, change, 0.0)

    pl.when(member < 2)(lambda: rows(0, 0))
    pl.when(member >= 14)(lambda: rows(31, 31))
    pl.when(member == 0)(lambda: columns(0, 0))
    pl.when(member == 15)(lambda: columns(127, 127))


def shards(object_tiles, amplitudes, probe, frame_pos):
    dev = lax.axis_index(ALL).astype(jnp.int32).reshape(1)
    forward, inverse = dft_blocks()

    lines = tiles_to_windows(dev, object_tiles)
    pieces = lax.all_to_all(amplitude_pieces(frame_pos, amplitudes), ALL, 0, 0, tiled=True)
    sums, counts = window_sums(dev, pieces)
    counts = jnp.concatenate([counts, counts], axis=1)
    lines, sums = lax.optimization_barrier((lines, sums))
    tiles = windows_from_lines(lines)
    sums = lax.all_to_all(sums, ALL, 0, 0, tiled=True)
    totals, relaxed, own, *edges = pl.pallas_call(
        first_kernel,
        in_specs=[SCALAR] + [BLOCK] * 15,
        out_specs=[BLOCK] * 9,
        out_shape=[jax.ShapeDtypeStruct((2, SIDE, SIDE), F32), PAIR] + [EDGE] * 7,
        scratch_shapes=[pltpu.VMEM((2, 2, 2, SIDE, 128), BF16)],
        compiler_params=params(),
        name="first_sweep",
    )(dev, *tiles, sums, counts, probe, forward, inverse)
    tiles = pl.pallas_call(
        second_kernel,
        in_specs=[SCALAR] + [BLOCK] * 13,
        out_specs=BLOCK,
        out_shape=jax.ShapeDtypeStruct((16, 144, 128), BF16),
        scratch_shapes=[pltpu.VMEM((16, 16, 128), F32)],
        compiler_params=params(),
        name="second_sweep",
    )(dev, relaxed, own, *exchange_edges(edges), totals, counts, probe, forward, inverse)
    tiles = lax.all_to_all(tiles, ALL, 0, 0, axis_index_groups=GROUPS, tiled=True)
    turns = ((8, 16), (9, 17), (7, -1), (6, -2))
    beyond = lax.ppermute(
        tiles[:, 136:], ALL, [(16 * g + k, (16 * g + to) % 128) for g in range(8) for k, to in turns]
    )
    result = jax.ShapeDtypeStruct((2, 32, 32, 128), F32)
    inner = pl.pallas_call(
        inner_kernel,
        in_specs=[SCALAR, BLOCK],
        out_specs=BLOCK,
        out_shape=result,
        compiler_params=params(),
        name="last_smoothing",
    )(dev, tiles)
    return pl.pallas_call(
        border_kernel,
        in_specs=[SCALAR] + [BLOCK] * 3,
        out_specs=BLOCK,
        out_shape=result,
        compiler_params=params(),
        name="last_borders",
    )(dev, tiles, beyond, inner)


def solution(mesh):
    return jax.shard_map(
        shards,
        mesh=mesh,
        in_specs=(P(None, ALL, None, None), P(ALL, None, None), P(), P(ALL, None)),
        out_specs=P(None, ALL, None, None),
        check_vma=False,
    )
```

```python
import jax
import jax.numpy as jnp
import numpy as np
from jax import lax
from jax.experimental import pallas as pl
from jax.experimental.pallas import tpu as pltpu
from jax.sharding import PartitionSpec as P

FLOOR = 0.3
DELTA = 1.0
STEP = 0.1
EPS = 0.1
CENTRE = 1.75
F32 = jnp.float32
BF16 = jnp.bfloat16
SIDE = 256
ALL = ("frames", "obj")
GROUPS = [list(range(16 * g, 16 * g + 16)) for g in range(8)]
SCALAR = pl.BlockSpec(memory_space=pltpu.SMEM)
BLOCK = pl.BlockSpec(memory_space=pltpu.VMEM)
EARLY, LATE = (0, 6, 5, 7, 2, 3), (4, 1)
ANYWHERE = pl.BlockSpec(memory_space=pl.ANY)
PAIR = jax.ShapeDtypeStruct((2, 2, SIDE, SIDE), F32)
EDGE = jax.ShapeDtypeStruct((8, SIDE), F32)


def place_of(group, member):
    far = (member // 8) ^ (group & 1)
    along = member % 4
    chip = along + far * (7 - 2 * along)
    return 2 * chip + (((member // 4) & 1) ^ (chip & 1))


def member_of(group, place):
    chip = place // 2
    far = chip // 4
    along = chip + far * (7 - 2 * chip)
    return 8 * (far ^ (group & 1)) + 4 * ((place & 1) ^ (chip & 1)) + along


def partners(move):
    pairs = []
    for dev in range(128):
        group, place = move(dev // 16, place_of(dev // 16, dev % 16))
        group, place = group % 8, place % 16
        pairs.append((dev, 16 * group + member_of(group, place)))
    return pairs


def params(limit_mb=40):
    return pltpu.CompilerParams(vmem_limit_bytes=limit_mb << 20)


def dft_blocks():
    index = np.arange(SIDE)
    angle = (index[:, None] * index[None, :] % SIDE) * (2.0 * np.pi / SIDE)
    cosine, sine = np.cos(angle) / 16.0, np.sin(angle) / 16.0
    forward = np.block([[cosine, sine], [-sine, cosine]])
    return jnp.asarray(forward, F32).astype(BF16), jnp.asarray(forward.T, F32).astype(BF16)


def iota(shape, axis):
    return lax.broadcasted_iota(jnp.int32, shape, axis)


def dot(a, b):
    return jnp.dot(a, b, preferred_element_type=F32)


def picker(source_of):
    return (iota((256, 256), 1) == source_of(iota((256, 256), 0))).astype(F32).astype(BF16)


def window_rows(dev):
    group = dev // 16
    place = place_of(group, dev % 16)
    return group, place, [(2 * place + 8 * group + w) % 32 for w in range(2)]


def pieces_kernel(pos_ref, amp_ref, out_ref, amp, out, in_sem, out_sem):
    fetch = [
        pltpu.make_async_copy(amp_ref.at[:, pl.ds(64 * b, 64), :], amp.at[:, pl.ds(64 * b, 64), :], in_sem.at[b])
        for b in range(4)
    ]
    store = [
        pltpu.make_async_copy(out.at[pl.ds(32 * b, 32)], out_ref.at[pl.ds(32 * b, 32)], out_sem.at[b])
        for b in range(4)
    ]
    for copy in fetch:
        copy.start()
    swap = picker(lambda o: (o % 16) * 16 + o // 16)
    row, column = pos_ref[0:1, :], pos_ref[1:2, :]
    group = ((column + 2 * row) & 127) >> 4
    local = (row - 8 * group) & 31
    owner = ((local & 1) * 128 + 16 * group + member_of(group, local >> 1)).astype(F32)
    code = jnp.where(iota((16, 16), 0) == iota((16, 16), 1), owner, 0.0)
    code = jnp.sum(code, axis=1, keepdims=True)
    mine = (iota((16, 128), 1) & 15) == iota((16, 128), 0)
    code = jnp.sum(jnp.where(mine, code, 0.0), axis=0, keepdims=True)
    code = jnp.broadcast_to(code, (8, 128)).astype(BF16)
    for b in range(4):
        fetch[b].wait()
        for block in range(4 * b, 4 * b + 4):
            rows = amp[:, 16 * block:16 * block + 16, :].reshape(256, 256)
            turned = dot(swap, rows).astype(BF16)
            for part in range(8):
                quad, half = part // 2, part % 2
                out[8 * block + part, 0:64, :] = turned[64 * quad:64 * quad + 64, 128 * half:128 * half + 128]
                out[8 * block + part, 64:72, :] = code
        store[b].start()
    for copy in store:
        copy.wait()


def amplitude_pieces(frame_pos, amplitudes):
    return pl.pallas_call(
        pieces_kernel,
        in_specs=[BLOCK, ANYWHERE],
        out_specs=ANYWHERE,
        out_shape=jax.ShapeDtypeStruct((128, 72, 128), BF16),
        scratch_shapes=[
            pltpu.VMEM((16, 256, 256), BF16),
            pltpu.VMEM((128, 72, 128), BF16),
            pltpu.SemaphoreType.DMA((4,)),
            pltpu.SemaphoreType.DMA((4,)),
        ],
        compiler_params=params(60),
        name="amplitude_pieces",
    )(frame_pos.T, amplitudes)


def sums_kernel(dev_ref, in_ref, out_ref, count_ref, pieces, total_ref, number_ref, sem):
    fetch = [
        pltpu.make_async_copy(in_ref.at[pl.ds(32 * b, 32)], pieces.at[pl.ds(32 * b, 32)], sem.at[b])
        for b in range(4)
    ]
    for copy in fetch:
        copy.start()
    lane = iota((8, 128), 1)
    owner = iota((256, 128), 0).astype(F32)
    turn = picker(lambda o: (o % 8) * 32 + o // 8)
    for b in range(4):
        fetch[b].wait()
        members, values = [], []
        for t in range(4 * b, 4 * b + 4):
            code = jnp.zeros((8, 128), F32)
            for s in range(8):
                code = jnp.where((lane >> 4) == s, pieces[8 * t + s, 64:72, :].astype(F32), code)
            members.append((owner == jnp.tile(code, (32, 1))).astype(F32).astype(BF16))
            values.append(
                jnp.concatenate(
                    [pieces[8 * t:8 * t + 8, 16 * c:16 * c + 16, :].reshape(128, 128) for c in range(4)]
                    + [jnp.ones((128, 128), BF16)],
                    axis=1,
                )
            )
        total = dot(jnp.concatenate(members, axis=1), jnp.concatenate(values, axis=0))
        total_ref[...] = total if b == 0 else total_ref[...] + total
    for block in range(4):
        parts = []
        for w in range(2):
            rows = slice(128 * w + 32 * block, 128 * w + 32 * block + 32)
            mean = CENTRE * total_ref[rows, 512:640]
            for c in range(4):
                parts.append(total_ref[rows, 128 * c:128 * c + 128] - mean)
        stacked = jnp.concatenate(parts, axis=0).astype(BF16)
        out_ref[32 * block:32 * block + 32] = dot(turn, stacked).reshape(32, 8, 128).astype(BF16)
    number_ref[...] = total_ref[:, 512:640]
    for w in range(2):
        own = number_ref[pl.ds(dev_ref[0] + 128 * w, 1), :]
        count_ref[8 * w:8 * w + 8, :] = jnp.broadcast_to(own, (8, 128))


def window_sums(dev, arrived):
    return pl.pallas_call(
        sums_kernel,
        in_specs=[SCALAR, ANYWHERE],
        out_specs=[BLOCK] * 2,
        out_shape=[
            jax.ShapeDtypeStruct((128, 8, 128), BF16),
            jax.ShapeDtypeStruct((16, 128), F32),
        ],
        scratch_shapes=[
            pltpu.VMEM((128, 72, 128), BF16),
            pltpu.VMEM((256, 640), F32),
            pltpu.VMEM((256, 128), F32),
            pltpu.SemaphoreType.DMA((4,)),
        ],
        compiler_params=params(60),
        name="window_sums",
    )(dev, arrived)


def outbound_kernel(dev_ref, in_ref, *out_refs):
    dev = dev_ref[0]
    member = dev % 16
    shift = 8 * (dev // 16) + member // 2
    for t in range(8):
        for e in range(2):
            target = member ^ (8 * (t // 4) + t % 4 + 4 * e)
            for w in range(2):
                row = (shift + 2 * place_of(dev // 16, target) + w) % 32
                for part in range(2):
                    out_refs[t][e, w, part] = in_ref[part, row].astype(BF16)


def tiles_to_windows(dev, tiles):
    blocks = pl.pallas_call(
        outbound_kernel,
        in_specs=[SCALAR, BLOCK],
        out_specs=[BLOCK] * 8,
        out_shape=[jax.ShapeDtypeStruct((2, 2, 2, 32, 128), BF16)] * 8,
        compiler_params=params(),
        name="outbound_tiles",
    )(dev, tiles)
    blocks = list(blocks)
    for t in EARLY[1:]:
        blocks[t] = across_chips(blocks[t], t)
    return blocks


def across_chips(block, t):
    return lax.ppermute(block, ALL, [(d, d ^ (8 * (t // 4) + t % 4)) for d in range(128)])


def windows_from_lines(blocks):
    for t in LATE:
        blocks[t] = across_chips(blocks[t], t)
    other = [
        lax.ppermute(jnp.stack([blocks[t][1] for t in part]), ALL, [(d, d ^ 4) for d in range(128)])
        for part in (EARLY, LATE)
    ]
    return blocks + other


def to_far_field(image, probe_ref, forward_ref, inverse_ref):
    waves = []
    for w in range(2):
        real, imag = [image[w][part].astype(BF16).astype(F32) for part in range(2)]
        waves.append(
            [
                (probe_ref[0] * real - probe_ref[1] * imag).astype(BF16),
                (probe_ref[0] * imag + probe_ref[1] * real).astype(BF16),
            ]
        )
    wave = jnp.concatenate(
        [jnp.concatenate([waves[0][part], waves[1][part]], axis=1) for part in range(2)], axis=0
    )
    midway = dot(forward_ref[...], wave).astype(BF16)
    midway = jnp.concatenate(
        [
            jnp.concatenate([midway[:256, 256 * w:256 * w + 256], midway[256:, 256 * w:256 * w + 256]], axis=1)
            for w in range(2)
        ],
        axis=0,
    )
    return dot(midway, inverse_ref[...])


def from_far_field(far, totals, counts, image, probe_ref, forward_ref, inverse_ref):
    changes = []
    for w in range(2):
        real, imag = far[256 * w:256 * w + 256, :256], far[256 * w:256 * w + 256, 256:]
        power = jnp.maximum(real * real + imag * imag, FLOOR * FLOOR)
        scale = totals[w] * lax.rsqrt(power) - counts[w]
        changes.append([(real * scale).astype(BF16), (imag * scale).astype(BF16)])
    change = jnp.concatenate(
        [jnp.concatenate([changes[0][part], changes[1][part]], axis=1) for part in range(2)], axis=0
    )
    halfway = dot(inverse_ref[...], change).astype(BF16)
    halfway = jnp.concatenate(
        [
            jnp.concatenate([halfway[:256, 256 * w:256 * w + 256], halfway[256:, 256 * w:256 * w + 256]], axis=1)
            for w in range(2)
        ],
        axis=0,
    )
    returned = dot(halfway, forward_ref[...])
    intensity = probe_ref[0] * probe_ref[0] + probe_ref[1] * probe_ref[1]
    relaxed = []
    for w in range(2):
        real, imag = returned[256 * w:256 * w + 256, :256], returned[256 * w:256 * w + 256, 256:]
        weight = 1.0 / (counts[w] * intensity + DELTA)
        relaxed.append(
            [
                image[w][0] + (probe_ref[0] * real + probe_ref[1] * imag) * weight,
                image[w][1] + (probe_ref[0] * imag - probe_ref[1] * real) * weight,
            ]
        )
    return relaxed


def own_counts(count_ref):
    return [jnp.tile(count_ref[8 * w:8 * w + 8, :], (32, 1)) for w in range(2)]


def write_relaxed(dev, relaxed, relaxed_ref, own_ref, edge_refs):
    for w in range(2):
        for part in range(2):
            relaxed_ref[w, part] = relaxed[w][part]
    rows = columns_as_rows(
        [(relaxed[w][part], 255 * side) for w, side in ((0, 1), (1, 0), (1, 1), (0, 0)) for part in range(2)]
    )[:8]
    own_ref[...] = rows
    place = iota((8, 256), 0)
    ahead, behind = pltpu.roll(rows, 6, 0), pltpu.roll(rows, 4, 0)
    up, down = rows, pltpu.roll(rows, 6, 0)
    for w in range(2):
        for part in range(2):
            at = 2 * w + part
            up = jnp.where(place == at, pltpu.roll(relaxed[w][part][248:], (at - 7) % 8, 0), up)
            first = relaxed[w][part][:8]
            down = jnp.where(place == at, pltpu.roll(first, at, 0) if at else first, down)
    group, spot, _ = window_rows(dev)
    odd_group, odd_spot = (group & 1) == 1, (spot & 1) == 1
    for ref, odd, even_edge, odd_edge in (
        (edge_refs[0], odd_group, down, up),
        (edge_refs[1], odd_group, behind, ahead),
        (edge_refs[2], odd_spot, ahead, behind),
        (edge_refs[3], odd_group, up, down),
        (edge_refs[4], odd_group, ahead, behind),
        (edge_refs[5], odd_spot, behind, ahead),
    ):
        ref[...] = jnp.where(odd, odd_edge, even_edge)


def exchange_edges(edges):
    moves = []
    for odd in (1, 0):
        moves.append(lambda g, q, odd=odd: (g + 1 if g % 2 == odd else g - 1, q))
        moves.append(lambda g, q, odd=odd: (g + 1, q - 1) if g % 2 == odd else (g - 1, q + 1))
        moves.append(lambda g, q, odd=odd: (g, q + 1 if q % 2 == odd else q - 1))
    return [lax.ppermute(edge, ALL, partners(move)) for edge, move in zip(edges, moves)]


def descend(x, left, right, up, down, keep_left, keep_right, keep_up, keep_down):
    rows, lanes = x[0].shape
    lane, row, row8 = iota((rows, lanes), 1), iota((rows, lanes), 0), iota((8, lanes), 0)

    def wide(narrow):
        return jnp.concatenate([narrow] * (lanes // 128), axis=1)

    across, edge, below, top = [], [], [], []
    for part in range(2):
        next_lane = jnp.where(lane == lanes - 1, wide(right[part]), pltpu.roll(x[part], lanes - 1, 1))
        across.append(next_lane - x[part])
        edge.append(x[part][:, :128] - left[part])
        next_row = jnp.where(
            row == rows - 1, jnp.broadcast_to(down[part], (rows, lanes)), pltpu.roll(x[part], rows - 1, 0)
        )
        below.append(next_row - x[part])
        top.append(x[part][:8] - jnp.broadcast_to(up[part], (8, lanes)))
    across_weight, edge_weight, below_weight, top_weight = [
        lax.rsqrt(d[0] * d[0] + d[1] * d[1] + EPS) * keep
        for d, keep in ((across, keep_right), (edge, keep_left), (below, keep_down), (top, keep_up))
    ]
    result = []
    for part in range(2):
        to_right = across[part] * across_weight
        to_left = jnp.where(lane == 0, wide(edge[part] * edge_weight), pltpu.roll(to_right, 1, 1))
        to_below = below[part] * below_weight
        moved = pltpu.roll(to_below, 1, 0)
        to_above = jnp.concatenate(
            [jnp.where(row8 == 0, top[part] * top_weight, moved[:8]), moved[8:]], axis=0
        )
        result.append(x[part] - STEP * ((to_left - to_right) + (to_above - to_below)))
    return result


def to_lane(block, source, lane):
    shift = (lane - source) % 128
    return pltpu.roll(block, shift, 1) if shift else block


def smooth(dev, relaxed_ref, own_ref, halo_refs):
    group, spot, starts = window_rows(dev)
    odd_group, odd_spot = (group & 1) == 1, (spot & 1) == 1
    above1, corner1, beside1, above0, corner0, beside0 = [ref[...] for ref in halo_refs]
    extra = iota((8, 256), 0) >= 6
    up_own = jnp.where(extra, jnp.where(odd_spot, beside1, beside0), own_ref[...])
    down_own = jnp.where(extra, jnp.where(odd_spot, beside0, beside1), pltpu.roll(own_ref[...], 6, 0))
    up_in = jnp.where(extra, jnp.where(odd_group, corner0, corner1), jnp.where(odd_group, above0, above1))
    down_in = jnp.where(extra, jnp.where(odd_group, corner1, corner0), jnp.where(odd_group, above1, above0))
    lane8 = iota((8, 256), 1)
    left = jnp.where(lane8 < 32, pltpu.roll(up_in, 32, 1), pltpu.roll(up_own, 32, 1))
    right = jnp.where(lane8 >= 224, pltpu.roll(down_in, 224, 1), pltpu.roll(down_own, 224, 1))
    sides = jnp.concatenate([left, right, jnp.zeros((112, 256), F32)], axis=0).T
    lane, row = iota((256, 256), 1), iota((256, 256), 0)
    image = []
    for w in range(2):
        start = starts[w]
        wrapped = (row // 32 + start) >= 32
        column = (16 * group - 2 * start + jnp.where(wrapped, 64, 0)) & 127
        image.append(
            descend(
                [relaxed_ref[w, part] for part in range(2)],
                [to_lane(sides, 4 + 2 * w + part, 0) for part in range(2)],
                [to_lane(sides, 8 + 4 + 2 * (1 - w) + part, 127) for part in range(2)],
                [up_in[2 * w + part:2 * w + part + 1] for part in range(2)],
                [down_in[2 * w + part:2 * w + part + 1] for part in range(2)],
                (column[:, :128] != 0).astype(F32),
                jnp.logical_not((lane == 255) & (column == 126)).astype(F32),
                (start != 0).astype(F32),
                (((32 * start + row) & 1023) != 1023).astype(F32),
            )
        )
    return image


def first_kernel(dev_ref, *refs):
    block_refs, other_refs, (sums_ref, count_ref, probe_ref, forward_ref, inverse_ref) = refs[:8], refs[8:10], refs[10:15]
    total_ref, relaxed_ref, own_ref, *edge_refs, half_ref = refs[15:]
    member = dev_ref[0] % 16
    for t in range(8):
        for e in range(2):
            source = member ^ (8 * (t // 4) + t % 4 + 4 * e)
            rows = pl.ds(pl.multiple_of(source // 2 * 32, 32), 32)
            for w in range(2):
                for part in range(2):
                    if e == 0:
                        tile = block_refs[t][0, w, part]
                    elif t in LATE:
                        tile = other_refs[1][LATE.index(t), w, part]
                    else:
                        tile = other_refs[0][EARLY.index(t), w, part]
                    half_ref[w, part, source % 2, rows, :] = tile
    image = [
        [jnp.concatenate([half_ref[w, part, 0], half_ref[w, part, 1]], axis=1).astype(F32) for part in range(2)]
        for w in range(2)
    ]
    far = to_far_field(image, probe_ref, forward_ref, inverse_ref)
    counts = own_counts(count_ref)

    def source(o):
        w, half, row = o // 128, (o // 64) % 2, o % 64
        return ((row // 4) * 2 + half) * 8 + w * 4 + row % 4

    place = picker(source)
    blocks = []
    for block in range(4):
        rows = sums_ref[32 * block:32 * block + 32].astype(F32).reshape(256, 128).astype(BF16)
        blocks.append(dot(place, rows))
    totals = []
    for w in range(2):
        total = jnp.concatenate(
            [
                jnp.concatenate([b[128 * w:128 * w + 64], b[128 * w + 64:128 * w + 128]], axis=1)
                for b in blocks
            ],
            axis=0,
        ) + CENTRE * counts[w]
        total_ref[w] = total
        totals.append(total)
    relaxed = from_far_field(far, totals, counts, image, probe_ref, forward_ref, inverse_ref)
    write_relaxed(dev_ref[0], relaxed, relaxed_ref, own_ref, edge_refs)


def columns_as_rows(columns):
    lane = iota((256, 128), 1)
    gathered = jnp.zeros((256, 128), F32)
    for place, (image, at) in enumerate(columns):
        block = image[:, at // 128 * 128:at // 128 * 128 + 128]
        gathered = jnp.where(lane == place, to_lane(block, at % 128, place), gathered)
    return gathered.T


def second_kernel(
    dev_ref, in_ref, own_in, in0, in1, in2, in3, in4, in5, total_ref, count_ref, probe_ref, forward_ref, inverse_ref,
    out_ref, extra_ref
):
    image = smooth(dev_ref[0], in_ref, own_in, (in0, in1, in2, in3, in4, in5))
    far = to_far_field(image, probe_ref, forward_ref, inverse_ref)
    totals = [total_ref[w] for w in range(2)]
    relaxed = from_far_field(far, totals, own_counts(count_ref), image, probe_ref, forward_ref, inverse_ref)
    planes = [relaxed[w][part] for w in range(2) for part in range(2)]
    rows = columns_as_rows([(plane, at) for at in (127, 255, 128, 0) for plane in planes])
    lines = {}
    place, lane = iota((8, 256), 0), iota((8, 128), 1)
    for names, both in (((127, 255), rows[0:8]), ((128, 0), rows[8:16])):
        skewed = both
        for q in range(1, 4):
            skewed = jnp.where((place & 3) == q, pltpu.roll(both, 32 * q, 1), skewed)
        for i in range(8):
            turned = (pltpu.roll(skewed, 256 - 32 * i, 1) if i else skewed)[:, :128]
            turned = jnp.where((lane >> 5) == (place[:, :128] & 3), turned, 0.0)
            for at, half in zip(names, (turned[0:4], turned[4:8])):
                lines[at, i] = jnp.sum(half, axis=0, keepdims=True)
    extra_ref[...] = jnp.zeros_like(extra_ref)
    for k in range(16):
        i, j = k // 2, k % 2
        across, other = slice(128 * j, 128 * j + 128), slice(128 - 128 * j, 256 - 128 * j)
        for q, plane in enumerate(planes):
            out_ref[k, 32 * q:32 * q + 32, :] = plane[32 * i:32 * i + 32, across].astype(BF16)
            if i > 0:
                extra_ref[k, q:q + 1, :] = plane[32 * i - 1:32 * i, across]
            if i < 7:
                extra_ref[k, 4 + q:5 + q, :] = plane[32 * i + 32:32 * i + 33, across]
            if k in (8, 9):
                extra_ref[k, 8 + q:9 + q, :] = plane[255:256, across]
            if k in (6, 7):
                extra_ref[k, 8 + q:9 + q, :] = plane[0:1, across]
        if j == 1:
            extra_ref[k, 12:13, :] = lines[127, i]
            if i < 7:
                extra_ref[k, 13:14, :] = lines[0, i + 1]
        else:
            if i > 0:
                extra_ref[k, 12:13, :] = lines[255, i - 1]
            extra_ref[k, 13:14, :] = lines[128, i]
        if k == 8:
            extra_ref[k, 14:15, :] = lines[255, 7]
        if k == 7:
            extra_ref[k, 14:15, :] = lines[0, 0]
        out_ref[k, 128:144, :] = extra_ref[k].astype(BF16)


def inner_kernel(dev_ref, in_ref, out_ref):
    dev = dev_ref[0]
    group, member = dev // 16, dev % 16
    i, j = member // 2, member % 2
    order = [member_of(group, place) for place in range(16)]
    extra = [in_ref[m, 128:144, :].astype(F32) for m in order]
    left = jnp.concatenate([e[12:13] for e in extra], axis=0)
    right = jnp.concatenate([e[13:14] for e in extra], axis=0)
    first_half = iota((16, 128), 1) < 64
    turned = pltpu.roll(left, 64, 1)
    left = jnp.where(j == 1, left, jnp.where(first_half, turned, pltpu.roll(turned, 15, 0)))
    turned = pltpu.roll(right, 64, 1)
    right = jnp.where(j == 0, right, jnp.where(first_half, pltpu.roll(turned, 1, 0), turned))
    fill = jnp.zeros((112, 128), F32)
    left = jnp.concatenate([left, fill], axis=0).T
    right = jnp.concatenate([right, fill], axis=0).T
    last_lane = (iota((32, 128), 1) == 127).astype(F32)
    last_row = (iota((32, 128), 0) == 31).astype(F32)
    for u in range(32):
        place, w = u // 2, u % 2
        tile_row = (u + 8 * group + i) % 32
        tile_column = (dev - 2 * tile_row) & 127
        near, q = extra[place], [2 * w, 2 * w + 1]
        image = descend(
            [in_ref[order[place], pl.ds(32 * at, 32), :].astype(F32) for at in q],
            [to_lane(left[32 * at:32 * at + 32], place, 0) for at in q],
            [to_lane(right[32 * at:32 * at + 32], place, 127) for at in q],
            [near[at:at + 1] for at in q],
            [near[4 + at:5 + at] for at in q],
            ((tile_column != 0) & (member != 0)).astype(F32),
            1.0 - last_lane * ((tile_column == 127) | (member == 15)).astype(F32),
            ((tile_row != 0) & (i != 0)).astype(F32),
            1.0 - last_row * ((tile_row == 31) | (i == 7)).astype(F32),
        )
        for part in range(2):
            out_ref[part, tile_row] = image[part]


def border_kernel(dev_ref, in_ref, beyond_ref, inner_ref, out_ref):
    dev = dev_ref[0]
    group, member = dev // 16, dev % 16
    out_ref[...] = inner_ref[...]
    tiles = []
    for u in range(32):
        tile_row = (u + 8 * group + member // 2) % 32
        at = [32 * (2 * (u % 2) + part) for part in range(2)]
        tiles.append((u // 2, u % 2, tile_row, (dev - 2 * tile_row) & 127, member_of(group, u // 2), at))

    def beyond(place):
        return beyond_ref[member_of(group + 1, place)].astype(F32)

    def pull(d, keep):
        weight = STEP * lax.rsqrt(d[0] * d[0] + d[1] * d[1] + EPS) * keep
        return [d[0] * weight, d[1] * weight]

    def rows(at_row, edge_row):
        here = iota((8, 128), 0) == at_row % 8
        start = at_row // 8 * 8
        for place, w, tile_row, _, source, at in tiles:
            block = beyond(place)
            d = []
            for part in range(2):
                own = in_ref[source, pl.ds(at[part] + start // 16 * 16, 16), :].astype(F32)
                row = 2 * w + part
                d.append(own[start % 16:start % 16 + 8] - jnp.broadcast_to(block[row:row + 1], (8, 128)))
            for part, change in enumerate(pull(d, (tile_row != edge_row).astype(F32))):
                slot = out_ref.at[part, tile_row]
                slot[start:start + 8, :] = slot[start:start + 8, :] - jnp.where(here, change, 0.0)

    def columns(at_lane, edge_column):
        here = iota((32, 128), 1) == at_lane
        side = jnp.concatenate([beyond(place)[6:7] for place in range(16)], axis=0)
        half = iota((16, 128), 1) < 64
        turned = pltpu.roll(side, 64, 1)
        if at_lane == 0:
            side = jnp.where(half, turned, pltpu.roll(turned, 15, 0))
        else:
            side = jnp.where(half, pltpu.roll(turned, 1, 0), turned)
        side = jnp.concatenate([side, jnp.zeros((112, 128), F32)], axis=0).T
        for place, w, tile_row, tile_column, source, at in tiles:
            d = []
            for part in range(2):
                own = in_ref[source, pl.ds(at[part], 32), :].astype(F32)
                d.append(own - to_lane(side[at[part]:at[part] + 32], place, at_lane))
            for part, change in enumerate(pull(d, (tile_column != edge_column).astype(F32))):
                out_ref[part, tile_row] = out_ref[part, tile_row] - jnp.where(here, change, 0.0)

    pl.when(member < 2)(lambda: rows(0, 0))
    pl.when(member >= 14)(lambda: rows(31, 31))
    pl.when(member == 0)(lambda: columns(0, 0))
    pl.when(member == 15)(lambda: columns(127, 127))


def shards(object_tiles, amplitudes, probe, frame_pos):
    dev = lax.axis_index(ALL).astype(jnp.int32).reshape(1)
    forward, inverse = dft_blocks()

    lines = tiles_to_windows(dev, object_tiles)
    pieces = lax.all_to_all(amplitude_pieces(frame_pos, amplitudes), ALL, 0, 0, tiled=True)
    sums, counts = window_sums(dev, pieces)
    counts = jnp.concatenate([counts, counts], axis=1)
    lines, sums = lax.optimization_barrier((lines, sums))
    tiles = windows_from_lines(lines)
    sums = lax.all_to_all(sums, ALL, 0, 0, tiled=True)
    totals, relaxed, own, *edges = pl.pallas_call(
        first_kernel,
        in_specs=[SCALAR] + [BLOCK] * 15,
        out_specs=[BLOCK] * 9,
        out_shape=[jax.ShapeDtypeStruct((2, SIDE, SIDE), F32), PAIR] + [EDGE] * 7,
        scratch_shapes=[pltpu.VMEM((2, 2, 2, SIDE, 128), BF16)],
        compiler_params=params(),
        name="first_sweep",
    )(dev, *tiles, sums, counts, probe, forward, inverse)
    tiles = pl.pallas_call(
        second_kernel,
        in_specs=[SCALAR] + [BLOCK] * 13,
        out_specs=BLOCK,
        out_shape=jax.ShapeDtypeStruct((16, 144, 128), BF16),
        scratch_shapes=[pltpu.VMEM((16, 16, 128), F32)],
        compiler_params=params(),
        name="second_sweep",
    )(dev, relaxed, own, *exchange_edges(edges), totals, counts, probe, forward, inverse)
    tiles = lax.all_to_all(tiles, ALL, 0, 0, axis_index_groups=GROUPS, tiled=True)
    turns = ((8, 16), (9, 17), (7, -1), (6, -2))
    beyond = lax.ppermute(
        tiles[:, 136:], ALL, [(16 * g + k, (16 * g + to) % 128) for g in range(8) for k, to in turns]
    )
    result = jax.ShapeDtypeStruct((2, 32, 32, 128), F32)
    inner = pl.pallas_call(
        inner_kernel,
        in_specs=[SCALAR, BLOCK],
        out_specs=BLOCK,
        out_shape=result,
        compiler_params=params(),
        name="last_smoothing",
    )(dev, tiles)
    return pl.pallas_call(
        border_kernel,
        in_specs=[SCALAR] + [BLOCK] * 3,
        out_specs=BLOCK,
        out_shape=result,
        compiler_params=params(),
        name="last_borders",
    )(dev, tiles, beyond, inner)


def solution(mesh):
    return jax.shard_map(
        shards,
        mesh=mesh,
        in_specs=(P(None, ALL, None, None), P(ALL, None, None), P(), P(ALL, None)),
        out_specs=P(None, ALL, None, None),
        check_vma=False,
    )
```

```python
import jax
import jax.numpy as jnp
import numpy as np
from jax import lax
from jax.experimental import pallas as pl
from jax.experimental.pallas import tpu as pltpu
from jax.sharding import PartitionSpec as P

FLOOR = 0.3
DELTA = 1.0
STEP = 0.1
EPS = 0.1
CENTRE = 1.75
F32 = jnp.float32
BF16 = jnp.bfloat16
SIDE = 256
ALL = ("frames", "obj")
GROUPS = [list(range(16 * g, 16 * g + 16)) for g in range(8)]
SCALAR = pl.BlockSpec(memory_space=pltpu.SMEM)
BLOCK = pl.BlockSpec(memory_space=pltpu.VMEM)
EARLY, LATE = (0, 6, 5, 7, 2, 3), (4, 1)
ANYWHERE = pl.BlockSpec(memory_space=pl.ANY)
PAIR = jax.ShapeDtypeStruct((2, 2, SIDE, SIDE), F32)
EDGE = jax.ShapeDtypeStruct((8, SIDE), F32)


def place_of(group, member):
    far = (member // 8) ^ (group & 1)
    along = member % 4
    chip = along + far * (7 - 2 * along)
    return 2 * chip + (((member // 4) & 1) ^ (chip & 1))


def member_of(group, place):
    chip = place // 2
    far = chip // 4
    along = chip + far * (7 - 2 * chip)
    return 8 * (far ^ (group & 1)) + 4 * ((place & 1) ^ (chip & 1)) + along


def partners(move):
    pairs = []
    for dev in range(128):
        group, place = move(dev // 16, place_of(dev // 16, dev % 16))
        group, place = group % 8, place % 16
        pairs.append((dev, 16 * group + member_of(group, place)))
    return pairs


def params(limit_mb=40):
    return pltpu.CompilerParams(vmem_limit_bytes=limit_mb << 20)


def dft_blocks():
    index = np.arange(SIDE)
    angle = (index[:, None] * index[None, :] % SIDE) * (2.0 * np.pi / SIDE)
    cosine, sine = np.cos(angle) / 16.0, np.sin(angle) / 16.0
    forward = np.block([[cosine, sine], [-sine, cosine]])
    return jnp.asarray(forward, F32).astype(BF16), jnp.asarray(forward.T, F32).astype(BF16)


def iota(shape, axis):
    return lax.broadcasted_iota(jnp.int32, shape, axis)


def dot(a, b):
    return jnp.dot(a, b, preferred_element_type=F32)


def picker(source_of):
    return (iota((256, 256), 1) == source_of(iota((256, 256), 0))).astype(F32).astype(BF16)


def window_rows(dev):
    group = dev // 16
    place = place_of(group, dev % 16)
    return group, place, [(2 * place + 8 * group + w) % 32 for w in range(2)]


def pieces_kernel(pos_ref, amp_ref, out_ref, amp, out, in_sem, out_sem):
    fetch = [
        pltpu.make_async_copy(amp_ref.at[:, pl.ds(64 * b, 64), :], amp.at[:, pl.ds(64 * b, 64), :], in_sem.at[b])
        for b in range(4)
    ]
    store = [
        pltpu.make_async_copy(out.at[pl.ds(32 * b, 32)], out_ref.at[pl.ds(32 * b, 32)], out_sem.at[b])
        for b in range(4)
    ]
    for copy in fetch:
        copy.start()
    swap = picker(lambda o: (o % 16) * 16 + o // 16)
    row, column = pos_ref[0:1, :], pos_ref[1:2, :]
    group = ((column + 2 * row) & 127) >> 4
    local = (row - 8 * group) & 31
    owner = ((local & 1) * 128 + 16 * group + member_of(group, local >> 1)).astype(F32)
    code = jnp.where(iota((16, 16), 0) == iota((16, 16), 1), owner, 0.0)
    code = jnp.sum(code, axis=1, keepdims=True)
    mine = (iota((16, 128), 1) & 15) == iota((16, 128), 0)
    code = jnp.sum(jnp.where(mine, code, 0.0), axis=0, keepdims=True)
    code = jnp.broadcast_to(code, (8, 128)).astype(BF16)
    for b in range(4):
        fetch[b].wait()
        for block in range(4 * b, 4 * b + 4):
            rows = amp[:, 16 * block:16 * block + 16, :].reshape(256, 256)
            turned = dot(swap, rows).astype(BF16)
            for part in range(8):
                quad, half = part // 2, part % 2
                out[8 * block + part, 0:64, :] = turned[64 * quad:64 * quad + 64, 128 * half:128 * half + 128]
                out[8 * block + part, 64:72, :] = code
        store[b].start()
    for copy in store:
        copy.wait()


def amplitude_pieces(frame_pos, amplitudes):
    return pl.pallas_call(
        pieces_kernel,
        in_specs=[BLOCK, ANYWHERE],
        out_specs=ANYWHERE,
        out_shape=jax.ShapeDtypeStruct((128, 72, 128), BF16),
        scratch_shapes=[
            pltpu.VMEM((16, 256, 256), BF16),
            pltpu.VMEM((128, 72, 128), BF16),
            pltpu.SemaphoreType.DMA((4,)),
            pltpu.SemaphoreType.DMA((4,)),
        ],
        compiler_params=params(60),
        name="amplitude_pieces",
    )(frame_pos.T, amplitudes)


def sums_kernel(dev_ref, in_ref, out_ref, count_ref, pieces, total_ref, number_ref, sem):
    fetch = [
        pltpu.make_async_copy(in_ref.at[pl.ds(32 * b, 32)], pieces.at[pl.ds(32 * b, 32)], sem.at[b])
        for b in range(4)
    ]
    for copy in fetch:
        copy.start()
    lane = iota((8, 128), 1)
    owner = iota((256, 128), 0).astype(F32)
    turn = picker(lambda o: (o % 8) * 32 + o // 8)
    for b in range(4):
        fetch[b].wait()
        members, values = [], []
        for t in range(4 * b, 4 * b + 4):
            code = jnp.zeros((8, 128), F32)
            for s in range(8):
                code = jnp.where((lane >> 4) == s, pieces[8 * t + s, 64:72, :].astype(F32), code)
            members.append((owner == jnp.tile(code, (32, 1))).astype(F32).astype(BF16))
            values.append(
                jnp.concatenate(
                    [pieces[8 * t:8 * t + 8, 16 * c:16 * c + 16, :].reshape(128, 128) for c in range(4)]
                    + [jnp.ones((128, 128), BF16)],
                    axis=1,
                )
            )
        total = dot(jnp.concatenate(members, axis=1), jnp.concatenate(values, axis=0))
        total_ref[...] = total if b == 0 else total_ref[...] + total
    for block in range(4):
        parts = []
        for w in range(2):
            rows = slice(128 * w + 32 * block, 128 * w + 32 * block + 32)
            mean = CENTRE * total_ref[rows, 512:640]
            for c in range(4):
                parts.append(total_ref[rows, 128 * c:128 * c + 128] - mean)
        stacked = jnp.concatenate(parts, axis=0).astype(BF16)
        out_ref[32 * block:32 * block + 32] = dot(turn, stacked).reshape(32, 8, 128).astype(BF16)
    number_ref[...] = total_ref[:, 512:640]
    for w in range(2):
        own = number_ref[pl.ds(dev_ref[0] + 128 * w, 1), :]
        count_ref[8 * w:8 * w + 8, :] = jnp.broadcast_to(own, (8, 128))


def window_sums(dev, arrived):
    return pl.pallas_call(
        sums_kernel,
        in_specs=[SCALAR, ANYWHERE],
        out_specs=[BLOCK] * 2,
        out_shape=[
            jax.ShapeDtypeStruct((128, 8, 128), BF16),
            jax.ShapeDtypeStruct((16, 128), F32),
        ],
        scratch_shapes=[
            pltpu.VMEM((128, 72, 128), BF16),
            pltpu.VMEM((256, 640), F32),
            pltpu.VMEM((256, 128), F32),
            pltpu.SemaphoreType.DMA((4,)),
        ],
        compiler_params=params(60),
        name="window_sums",
    )(dev, arrived)


def outbound_kernel(dev_ref, in_ref, *out_refs):
    dev = dev_ref[0]
    member = dev % 16
    shift = 8 * (dev // 16) + member // 2
    for t in range(8):
        for e in range(2):
            target = member ^ (8 * (t // 4) + t % 4 + 4 * e)
            for w in range(2):
                row = (shift + 2 * place_of(dev // 16, target) + w) % 32
                for part in range(2):
                    out_refs[t][e, w, part] = in_ref[part, row].astype(BF16)


def tiles_to_windows(dev, tiles):
    blocks = pl.pallas_call(
        outbound_kernel,
        in_specs=[SCALAR, BLOCK],
        out_specs=[BLOCK] * 8,
        out_shape=[jax.ShapeDtypeStruct((2, 2, 2, 32, 128), BF16)] * 8,
        compiler_params=params(),
        name="outbound_tiles",
    )(dev, tiles)
    blocks = list(blocks)
    for t in EARLY[1:]:
        blocks[t] = across_chips(blocks[t], t)
    return blocks


def across_chips(block, t):
    return lax.ppermute(block, ALL, [(d, d ^ (8 * (t // 4) + t % 4)) for d in range(128)])


def windows_from_lines(blocks):
    for t in LATE:
        blocks[t] = across_chips(blocks[t], t)
    other = [
        lax.ppermute(jnp.stack([blocks[t][1] for t in part]), ALL, [(d, d ^ 4) for d in range(128)])
        for part in (EARLY, LATE)
    ]
    return blocks + other


def to_far_field(image, probe_ref, forward_ref, inverse_ref):
    waves = []
    for w in range(2):
        real, imag = [image[w][part].astype(BF16).astype(F32) for part in range(2)]
        waves.append(
            [
                (probe_ref[0] * real - probe_ref[1] * imag).astype(BF16),
                (probe_ref[0] * imag + probe_ref[1] * real).astype(BF16),
            ]
        )
    wave = jnp.concatenate(
        [jnp.concatenate([waves[0][part], waves[1][part]], axis=1) for part in range(2)], axis=0
    )
    midway = dot(forward_ref[...], wave).astype(BF16)
    midway = jnp.concatenate(
        [
            jnp.concatenate([midway[:256, 256 * w:256 * w + 256], midway[256:, 256 * w:256 * w + 256]], axis=1)
            for w in range(2)
        ],
        axis=0,
    )
    return dot(midway, inverse_ref[...])


def from_far_field(far, totals, counts, image, probe_ref, forward_ref, inverse_ref):
    changes = []
    for w in range(2):
        real, imag = far[256 * w:256 * w + 256, :256], far[256 * w:256 * w + 256, 256:]
        power = jnp.maximum(real * real + imag * imag, FLOOR * FLOOR)
        scale = totals[w] * lax.rsqrt(power) - counts[w]
        changes.append([(real * scale).astype(BF16), (imag * scale).astype(BF16)])
    change = jnp.concatenate(
        [jnp.concatenate([changes[0][part], changes[1][part]], axis=1) for part in range(2)], axis=0
    )
    halfway = dot(inverse_ref[...], change).astype(BF16)
    halfway = jnp.concatenate(
        [
            jnp.concatenate([halfway[:256, 256 * w:256 * w + 256], halfway[256:, 256 * w:256 * w + 256]], axis=1)
            for w in range(2)
        ],
        axis=0,
    )
    returned = dot(halfway, forward_ref[...])
    intensity = probe_ref[0] * probe_ref[0] + probe_ref[1] * probe_ref[1]
    relaxed = []
    for w in range(2):
        real, imag = returned[256 * w:256 * w + 256, :256], returned[256 * w:256 * w + 256, 256:]
        weight = 1.0 / (counts[w] * intensity + DELTA)
        relaxed.append(
            [
                image[w][0] + (probe_ref[0] * real + probe_ref[1] * imag) * weight,
                image[w][1] + (probe_ref[0] * imag - probe_ref[1] * real) * weight,
            ]
        )
    return relaxed


def own_counts(count_ref):
    return [jnp.tile(count_ref[8 * w:8 * w + 8, :], (32, 1)) for w in range(2)]


def write_relaxed(dev, relaxed, relaxed_ref, own_ref, edge_refs):
    for w in range(2):
        for part in range(2):
            relaxed_ref[w, part] = relaxed[w][part]
    rows = columns_as_rows(
        [(relaxed[w][part], 255 * side) for w, side in ((0, 1), (1, 0), (1, 1), (0, 0)) for part in range(2)]
    )[:8]
    own_ref[...] = rows
    place = iota((8, 256), 0)
    ahead, behind = pltpu.roll(rows, 6, 0), pltpu.roll(rows, 4, 0)
    up, down = rows, pltpu.roll(rows, 6, 0)
    for w in range(2):
        for part in range(2):
            at = 2 * w + part
            up = jnp.where(place == at, pltpu.roll(relaxed[w][part][248:], (at - 7) % 8, 0), up)
            first = relaxed[w][part][:8]
            down = jnp.where(place == at, pltpu.roll(first, at, 0) if at else first, down)
    group, spot, _ = window_rows(dev)
    odd_group, odd_spot = (group & 1) == 1, (spot & 1) == 1
    for ref, odd, even_edge, odd_edge in (
        (edge_refs[0], odd_group, behind, ahead),
        (edge_refs[1], odd_group, down, up),
        (edge_refs[2], odd_group, ahead, behind),
        (edge_refs[3], odd_group, up, down),
        (edge_refs[4], odd_spot, ahead, behind),
        (edge_refs[5], odd_spot, behind, ahead),
    ):
        ref[...] = jnp.where(odd, odd_edge, even_edge)


def exchange_edges(edges):
    moves = []
    for odd in (1, 0):
        moves.append(lambda g, q, odd=odd: (g + 1, q - 1) if g % 2 == odd else (g - 1, q + 1))
        moves.append(lambda g, q, odd=odd: (g + 1 if g % 2 == odd else g - 1, q))
    for odd in (1, 0):
        moves.append(lambda g, q, odd=odd: (g, q + 1 if q % 2 == odd else q - 1))
    return [lax.ppermute(edge, ALL, partners(move)) for edge, move in zip(edges, moves)]


def descend(x, left, right, up, down, keep_left, keep_right, keep_up, keep_down):
    rows, lanes = x[0].shape
    lane, row, row8 = iota((rows, lanes), 1), iota((rows, lanes), 0), iota((8, lanes), 0)

    def wide(narrow):
        return jnp.concatenate([narrow] * (lanes // 128), axis=1)

    across, edge, below, top = [], [], [], []
    for part in range(2):
        next_lane = jnp.where(lane == lanes - 1, wide(right[part]), pltpu.roll(x[part], lanes - 1, 1))
        across.append(next_lane - x[part])
        edge.append(x[part][:, :128] - left[part])
        next_row = jnp.where(
            row == rows - 1, jnp.broadcast_to(down[part], (rows, lanes)), pltpu.roll(x[part], rows - 1, 0)
        )
        below.append(next_row - x[part])
        top.append(x[part][:8] - jnp.broadcast_to(up[part], (8, lanes)))
    across_weight, edge_weight, below_weight, top_weight = [
        lax.rsqrt(d[0] * d[0] + d[1] * d[1] + EPS) * keep
        for d, keep in ((across, keep_right), (edge, keep_left), (below, keep_down), (top, keep_up))
    ]
    result = []
    for part in range(2):
        to_right = across[part] * across_weight
        to_left = jnp.where(lane == 0, wide(edge[part] * edge_weight), pltpu.roll(to_right, 1, 1))
        to_below = below[part] * below_weight
        moved = pltpu.roll(to_below, 1, 0)
        to_above = jnp.concatenate(
            [jnp.where(row8 == 0, top[part] * top_weight, moved[:8]), moved[8:]], axis=0
        )
        result.append(x[part] - STEP * ((to_left - to_right) + (to_above - to_below)))
    return result


def to_lane(block, source, lane):
    shift = (lane - source) % 128
    return pltpu.roll(block, shift, 1) if shift else block


def smooth(dev, relaxed_ref, own_ref, halo_refs):
    group, spot, starts = window_rows(dev)
    odd_group, odd_spot = (group & 1) == 1, (spot & 1) == 1
    corner1, above1, corner0, above0, beside1, beside0 = [ref[...] for ref in halo_refs]
    extra = iota((8, 256), 0) >= 6
    up_own = jnp.where(extra, jnp.where(odd_spot, beside1, beside0), own_ref[...])
    down_own = jnp.where(extra, jnp.where(odd_spot, beside0, beside1), pltpu.roll(own_ref[...], 6, 0))
    up_in = jnp.where(extra, jnp.where(odd_group, corner0, corner1), jnp.where(odd_group, above0, above1))
    down_in = jnp.where(extra, jnp.where(odd_group, corner1, corner0), jnp.where(odd_group, above1, above0))
    lane8 = iota((8, 256), 1)
    left = jnp.where(lane8 < 32, pltpu.roll(up_in, 32, 1), pltpu.roll(up_own, 32, 1))
    right = jnp.where(lane8 >= 224, pltpu.roll(down_in, 224, 1), pltpu.roll(down_own, 224, 1))
    sides = jnp.concatenate([left, right, jnp.zeros((112, 256), F32)], axis=0).T
    lane, row = iota((256, 256), 1), iota((256, 256), 0)
    image = []
    for w in range(2):
        start = starts[w]
        wrapped = (row // 32 + start) >= 32
        column = (16 * group - 2 * start + jnp.where(wrapped, 64, 0)) & 127
        image.append(
            descend(
                [relaxed_ref[w, part] for part in range(2)],
                [to_lane(sides, 4 + 2 * w + part, 0) for part in range(2)],
                [to_lane(sides, 8 + 4 + 2 * (1 - w) + part, 127) for part in range(2)],
                [up_in[2 * w + part:2 * w + part + 1] for part in range(2)],
                [down_in[2 * w + part:2 * w + part + 1] for part in range(2)],
                (column[:, :128] != 0).astype(F32),
                jnp.logical_not((lane == 255) & (column == 126)).astype(F32),
                (start != 0).astype(F32),
                (((32 * start + row) & 1023) != 1023).astype(F32),
            )
        )
    return image


def first_kernel(dev_ref, *refs):
    block_refs, other_refs, (sums_ref, count_ref, probe_ref, forward_ref, inverse_ref) = refs[:8], refs[8:10], refs[10:15]
    total_ref, relaxed_ref, own_ref, *edge_refs, half_ref = refs[15:]
    member = dev_ref[0] % 16
    for t in range(8):
        for e in range(2):
            source = member ^ (8 * (t // 4) + t % 4 + 4 * e)
            rows = pl.ds(pl.multiple_of(source // 2 * 32, 32), 32)
            for w in range(2):
                for part in range(2):
                    if e == 0:
                        tile = block_refs[t][0, w, part]
                    elif t in LATE:
                        tile = other_refs[1][LATE.index(t), w, part]
                    else:
                        tile = other_refs[0][EARLY.index(t), w, part]
                    half_ref[w, part, source % 2, rows, :] = tile
    image = [
        [jnp.concatenate([half_ref[w, part, 0], half_ref[w, part, 1]], axis=1).astype(F32) for part in range(2)]
        for w in range(2)
    ]
    far = to_far_field(image, probe_ref, forward_ref, inverse_ref)
    counts = own_counts(count_ref)

    def source(o):
        w, half, row = o // 128, (o // 64) % 2, o % 64
        return ((row // 4) * 2 + half) * 8 + w * 4 + row % 4

    place = picker(source)
    blocks = []
    for block in range(4):
        rows = sums_ref[32 * block:32 * block + 32].astype(F32).reshape(256, 128).astype(BF16)
        blocks.append(dot(place, rows))
    totals = []
    for w in range(2):
        total = jnp.concatenate(
            [
                jnp.concatenate([b[128 * w:128 * w + 64], b[128 * w + 64:128 * w + 128]], axis=1)
                for b in blocks
            ],
            axis=0,
        ) + CENTRE * counts[w]
        total_ref[w] = total
        totals.append(total)
    relaxed = from_far_field(far, totals, counts, image, probe_ref, forward_ref, inverse_ref)
    write_relaxed(dev_ref[0], relaxed, relaxed_ref, own_ref, edge_refs)


def columns_as_rows(columns):
    lane = iota((256, 128), 1)
    gathered = jnp.zeros((256, 128), F32)
    for place, (image, at) in enumerate(columns):
        block = image[:, at // 128 * 128:at // 128 * 128 + 128]
        gathered = jnp.where(lane == place, to_lane(block, at % 128, place), gathered)
    return gathered.T


def second_kernel(
    dev_ref, in_ref, own_in, in0, in1, in2, in3, in4, in5, total_ref, count_ref, probe_ref, forward_ref, inverse_ref,
    out_ref, extra_ref
):
    image = smooth(dev_ref[0], in_ref, own_in, (in0, in1, in2, in3, in4, in5))
    far = to_far_field(image, probe_ref, forward_ref, inverse_ref)
    totals = [total_ref[w] for w in range(2)]
    relaxed = from_far_field(far, totals, own_counts(count_ref), image, probe_ref, forward_ref, inverse_ref)
    planes = [relaxed[w][part] for w in range(2) for part in range(2)]
    rows = columns_as_rows([(plane, at) for at in (127, 255, 128, 0) for plane in planes])
    lines = {}
    place, lane = iota((8, 256), 0), iota((8, 128), 1)
    for names, both in (((127, 255), rows[0:8]), ((128, 0), rows[8:16])):
        skewed = both
        for q in range(1, 4):
            skewed = jnp.where((place & 3) == q, pltpu.roll(both, 32 * q, 1), skewed)
        for i in range(8):
            turned = (pltpu.roll(skewed, 256 - 32 * i, 1) if i else skewed)[:, :128]
            turned = jnp.where((lane >> 5) == (place[:, :128] & 3), turned, 0.0)
            for at, half in zip(names, (turned[0:4], turned[4:8])):
                lines[at, i] = jnp.sum(half, axis=0, keepdims=True)
    extra_ref[...] = jnp.zeros_like(extra_ref)
    for k in range(16):
        i, j = k // 2, k % 2
        across, other = slice(128 * j, 128 * j + 128), slice(128 - 128 * j, 256 - 128 * j)
        for q, plane in enumerate(planes):
            out_ref[k, 32 * q:32 * q + 32, :] = plane[32 * i:32 * i + 32, across].astype(BF16)
            if i > 0:
                extra_ref[k, q:q + 1, :] = plane[32 * i - 1:32 * i, across]
            if i < 7:
                extra_ref[k, 4 + q:5 + q, :] = plane[32 * i + 32:32 * i + 33, across]
            if k in (8, 9):
                extra_ref[k, 8 + q:9 + q, :] = plane[255:256, across]
            if k in (6, 7):
                extra_ref[k, 8 + q:9 + q, :] = plane[0:1, across]
        if j == 1:
            extra_ref[k, 12:13, :] = lines[127, i]
            if i < 7:
                extra_ref[k, 13:14, :] = lines[0, i + 1]
        else:
            if i > 0:
                extra_ref[k, 12:13, :] = lines[255, i - 1]
            extra_ref[k, 13:14, :] = lines[128, i]
        if k == 8:
            extra_ref[k, 14:15, :] = lines[255, 7]
        if k == 7:
            extra_ref[k, 14:15, :] = lines[0, 0]
        out_ref[k, 128:144, :] = extra_ref[k].astype(BF16)


def inner_kernel(dev_ref, in_ref, out_ref):
    dev = dev_ref[0]
    group, member = dev // 16, dev % 16
    i, j = member // 2, member % 2
    order = [member_of(group, place) for place in range(16)]
    extra = [in_ref[m, 128:144, :].astype(F32) for m in order]
    left = jnp.concatenate([e[12:13] for e in extra], axis=0)
    right = jnp.concatenate([e[13:14] for e in extra], axis=0)
    first_half = iota((16, 128), 1) < 64
    turned = pltpu.roll(left, 64, 1)
    left = jnp.where(j == 1, left, jnp.where(first_half, turned, pltpu.roll(turned, 15, 0)))
    turned = pltpu.roll(right, 64, 1)
    right = jnp.where(j == 0, right, jnp.where(first_half, pltpu.roll(turned, 1, 0), turned))
    fill = jnp.zeros((112, 128), F32)
    left = jnp.concatenate([left, fill], axis=0).T
    right = jnp.concatenate([right, fill], axis=0).T
    last_lane = (iota((32, 128), 1) == 127).astype(F32)
    last_row = (iota((32, 128), 0) == 31).astype(F32)
    for u in range(32):
        place, w = u // 2, u % 2
        tile_row = (u + 8 * group + i) % 32
        tile_column = (dev - 2 * tile_row) & 127
        near, q = extra[place], [2 * w, 2 * w + 1]
        image = descend(
            [in_ref[order[place], pl.ds(32 * at, 32), :].astype(F32) for at in q],
            [to_lane(left[32 * at:32 * at + 32], place, 0) for at in q],
            [to_lane(right[32 * at:32 * at + 32], place, 127) for at in q],
            [near[at:at + 1] for at in q],
            [near[4 + at:5 + at] for at in q],
            ((tile_column != 0) & (member != 0)).astype(F32),
            1.0 - last_lane * ((tile_column == 127) | (member == 15)).astype(F32),
            ((tile_row != 0) & (i != 0)).astype(F32),
            1.0 - last_row * ((tile_row == 31) | (i == 7)).astype(F32),
        )
        for part in range(2):
            out_ref[part, tile_row] = image[part]


def border_kernel(dev_ref, in_ref, beyond_ref, inner_ref, out_ref):
    dev = dev_ref[0]
    group, member = dev // 16, dev % 16
    out_ref[...] = inner_ref[...]
    tiles = []
    for u in range(32):
        tile_row = (u + 8 * group + member // 2) % 32
        at = [32 * (2 * (u % 2) + part) for part in range(2)]
        tiles.append((u // 2, u % 2, tile_row, (dev - 2 * tile_row) & 127, member_of(group, u // 2), at))

    def beyond(place):
        return beyond_ref[member_of(group + 1, place)].astype(F32)

    def pull(d, keep):
        weight = STEP * lax.rsqrt(d[0] * d[0] + d[1] * d[1] + EPS) * keep
        return [d[0] * weight, d[1] * weight]

    def rows(at_row, edge_row):
        here = iota((8, 128), 0) == at_row % 8
        start = at_row // 8 * 8
        for place, w, tile_row, _, source, at in tiles:
            block = beyond(place)
            d = []
            for part in range(2):
                own = in_ref[source, pl.ds(at[part] + start // 16 * 16, 16), :].astype(F32)
                row = 2 * w + part
                d.append(own[start % 16:start % 16 + 8] - jnp.broadcast_to(block[row:row + 1], (8, 128)))
            for part, change in enumerate(pull(d, (tile_row != edge_row).astype(F32))):
                slot = out_ref.at[part, tile_row]
                slot[start:start + 8, :] = slot[start:start + 8, :] - jnp.where(here, change, 0.0)

    def columns(at_lane, edge_column):
        here = iota((32, 128), 1) == at_lane
        side = jnp.concatenate([beyond(place)[6:7] for place in range(16)], axis=0)
        half = iota((16, 128), 1) < 64
        turned = pltpu.roll(side, 64, 1)
        if at_lane == 0:
            side = jnp.where(half, turned, pltpu.roll(turned, 15, 0))
        else:
            side = jnp.where(half, pltpu.roll(turned, 1, 0), turned)
        side = jnp.concatenate([side, jnp.zeros((112, 128), F32)], axis=0).T
        for place, w, tile_row, tile_column, source, at in tiles:
            d = []
            for part in range(2):
                own = in_ref[source, pl.ds(at[part], 32), :].astype(F32)
                d.append(own - to_lane(side[at[part]:at[part] + 32], place, at_lane))
            for part, change in enumerate(pull(d, (tile_column != edge_column).astype(F32))):
                out_ref[part, tile_row] = out_ref[part, tile_row] - jnp.where(here, change, 0.0)

    pl.when(member < 2)(lambda: rows(0, 0))
    pl.when(member >= 14)(lambda: rows(31, 31))
    pl.when(member == 0)(lambda: columns(0, 0))
    pl.when(member == 15)(lambda: columns(127, 127))


def shards(object_tiles, amplitudes, probe, frame_pos):
    dev = lax.axis_index(ALL).astype(jnp.int32).reshape(1)
    forward, inverse = dft_blocks()

    lines = tiles_to_windows(dev, object_tiles)
    pieces = lax.all_to_all(amplitude_pieces(frame_pos, amplitudes), ALL, 0, 0, tiled=True)
    sums, counts = window_sums(dev, pieces)
    counts = jnp.concatenate([counts, counts], axis=1)
    lines, sums = lax.optimization_barrier((lines, sums))
    tiles = windows_from_lines(lines)
    sums = lax.all_to_all(sums, ALL, 0, 0, tiled=True)
    totals, relaxed, own, *edges = pl.pallas_call(
        first_kernel,
        in_specs=[SCALAR] + [BLOCK] * 15,
        out_specs=[BLOCK] * 9,
        out_shape=[jax.ShapeDtypeStruct((2, SIDE, SIDE), F32), PAIR] + [EDGE] * 7,
        scratch_shapes=[pltpu.VMEM((2, 2, 2, SIDE, 128), BF16)],
        compiler_params=params(),
        name="first_sweep",
    )(dev, *tiles, sums, counts, probe, forward, inverse)
    tiles = pl.pallas_call(
        second_kernel,
        in_specs=[SCALAR] + [BLOCK] * 13,
        out_specs=BLOCK,
        out_shape=jax.ShapeDtypeStruct((16, 144, 128), BF16),
        scratch_shapes=[pltpu.VMEM((16, 16, 128), F32)],
        compiler_params=params(),
        name="second_sweep",
    )(dev, relaxed, own, *exchange_edges(edges), totals, counts, probe, forward, inverse)
    tiles = lax.all_to_all(tiles, ALL, 0, 0, axis_index_groups=GROUPS, tiled=True)
    turns = ((8, 16), (9, 17), (7, -1), (6, -2))
    beyond = lax.ppermute(
        tiles[:, 136:], ALL, [(16 * g + k, (16 * g + to) % 128) for g in range(8) for k, to in turns]
    )
    result = jax.ShapeDtypeStruct((2, 32, 32, 128), F32)
    inner = pl.pallas_call(
        inner_kernel,
        in_specs=[SCALAR, BLOCK],
        out_specs=BLOCK,
        out_shape=result,
        compiler_params=params(),
        name="last_smoothing",
    )(dev, tiles)
    return pl.pallas_call(
        border_kernel,
        in_specs=[SCALAR] + [BLOCK] * 3,
        out_specs=BLOCK,
        out_shape=result,
        compiler_params=params(),
        name="last_borders",
    )(dev, tiles, beyond, inner)


def solution(mesh):
    return jax.shard_map(
        shards,
        mesh=mesh,
        in_specs=(P(None, ALL, None, None), P(ALL, None, None), P(), P(ALL, None)),
        out_specs=P(None, ALL, None, None),
        check_vma=False,
    )
```
